32 devices in a mesh: fsdp: 32 (over z, y, x, core).
Axes of the slice: x: 2, y: 2, z: 4, core: 2. Of those that a mesh axis runs over, the one named last changes fastest.
Arguments:
- tokens: bfloat16 [8192, 2048], P('fsdp'), may hold values from -6 to 6
- cotangent: bfloat16 [8192, 2048], P('fsdp'), may hold values from -6 to 6
- block_first: int32 [64], P('fsdp'), may hold values from 0 to 1, as said below
- block_live: int32 [64], P('fsdp'), may hold values from 0 to 128, as said below
- w_qkv: float32 [2048, 6144], P('fsdp')
- w_attn_out: float32 [2048, 2048], P('fsdp'), may hold values from -1 to 1
- w_mlp_in: float32 [2048, 8192], P('fsdp'), may hold values from -0.125 to 0.125
- w_mlp_out: float32 [2048, 8192], P('fsdp'), may hold values from -0.0625 to 0.0625
- vectors: float32 [24576], P('fsdp')
- first_qkv: float32 [2048, 6144], P('fsdp'), may hold values from -6 to 6
- second_qkv: float32 [2048, 6144], P('fsdp'), may hold values from 204.8 to 3276.8
- first_attn_out: float32 [2048, 2048], P('fsdp'), may hold values from -6 to 6
- second_attn_out: float32 [2048, 2048], P('fsdp'), may hold values from 18.432 to 294.912
- first_mlp_in: float32 [2048, 8192], P('fsdp'), may hold values from -6 to 6
- second_mlp_in: float32 [2048, 8192], P('fsdp'), may hold values from 51.2 to 819.2
- first_mlp_out: float32 [2048, 8192], P('fsdp'), may hold values from -6 to 6
- second_mlp_out: float32 [2048, 8192], P('fsdp'), may hold values from 32.768 to 524.288
- first_vectors: float32 [24576], P('fsdp'), may hold values from -6 to 6
- second_vectors: float32 [24576], P('fsdp'), may hold values from 3276.8 to 52428.8
Outputs:
- out: bfloat16 [8192, 2048], P('fsdp')
- grad_tokens: bfloat16 [8192, 2048], P('fsdp')
- grad_qkv: float32 [2048, 6144], P('fsdp')
- grad_attn_out: float32 [2048, 2048], P('fsdp')
- grad_mlp_in: float32 [2048, 8192], P('fsdp')
- grad_mlp_out: float32 [2048, 8192], P('fsdp')
- grad_vectors: float32 [24576], P('fsdp')
- new_qkv: float32 [2048, 6144], P('fsdp')
- new_attn_out: float32 [2048, 2048], P('fsdp')
- new_mlp_in: float32 [2048, 8192], P('fsdp')
- new_mlp_out: float32 [2048, 8192], P('fsdp')
- new_vectors: float32 [24576], P('fsdp')
- new_first_qkv: float32 [2048, 6144], P('fsdp')
- new_second_qkv: float32 [2048, 6144], P('fsdp')
- new_first_attn_out: float32 [2048, 2048], P('fsdp')
- new_second_attn_out: float32 [2048, 2048], P('fsdp')
- new_first_mlp_in: float32 [2048, 8192], P('fsdp')
- new_second_mlp_in: float32 [2048, 8192], P('fsdp')
- new_first_mlp_out: float32 [2048, 8192], P('fsdp')
- new_second_mlp_out: float32 [2048, 8192], P('fsdp')
- new_first_vectors: float32 [24576], P('fsdp')
- new_second_vectors: float32 [24576], P('fsdp')
The draws below stay inside these ranges and needn't reach their ends.
Inputs may be any that keep to these rules, and one draw needn't show every extreme that they name: Each device holds 2 blocks of 128 slots. A sequence fills consecutive blocks of one device, every block of it full but its last, which holds 1 to 128 live slots at its start; block_first gives its first block's index among the device's blocks. Blocks of no sequence follow the used ones of their device, with block_live 0 and block_first their own index. The first device holds one sequence of 256 live tokens. `block_live`: as for block_first.
All inputs are finite; a program needn't handle non-finite values.
Results may differ from the reference program's by a relative error of at most 0.012.
Values may be sent and summed in bfloat16 or wider, within the bound.
No kernel may reach another device: no remote copies, remote signals or barrier semaphores. Data moves between devices by JAX's collectives and lax.ppermute only.
A program may use at most 832 MiB of HBM per device.

```python
import math
import jax
import jax.numpy as jnp
from jax import lax

D = 2048
HEADS = 8
HEAD = 256
FF = 8192
ROT = 64
BLOCK = 128
BLK_DEV = 2
STEP = 3
SLOTS = 256
TOKENS = 8192
NBLK = 64
VEC = 24576
N_FSDP = 32


def block_layout(key):
    device_count = NBLK // BLK_DEV
    base = jax.random.fold_in(key, 11)
    key_used, key_starts, key_partial = jax.random.split(base, 3)
    dev_index = jnp.arange(device_count, dtype=jnp.int32)[:, None]
    blk_index = jnp.arange(BLK_DEV, dtype=jnp.int32)[None, :]
    used_count = jax.random.randint(key_used, (device_count, 1), 1, BLK_DEV + 1)
    used_count = jnp.where(dev_index == 0, BLK_DEV, used_count)
    starts = jax.random.randint(key_starts, (device_count, BLK_DEV), 0, 2)
    starts = jnp.where(blk_index == 0, 1, starts)
    starts = jnp.where(dev_index == 0, (blk_index == 0).astype(jnp.int32), starts)
    inside = blk_index < used_count
    first_raw = lax.cummax(jnp.where(starts == 1, blk_index, 0), axis=1)
    first_blocks = jnp.where(inside, first_raw, blk_index)
    next_start = jnp.concatenate([starts[:, 1:], jnp.ones((device_count, 1), jnp.int32)], axis=1)
    closing = inside & ((blk_index + 1 == used_count) | (next_start == 1))
    partial_fill = jax.random.randint(key_partial, (device_count, BLK_DEV), 1, BLOCK + 1)
    partial_fill = jnp.where(dev_index == 0, BLOCK, partial_fill)
    live_blocks = jnp.where(inside, jnp.where(closing, partial_fill, BLOCK), 0)
    return (first_blocks.reshape(NBLK).astype(jnp.int32), live_blocks.reshape(NBLK).astype(jnp.int32))


def draw_block_first(key, part):
    return block_layout(key)[0]


def draw_block_live(key, part):
    return block_layout(key)[1]


def draw_w_qkv(key, part):
    base = jax.random.fold_in(key, 23)
    whole = jax.random.normal(base, (D, 3 * D), jnp.float32) * D ** (-0.5)
    return whole


def draw_vectors(key, part):
    base = jax.random.fold_in(key, 31)
    key_bias, key_gain = jax.random.split(base, 2)
    index = jnp.arange(VEC, dtype=jnp.int32)
    gain_zone = (index >= 4 * D + FF) & (index < 5 * D + FF) | (index >= 6 * D + FF) & (index < 7 * D + FF)
    biases = jnp.clip(jax.random.normal(key_bias, (VEC,), jnp.float32) * 0.3, -1.2, 1.2)
    gains = jax.random.uniform(key_gain, (VEC,), jnp.float32, 0.7, 1.3)
    return jnp.where(gain_zone, gains, biases)


def levels(rng, dims, shards, low, largest):
    def one(dim, shards_of):
        heights = jax.random.uniform(jax.random.fold_in(jax.random.fold_in(rng, 6), dim), (shards_of,), jnp.float32, low / len(shards), largest / len(shards))
        return jnp.repeat(jnp.exp(heights), dims[dim] // shards_of).reshape((-1,) + (1,) * (len(dims) - dim - 1))

    level = one(*shards[0])
    for cut in shards[1:]:
        level = level * one(*cut)
    return level


def bell_draw(key, dims, deviation, bound, cuts=(), held_as=jnp.bfloat16):
    entries = jax.random.normal(key, dims, jnp.float32) * deviation
    if len(cuts) > 0:
        entries = levels(key, dims, cuts, -0.22, 0.18) * entries
    return jnp.clip(entries, min=-bound, max=bound).astype(held_as)


def setup_inputs(seed: int = 0) -> dict:
    keys = jax.random.split(jax.random.key(seed), 20)
    tokens = bell_draw(keys[0], (TOKENS, D), 1.0, 6.0, ((0, 32),))
    cotangent = bell_draw(keys[1], (TOKENS, D), 1.0, 6.0, ((0, 32),))
    block_first = draw_block_first(jax.random.fold_in(keys[19], 71), 0)
    block_live = draw_block_live(jax.random.fold_in(keys[19], 71), 0)
    w_qkv = draw_w_qkv(jax.random.fold_in(keys[19], 71), 0)
    w_attn_out = bell_draw(keys[5], (D, D), (D // 64) ** -0.5, 1.0, ((0, 32),), jnp.float32)
    w_mlp_in = bell_draw(keys[6], (D, FF), D ** -0.5, 0.125, ((0, 32),), jnp.float32)
    w_mlp_out = bell_draw(keys[7], (D, FF), FF ** -0.5, 0.0625, ((0, 32),), jnp.float32)
    vectors = draw_vectors(jax.random.fold_in(keys[19], 71), 0)
    first_qkv = bell_draw(keys[9], (D, 3 * D), 1.0, 6.0, ((0, 32),), jnp.float32)
    second_qkv = jnp.clip(jnp.exp(math.log(3276.8) - 2.7725887 * jax.random.uniform(keys[10], (D, 3 * D), jnp.float32) ** levels(keys[10], (D, 3 * D), ((0, 32),), -0.2, 0.2)), 204.8, 3276.8)
    first_attn_out = bell_draw(keys[11], (D, D), 1.0, 6.0, ((0, 32),), jnp.float32)
    second_attn_out = jnp.clip(jnp.exp(math.log(294.912) - 2.7725887 * jax.random.uniform(keys[12], (D, D), jnp.float32) ** levels(keys[12], (D, D), ((0, 32),), -0.2, 0.2)), 18.432, 294.912)
    first_mlp_in = bell_draw(keys[13], (D, FF), 1.0, 6.0, ((0, 32),), jnp.float32)
    second_mlp_in = jnp.clip(jnp.exp(math.log(819.2) - 2.7725887 * jax.random.uniform(keys[14], (D, FF), jnp.float32) ** levels(keys[14], (D, FF), ((0, 32),), -0.2, 0.2)), 51.2, 819.2)
    first_mlp_out = bell_draw(keys[15], (D, FF), 1.0, 6.0, ((0, 32),), jnp.float32)
    second_mlp_out = jnp.clip(jnp.exp(math.log(524.288) - 2.7725887 * jax.random.uniform(keys[16], (D, FF), jnp.float32) ** levels(keys[16], (D, FF), ((0, 32),), -0.2, 0.2)), 32.768, 524.288)
    first_vectors = bell_draw(keys[17], (VEC,), 1.0, 6.0, ((0, 32),), jnp.float32)
    second_vectors = jnp.clip(jnp.exp(math.log(52428.8) - 2.7725887 * jax.random.uniform(keys[18], (VEC,), jnp.float32) ** levels(keys[18], (VEC,), ((0, 32),), -0.2, 0.2)), 3276.8, 52428.8)
    return dict(tokens=tokens, cotangent=cotangent, block_first=block_first, block_live=block_live, w_qkv=w_qkv, w_attn_out=w_attn_out, w_mlp_in=w_mlp_in, w_mlp_out=w_mlp_out, vectors=vectors, first_qkv=first_qkv, second_qkv=second_qkv, first_attn_out=first_attn_out, second_attn_out=second_attn_out, first_mlp_in=first_mlp_in, second_mlp_in=second_mlp_in, first_mlp_out=first_mlp_out, second_mlp_out=second_mlp_out, first_vectors=first_vectors, second_vectors=second_vectors)


highest = lax.Precision.HIGHEST
eps_norm = 1e-05
beta_one = 0.9
beta_two = 0.95
learn_rate = 0.03
vector_rate = 0.3
decay_matrix = 0.1
eps_adam = 1e-08
masked_score = -1e+30

@jax.custom_vjp
def low(v):
    return lax.optimization_barrier(v.astype(jnp.bfloat16)).astype(jnp.float32)

@jax.custom_vjp
def low_back(v):
    return v

def low_keep(v):
    return (low(v), None)

def low_pass(kept, grad):
    return (grad,)

def back_keep(v):
    return (v, None)

def back_low(kept, grad):
    return (low(grad),)
low.defvjp(low_keep, low_pass)
low_back.defvjp(back_keep, back_low)

def layer_norm(values, gain_vec, shift_vec):
    row_mean = lax.optimization_barrier(jnp.mean(values, axis=-1, keepdims=True))
    centred = values - row_mean
    spread = lax.optimization_barrier(jnp.mean(centred * centred, axis=-1, keepdims=True))
    return centred * lax.rsqrt(spread + eps_norm) * gain_vec + shift_vec

def gelu_exact(values):
    return jax.nn.gelu(values, approximate=False)

def split_vectors(vec_all):
    boundaries = [D, 2 * D, 3 * D, 3 * D + FF, 4 * D + FF, 5 * D + FF, 6 * D + FF, 7 * D + FF]
    b_query, b_value, b_att, b_in, b_mlp, gain_one, shift_one, gain_two, shift_two = jnp.split(vec_all, boundaries)
    b_qkv = jnp.concatenate([b_query, jnp.zeros_like(b_query), b_value])
    return (b_qkv, b_att, b_in, b_mlp, gain_one, shift_one, gain_two, shift_two)

def slot_tables(first_blocks, live_blocks):
    slot_index = jnp.arange(SLOTS, dtype=jnp.int32)
    seq_of = jnp.broadcast_to(first_blocks[:, None], (BLK_DEV, BLOCK)).reshape(SLOTS)
    live_of = jnp.broadcast_to(live_blocks[:, None], (BLK_DEV, BLOCK)).reshape(SLOTS)
    offset = slot_index % BLOCK
    position = (slot_index - seq_of * BLOCK).astype(jnp.float32)
    alive_slot = offset < live_of
    allowed = (seq_of[:, None] == seq_of[None, :]) & (slot_index[None, :] <= slot_index[:, None]) & (alive_slot[None, :] | (slot_index[None, :] == slot_index[:, None]))
    return (position, alive_slot, allowed)

def rotary_tables(position):
    frequency = 10000.0 ** (-(2.0 * jnp.arange(ROT // 2, dtype=jnp.float32)) / ROT)
    angles = position[:, None] * frequency[None, :]
    cosine_table = jnp.concatenate([jnp.cos(angles), jnp.cos(angles)], axis=1)
    sine_table = jnp.concatenate([jnp.sin(angles), jnp.sin(angles)], axis=1)
    return (cosine_table, sine_table)

def apply_rotary(values, cosine_table, sine_table):
    rot_part = values[..., :ROT]
    turned = jnp.concatenate([-rot_part[..., ROT // 2:], rot_part[..., :ROT // 2]], axis=-1)
    rotated = rot_part * cosine_table[:, None, :] + turned * sine_table[:, None, :]
    return jnp.concatenate([rotated, values[..., ROT:]], axis=-1)

def buffer_forward(inputs, first_blocks, live_blocks, w_qkv, w_attn_out, w_mlp_in, w_mlp_out, vec_all):
    position, alive_slot, allowed = slot_tables(first_blocks, live_blocks)
    cosine_table, sine_table = rotary_tables(position)
    b_qkv, b_att, b_in, b_mlp, gain_one, shift_one, gain_two, shift_two = split_vectors(vec_all)
    attn_in = low(layer_norm(inputs, gain_one, shift_one))
    mixed_qkv = jnp.dot(attn_in, w_qkv, precision=highest, preferred_element_type=jnp.float32) + b_qkv
    mixed_qkv = low_back(mixed_qkv).reshape(SLOTS, 3, HEADS, HEAD)
    queries = low(apply_rotary(mixed_qkv[:, 0], cosine_table, sine_table))
    keys_rot = low(apply_rotary(mixed_qkv[:, 1], cosine_table, sine_table))
    values = low(mixed_qkv[:, 2])
    scores = jnp.einsum('qhd,khd->hqk', queries, keys_rot, precision=highest) * HEAD ** (-0.5)
    scores = low_back(scores)
    scores = jnp.where(allowed[None], scores, masked_score)
    row_max = lax.optimization_barrier(jnp.max(scores, axis=-1, keepdims=True))
    raised = jnp.exp(scores - row_max)
    weights_soft = raised / lax.optimization_barrier(jnp.sum(raised, axis=-1, keepdims=True))
    attended = jnp.einsum('hqk,khd->qhd', low(weights_soft), values, precision=highest).reshape(SLOTS, D)
    attended = low(low_back(attended))
    attn_branch = jnp.dot(attended, w_attn_out.T, precision=highest, preferred_element_type=jnp.float32) + b_att
    mlp_in = low(layer_norm(inputs, gain_two, shift_two))
    hidden = low_back(jnp.dot(mlp_in, w_mlp_in, precision=highest, preferred_element_type=jnp.float32) + b_in)
    activated = low(gelu_exact(hidden))
    mlp_branch = jnp.dot(activated, w_mlp_out.T, precision=highest, preferred_element_type=jnp.float32) + b_mlp
    return inputs + attn_branch + mlp_branch

def forward(inputs, w_qkv, w_attn_out, w_mlp_in, w_mlp_out, vectors, block_first, block_live):
    low_qkv = low(w_qkv)
    low_att = low(w_attn_out)
    low_in = low(w_mlp_in)
    low_out = low(w_mlp_out)
    low_vec = low(vectors)

    def buffer_step(pieces):
        return buffer_forward(pieces[0], pieces[1], pieces[2], low_qkv, low_att, low_in, low_out, low_vec)
    stacked = (inputs.reshape(N_FSDP, SLOTS, D), block_first.reshape(N_FSDP, BLK_DEV), block_live.reshape(N_FSDP, BLK_DEV))
    return lax.map(jax.checkpoint(buffer_step), stacked).reshape(TOKENS, D)

def adamw_update(weight, grad, first_m, second_m, rate_value, decay_value):
    first_new = beta_one * first_m + (1.0 - beta_one) * grad
    second_new = beta_two * second_m + (1.0 - beta_two) * grad * grad
    fix_one = 1.0 - beta_one ** STEP
    fix_two = 1.0 - beta_two ** STEP
    direction = first_new / fix_one / (jnp.sqrt(second_new / fix_two) + eps_adam)
    return (weight - rate_value * (direction + decay_value * weight), first_new, second_new)

def reference(tokens, cotangent, block_first, block_live, w_qkv, w_attn_out, w_mlp_in, w_mlp_out, vectors, first_qkv, second_qkv, first_attn_out, second_attn_out, first_mlp_in, second_mlp_in, first_mlp_out, second_mlp_out, first_vectors, second_vectors):
    inputs = tokens.astype(jnp.float32)

    def whole_layer(values, wq, wo, wi, wm, vec):
        return forward(values, wq, wo, wi, wm, vec, block_first, block_live)
    outputs, pullback = jax.vjp(whole_layer, inputs, w_qkv, w_attn_out, w_mlp_in, w_mlp_out, vectors)
    alive_tok = (jnp.arange(BLOCK, dtype=jnp.int32)[None, :] < block_live[:, None]).reshape(TOKENS)
    grad_seed = jnp.where(alive_tok[:, None], cotangent.astype(jnp.float32), jnp.float32(0.0))
    d_inputs, g_qkv, g_att, g_in, g_out, g_vec = pullback(grad_seed)
    new_qkv, m_qkv, u_qkv = adamw_update(w_qkv, g_qkv, first_qkv, second_qkv, learn_rate, decay_matrix)
    new_att, m_att, u_att = adamw_update(w_attn_out, g_att, first_attn_out, second_attn_out, learn_rate, decay_matrix)
    new_in, m_in, u_in = adamw_update(w_mlp_in, g_in, first_mlp_in, second_mlp_in, learn_rate, decay_matrix)
    new_out, m_out, u_out = adamw_update(w_mlp_out, g_out, first_mlp_out, second_mlp_out, learn_rate, decay_matrix)
    new_vec, m_vec, u_vec = adamw_update(vectors, g_vec, first_vectors, second_vectors, vector_rate, 0.0)
    return (outputs.astype(jnp.bfloat16), d_inputs.astype(jnp.bfloat16), g_qkv, g_att, g_in, g_out, g_vec, new_qkv, new_att, new_in, new_out, new_vec, m_qkv, u_qkv, m_att, u_att, m_in, u_in, m_out, u_out, m_vec, u_vec)
```

```python
import jax
import jax.numpy as jnp
from jax import lax
from jax.sharding import Mesh, PartitionSpec as P

D = 2048
HEADS = 8
HEAD = 256
FF = 8192
ROT = 64
BLOCK = 128
BLK_DEV = 2
STEP = 3
VEC = 24576
TEAM = 8
SLICE_FF = FF // TEAM

eps_norm = 1e-05
beta_one = 0.9
beta_two = 0.95
learn_rate = 0.03
vector_rate = 0.3
decay_matrix = 0.1
eps_adam = 1e-08
masked_score = -1e30
contract_rows = (((0,), (0,)), ((), ()))
contract_cols = (((1,), (1,)), ((), ()))
bf16 = jnp.bfloat16
f32 = jnp.float32
PLANE = ("row", "col", "core")
EVERY = ("far", "row", "col", "core")


def dot(left, right, dims=(((1,), (0,)), ((), ()))):
    return lax.dot_general(left, right, dims, preferred_element_type=f32)


def split_vectors(vec_all):
    boundaries = [D, 2 * D, 3 * D, 3 * D + FF, 4 * D + FF, 5 * D + FF, 6 * D + FF, 7 * D + FF]
    return jnp.split(vec_all, boundaries)


def slot_tables(first_blocks, live_blocks, slot_total):
    slot_index = jnp.arange(slot_total, dtype=jnp.int32)
    seq_of = jnp.repeat(first_blocks, BLOCK, axis=-1)
    live_of = jnp.repeat(live_blocks, BLOCK, axis=-1)
    offset = slot_index % BLOCK
    position = (slot_index - seq_of * BLOCK).astype(f32)
    alive_slot = offset < live_of
    same = seq_of[..., :, None] == seq_of[..., None, :]
    causal = slot_index[None, :] <= slot_index[:, None]
    itself = slot_index[None, :] == slot_index[:, None]
    allowed = same & causal & (alive_slot[..., None, :] | itself)
    return (position, alive_slot, allowed)


def rotary_tables(position):
    frequency = 10000.0 ** (-(2.0 * jnp.arange(ROT // 2, dtype=f32)) / ROT)
    angles = position[:, None] * frequency[None, :]
    cosine_table = jnp.concatenate([jnp.cos(angles), jnp.cos(angles)], axis=1)
    sine_table = jnp.concatenate([jnp.sin(angles), jnp.sin(angles)], axis=1)
    return (cosine_table, sine_table)


def apply_rotary(values, cosine_table, sine_table):
    rot_part = values[..., :ROT]
    turned = jnp.concatenate([-rot_part[..., ROT // 2 :], rot_part[..., : ROT // 2]], axis=-1)
    rotated = rot_part * cosine_table + turned * sine_table
    return jnp.concatenate([rotated, values[..., ROT:]], axis=-1)


def adamw_update(weight, grad, first_m, second_m, rate_value, decay_value):
    first_new = beta_one * first_m + (1.0 - beta_one) * grad
    second_new = beta_two * second_m + (1.0 - beta_two) * grad * grad
    fix_one = 1.0 - beta_one**STEP
    fix_two = 1.0 - beta_two**STEP
    direction = first_new / fix_one / (jnp.sqrt(second_new / fix_two) + eps_adam)
    return (weight - rate_value * (direction + decay_value * weight), first_new, second_new)


def normalize(values):
    centred = values - jnp.mean(values, axis=-1, keepdims=True)
    spread = jnp.mean(centred * centred, axis=-1, keepdims=True)
    scale = lax.rsqrt(spread + eps_norm)
    return centred * scale, scale


def body(
    tokens,
    cotangent,
    block_first,
    block_live,
    w_qkv,
    w_attn_out,
    w_mlp_in,
    w_mlp_out,
    vectors,
    first_qkv,
    second_qkv,
    first_attn_out,
    second_attn_out,
    first_mlp_in,
    second_mlp_in,
    first_mlp_out,
    second_mlp_out,
    first_vectors,
    second_vectors,
):
    groups = lax.axis_size("far")
    slot_total = tokens.shape[0]
    rows_dev = w_qkv.shape[0]
    rows_group = rows_dev * TEAM
    team_slots = slot_total * TEAM
    me = lax.axis_index(PLANE)

    attn_send = jnp.concatenate(
        [
            w_qkv.astype(bf16).reshape(rows_dev, 3, TEAM, HEAD).transpose(2, 0, 1, 3).reshape(TEAM, rows_dev, 3 * HEAD),
            w_attn_out.astype(bf16).reshape(rows_dev, TEAM, HEAD).transpose(1, 0, 2),
        ],
        axis=2,
    )
    mlp_send = jnp.concatenate(
        [
            w_mlp_in.astype(bf16).reshape(rows_dev, TEAM, SLICE_FF).transpose(1, 0, 2),
            w_mlp_out.astype(bf16).reshape(rows_dev, TEAM, SLICE_FF).transpose(1, 0, 2),
        ],
        axis=2,
    )

    def fetch(block):
        got = lax.all_to_all(block, PLANE, 0, 0, tiled=True)
        return lax.all_gather(got.reshape(rows_group, block.shape[2]), "far", axis=0, tiled=True)

    attn_w = fetch(attn_send)
    mlp_w = fetch(mlp_send)
    wq, wo = attn_w[:, : 3 * HEAD], attn_w[:, 3 * HEAD :]
    wi, wm = mlp_w[:, :SLICE_FF], mlp_w[:, SLICE_FF:]
    vec_full = lax.all_gather(vectors.astype(bf16), EVERY, axis=0, tiled=True).astype(f32)
    b_query, b_value, b_att, b_in, b_mlp, gain_one, shift_one, gain_two, shift_two = split_vectors(vec_full)

    alive_own = jnp.repeat(
        jnp.arange(BLOCK, dtype=jnp.int32)[None, :] < block_live[:, None], 1, axis=0
    ).reshape(slot_total)
    seed_own = jnp.where(alive_own[:, None], cotangent, jnp.zeros_like(cotangent))
    x_team = lax.all_gather(tokens, PLANE, axis=0, tiled=True)
    seed = lax.all_gather(seed_own, PLANE, axis=0, tiled=True)
    blocks = lax.all_gather(jnp.stack([block_first, block_live]), PLANE, axis=0, tiled=False)
    position, alive_slot, allowed = slot_tables(blocks[:, 0], blocks[:, 1], slot_total)
    cosine_table, sine_table = rotary_tables(position.reshape(team_slots))

    xhat, _ = normalize(x_team.astype(f32))
    attn_in = (xhat * gain_one + shift_one).astype(bf16)
    mlp_in = (xhat * gain_two + shift_two).astype(bf16)

    bias_q = lax.dynamic_slice(b_query, (me * HEAD,), (HEAD,))
    bias_v = lax.dynamic_slice(b_value, (me * HEAD,), (HEAD,))
    mixed = dot(attn_in, wq)
    shape = (TEAM, slot_total, HEAD)
    queries = apply_rotary(mixed[:, :HEAD] + bias_q, cosine_table, sine_table).astype(bf16).reshape(shape)
    keys_rot = apply_rotary(mixed[:, HEAD : 2 * HEAD], cosine_table, sine_table).astype(bf16).reshape(shape)
    values = (mixed[:, 2 * HEAD :] + bias_v).astype(bf16).reshape(shape)
    scores = jnp.einsum("bqd,bkd->bqk", queries, keys_rot, preferred_element_type=f32) * HEAD ** (-0.5)
    scores = jnp.where(allowed, scores, masked_score)
    raised = jnp.exp(scores - jnp.max(scores, axis=-1, keepdims=True))
    weights_soft = raised / jnp.sum(raised, axis=-1, keepdims=True)
    weights_low = weights_soft.astype(bf16)
    attended = (
        jnp.einsum("bqk,bkd->bqd", weights_low, values, preferred_element_type=f32).astype(bf16).reshape(team_slots, HEAD)
    )
    bias_in = lax.dynamic_slice(b_in, (me * SLICE_FF,), (SLICE_FF,))
    hidden = dot(mlp_in, wi) + bias_in
    activated_f, gelu_back = jax.vjp(lambda v: jax.nn.gelu(v, approximate=False), hidden)
    activated = activated_f.astype(bf16)
    part_out = dot(attended, wo, contract_cols) + dot(activated, wm, contract_cols)
    branch = lax.psum_scatter(part_out.astype(bf16), PLANE, scatter_dimension=0, tiled=True)
    inputs = tokens.astype(f32)
    out = (inputs + branch.astype(f32) + (b_att + b_mlp)).astype(bf16)

    d_hidden = gelu_back(dot(seed, wm))[0].astype(bf16)
    d_attended = dot(seed, wo).astype(bf16).reshape(shape)
    d_weights = jnp.einsum("bqd,bkd->bqk", d_attended, values, preferred_element_type=f32)
    row_inner = jnp.sum(weights_soft * d_weights, axis=-1, keepdims=True)
    d_scores = (weights_soft * (d_weights - row_inner)).astype(bf16)
    d_queries = jnp.einsum("bqk,bkd->bqd", d_scores, keys_rot, preferred_element_type=f32) * HEAD ** (-0.5)
    d_keys = jnp.einsum("bqk,bqd->bkd", d_scores, queries, preferred_element_type=f32) * HEAD ** (-0.5)
    d_values = jnp.einsum("bqk,bqd->bkd", weights_low, d_attended, preferred_element_type=f32)
    d_mixed = jnp.concatenate(
        [
            apply_rotary(d_queries.reshape(team_slots, HEAD), cosine_table, -sine_table),
            apply_rotary(d_keys.reshape(team_slots, HEAD), cosine_table, -sine_table),
            d_values.reshape(team_slots, HEAD),
        ],
        axis=1,
    ).astype(bf16)
    d_attn_in = dot(d_mixed, wq, contract_cols)
    d_mlp_in = dot(d_hidden, wi, contract_cols)
    d_gain_one = jnp.sum(d_attn_in * xhat, axis=0)
    d_shift_one = jnp.sum(d_attn_in, axis=0)
    d_gain_two = jnp.sum(d_mlp_in * xhat, axis=0)
    d_shift_two = jnp.sum(d_mlp_in, axis=0)
    part_back = d_attn_in * gain_one + d_mlp_in * gain_two
    back = lax.psum_scatter(part_back.astype(bf16), PLANE, scatter_dimension=0, tiled=True).astype(f32)
    own_hat, own_scale = normalize(inputs)
    seed_f = seed_own.astype(f32)
    d_inputs = own_scale * (
        back
        - jnp.mean(back, axis=-1, keepdims=True)
        - own_hat * jnp.mean(back * own_hat, axis=-1, keepdims=True)
    )
    grad_tokens = (seed_f + d_inputs).astype(bf16)

    attn_term = jnp.concatenate(
        [dot(attn_in, d_mixed, contract_rows), dot(seed, attended, contract_rows)], axis=1
    ).astype(bf16)
    mlp_term = jnp.concatenate(
        [dot(mlp_in, d_hidden, contract_rows), dot(seed, activated, contract_rows)], axis=1
    ).astype(bf16)

    def deliver(term):
        width = term.shape[1]
        mine = lax.psum_scatter(term, "far", scatter_dimension=0, tiled=True)
        return lax.all_to_all(mine.reshape(TEAM, rows_dev, width), PLANE, 0, 0, tiled=True)

    attn_got = deliver(attn_term).astype(f32)
    mlp_got = deliver(mlp_term).astype(f32)
    grad_qkv = (
        attn_got[:, :, : 3 * HEAD].reshape(TEAM, rows_dev, 3, HEAD).transpose(1, 2, 0, 3).reshape(rows_dev, 3 * D)
    )
    grad_attn_out = attn_got[:, :, 3 * HEAD :].transpose(1, 0, 2).reshape(rows_dev, D)
    grad_mlp_in = mlp_got[:, :, :SLICE_FF].transpose(1, 0, 2).reshape(rows_dev, FF)
    grad_mlp_out = mlp_got[:, :, SLICE_FF:].transpose(1, 0, 2).reshape(rows_dev, FF)

    seed_sum = jnp.sum(seed_f, axis=0)
    mixed_sum = jnp.sum(d_mixed.astype(f32), axis=0)
    hidden_sum = jnp.sum(d_hidden.astype(f32), axis=0)

    def place(part, width):
        return lax.dynamic_update_slice(jnp.zeros((width,), f32), part, (me * part.shape[0],))

    local_vec = jnp.concatenate(
        [
            place(mixed_sum[:HEAD], D),
            place(mixed_sum[2 * HEAD :], D),
            seed_sum,
            place(hidden_sum, FF),
            seed_sum,
            d_gain_one,
            d_shift_one,
            d_gain_two,
            d_shift_two,
        ]
    )
    piece = vectors.shape[0]
    vec_terms = local_vec.reshape(groups, TEAM, piece).transpose(1, 0, 2)
    vec_plane = jnp.sum(lax.all_to_all(vec_terms, PLANE, 0, 0, tiled=True), axis=0)
    vec_line = lax.all_to_all(vec_plane, "far", 0, 0, tiled=True)
    grad_vectors = jnp.sum(vec_line, axis=0)

    new_qkv, m_qkv, u_qkv = adamw_update(w_qkv, grad_qkv, first_qkv, second_qkv, learn_rate, decay_matrix)
    new_att, m_att, u_att = adamw_update(
        w_attn_out, grad_attn_out, first_attn_out, second_attn_out, learn_rate, decay_matrix
    )
    new_in, m_in, u_in = adamw_update(w_mlp_in, grad_mlp_in, first_mlp_in, second_mlp_in, learn_rate, decay_matrix)
    new_out, m_out, u_out = adamw_update(
        w_mlp_out, grad_mlp_out, first_mlp_out, second_mlp_out, learn_rate, decay_matrix
    )
    new_vec, m_vec, u_vec = adamw_update(vectors, grad_vectors, first_vectors, second_vectors, vector_rate, 0.0)
    return (
        out,
        grad_tokens,
        grad_qkv,
        grad_attn_out,
        grad_mlp_in,
        grad_mlp_out,
        grad_vectors,
        new_qkv,
        new_att,
        new_in,
        new_out,
        new_vec,
        m_qkv,
        u_qkv,
        m_att,
        u_att,
        m_in,
        u_in,
        m_out,
        u_out,
        m_vec,
        u_vec,
    )


def solution(mesh):
    devices = mesh.devices.reshape(-1)
    layout = Mesh(devices.reshape(devices.size // TEAM, 2, 2, 2), EVERY)
    matrix, line = P(EVERY, None), P(EVERY)
    in_specs = (matrix, matrix, line, line) + (matrix,) * 4 + (line,) + (matrix,) * 8 + (line,) * 2
    out_specs = (matrix,) * 6 + (line,) + (matrix,) * 4 + (line,) + (matrix,) * 8 + (line,) * 2
    return jax.shard_map(body, mesh=layout, in_specs=in_specs, out_specs=out_specs, check_vma=False)
```

```python
import jax
import jax.numpy as jnp
from jax import lax
from jax.experimental import pallas as pl
from jax.experimental.pallas import tpu as pltpu
from jax.sharding import Mesh, PartitionSpec as P

D = 2048
HEADS = 8
HEAD = 256
FF = 8192
ROT = 64
BLOCK = 128
BLK_DEV = 2
STEP = 3
VEC = 24576
TEAM = 8
SLICE_FF = FF // TEAM
CHUNKS = ((0, 256), None, (512, 1024), (256, 512))
PACK_ROWS = 16
FENCE = 20000
LANES = 128

eps_norm = 1e-05
beta_one = 0.9
beta_two = 0.95
learn_rate = 0.03
vector_rate = 0.3
decay_matrix = 0.1
eps_adam = 1e-08
masked_score = -1e30
plain = (((1,), (0,)), ((), ()))
contract_rows = (((0,), (0,)), ((), ()))
contract_cols = (((1,), (1,)), ((), ()))
bf16 = jnp.bfloat16
f32 = jnp.float32
VMEM_BYTES = 56 * 1024 * 1024
NEAR = ("low", "row", "core")
CROSS = ("col", "far")
EVERY = ("far", "low", "row", "col", "core")
SWAP = [(0, 1), (1, 0)]
COST_UNIT = 115000000
ANYWHERE = pl.BlockSpec(memory_space=pl.ANY)


def dot(left, right, dims=plain):
    return lax.dot_general(left, right, dims, preferred_element_type=f32)


def after(value, *others):
    return lax.optimization_barrier((value, *others))[0]


def params(cost):
    return dict(
        compiler_params=pltpu.CompilerParams(vmem_limit_bytes=VMEM_BYTES),
        cost_estimate=pl.CostEstimate(flops=int(cost * COST_UNIT), bytes_accessed=1024, transcendentals=0),
    )


def shaped(shape, dtype):
    return jax.ShapeDtypeStruct(shape, dtype)


def blocks(shape, index):
    return pl.BlockSpec(shape, index)


def split_vectors(vec_all):
    boundaries = [D, 2 * D, 3 * D, 3 * D + FF, 4 * D + FF, 5 * D + FF, 6 * D + FF, 7 * D + FF]
    return jnp.split(vec_all, boundaries)


def adamw_update(weight, grad, first_m, second_m, rate_value, decay_value):
    first_new = beta_one * first_m + (1.0 - beta_one) * grad
    second_new = beta_two * second_m + (1.0 - beta_two) * grad * grad
    fix_one = 1.0 - beta_one**STEP
    fix_two = 1.0 - beta_two**STEP
    direction = first_new / fix_one / (jnp.sqrt(second_new / fix_two) + eps_adam)
    return (weight - rate_value * (direction + decay_value * weight), first_new, second_new)


def normalize(values):
    centred = values - jnp.mean(values, axis=-1, keepdims=True)
    spread = jnp.mean(centred * centred, axis=-1, keepdims=True)
    scale = lax.rsqrt(spread + eps_norm)
    return centred * scale, scale


def rotary_rows(position):
    lane = jnp.arange(LANES)
    frequency = 10000.0 ** (-(2.0 * (lane % (ROT // 2)).astype(f32)) / ROT)
    angles = position[:, None] * frequency[None, :]
    sine = jnp.sin(angles)
    cosine = jnp.where(lane < ROT, jnp.cos(angles), 1.0)
    return (
        cosine,
        jnp.where(lane < ROT // 2, -sine, 0.0),
        jnp.where((lane >= ROT // 2) & (lane < ROT), sine, 0.0),
    )


def gelu_pair(hidden):
    cumulative = 0.5 * (1.0 + lax.erf(hidden * (0.5**0.5)))
    density = jnp.exp(-0.5 * hidden * hidden) * 0.3989422804014327
    return hidden * cumulative, cumulative + hidden * density


def stacked_copies(refs, buffer, sems, rows_dev, columns=None):
    copies, begin = [], 0
    for ref in refs:
        parts = [ref] if len(ref.shape) == 2 else [ref.at[k, 0:rows_dev] for k in range(ref.shape[0])]
        for part in parts:
            rows = part.shape[0]
            source = part if columns is None else part.at[:, columns]
            copies.append(pltpu.make_async_copy(source, buffer.at[begin : begin + rows], sems.at[len(copies)]))
            begin += rows
    return copies


def copy_count(pieces):
    return sum(1 if piece.ndim == 2 else piece.shape[0] for piece in pieces)


def member_copies(members_ref, team_ref, kind, buffer, sems):
    count, both, _ = team_ref.shape
    rows = both // 2
    return [
        pltpu.make_async_copy(
            team_ref.at[members_ref[k], kind * rows : (kind + 1) * rows],
            buffer.at[k * rows : (k + 1) * rows],
            sems.at[k],
        )
        for k in range(count)
    ]


def prepare_tokens(order, live, tokens, cotangent):
    slots = tokens.shape[0]

    def kernel(order_ref, live_ref, x_ref, y_ref, both_ref):
        row = lax.broadcasted_iota(jnp.int32, (slots, LANES), 0)
        end = jnp.where(row < BLOCK, live_ref[0], live_ref[1] + BLOCK)
        alive = row < end
        for k in range(D // LANES):
            source = pl.ds(pl.multiple_of(order_ref[k] * LANES, LANES), LANES)
            here = slice(k * LANES, (k + 1) * LANES)
            both_ref[:slots, here] = x_ref[:, source]
            both_ref[slots:, here] = jnp.where(alive, y_ref[:, source].astype(f32), 0.0).astype(bf16)

    whole = blocks((slots, D), lambda i, *_: (0, 0))
    return pl.pallas_call(
        kernel,
        grid_spec=pltpu.PrefetchScalarGridSpec(
            num_scalar_prefetch=2,
            grid=(1,),
            in_specs=[whole, whole],
            out_specs=blocks((2 * slots, D), lambda i, *_: (0, 0)),
        ),
        out_shape=shaped((2 * slots, D), bf16),
        **params(4),
    )(order, live, tokens, cotangent)


def norm_inputs(members, team, gain_one, shift_one, gain_two, shift_two):
    count, both, _ = team.shape
    rows = both // 2

    def kernel(members_ref, team_ref, g1, s1, g2, s2, one_ref, two_ref, hat_ref, buffer, sems):
        step = pl.program_id(0)
        copies = member_copies(members_ref, team_ref, 0, buffer, sems)

        @pl.when(step == 0)
        def _():
            for copy in copies:
                copy.start()

        for k in range(count):

            @pl.when(step == k)
            def _(k=k):
                copies[k].wait()

        hat, _ = normalize(buffer[pl.ds(pl.multiple_of(step * rows, rows), rows), :].astype(f32))
        hat_ref[...] = hat.astype(bf16)
        one_ref[...] = (hat * g1[...] + s1[...]).astype(bf16)
        two_ref[...] = (hat * g2[...] + s2[...]).astype(bf16)

    line = blocks((1, D), lambda i, *_: (0, 0))
    return pl.pallas_call(
        kernel,
        grid_spec=pltpu.PrefetchScalarGridSpec(
            num_scalar_prefetch=1,
            grid=(count,),
            in_specs=[ANYWHERE] + [line] * 4,
            out_specs=[blocks((rows, D), lambda i, *_: (i, 0))] * 3,
            scratch_shapes=[pltpu.VMEM((count * rows, D), bf16), pltpu.SemaphoreType.DMA((count,))],
        ),
        out_shape=[shaped((count * rows, D), bf16)] * 3,
        **params(FENCE),
    )(members, team, gain_one, shift_one, gain_two, shift_two)


def open_chunk(step, rows, rows_dev, members_ref, team_ref, w_refs, y_all, w_all, y_sems, w_sems):
    y_copies = member_copies(members_ref, team_ref, 1, y_all, y_sems)
    w_copies = stacked_copies(w_refs, w_all, w_sems, rows_dev)
    slots = team_ref.shape[1] // 2

    @pl.when(step == 0)
    def _():
        for copy in w_copies + y_copies:
            copy.start()
        for copy in w_copies:
            copy.wait()

    for k, copy in enumerate(y_copies):

        @pl.when(step == k * slots // rows)
        def _(copy=copy):
            copy.wait()

    return y_all[pl.ds(pl.multiple_of(step * rows, rows), rows), :]


def close_chunk(step, last, acc_ref, keep_ref, send_ref, sum_ref, cols, first_term, second_term, column_sum):
    @pl.when(step == 0)
    def _():
        acc_ref[:, :cols] = first_term
        acc_ref[:, cols:] = second_term
        sum_ref[...] = column_sum

    @pl.when((step > 0) & (step < last))
    def _():
        acc_ref[:, :cols] += first_term
        acc_ref[:, cols:] += second_term
        sum_ref[...] += column_sum

    @pl.when(step == last)
    def _():
        half = D // 2
        keep_ref[:, :cols] = (acc_ref[:half, :cols] + first_term[:half]).astype(bf16)
        keep_ref[:, cols:] = (acc_ref[:half, cols:] + second_term[:half]).astype(bf16)
        send_ref[:, :cols] = (acc_ref[half:, :cols] + first_term[half:]).astype(bf16)
        send_ref[:, cols:] = (acc_ref[half:, cols:] + second_term[half:]).astype(bf16)
        sum_ref[...] += column_sum


def chunk_scratch(total, width, y_count, w_count):
    return [
        pltpu.VMEM((D, width), f32),
        pltpu.VMEM((total, D), bf16),
        pltpu.VMEM((D, width), bf16),
        pltpu.SemaphoreType.DMA((y_count,)),
        pltpu.SemaphoreType.DMA((w_count,)),
    ]


def mlp_chunk(members, team, a, w_pieces, b, rows_dev, rows=512):
    total, width = a.shape[0], w_pieces[0].shape[-1]
    cols = width // 2
    nw = len(w_pieces)

    def kernel(members_ref, team_ref, *refs):
        w_refs = refs[:nw]
        a_ref, b_ref, act_ref, dh_ref, keep_ref, send_ref, sum_ref, acc_ref, y_all, w_all, y_sems, w_sems = refs[nw:]
        step, last = pl.program_id(0), pl.num_programs(0) - 1
        y = open_chunk(step, rows, rows_dev, members_ref, team_ref, w_refs, y_all, w_all, y_sems, w_sems)
        a = a_ref[...]
        act, slope = gelu_pair(dot(a, w_all[:, :cols]) + b_ref[...])
        act = act.astype(bf16)
        dh = (dot(y, w_all[:, cols:]) * slope).astype(bf16)
        act_ref[...] = act
        dh_ref[...] = dh
        column_sum = jnp.sum(dh.astype(f32), axis=0, keepdims=True)
        first_term, second_term = dot(a, dh, contract_rows), dot(y, act, contract_rows)
        close_chunk(step, last, acc_ref, keep_ref, send_ref, sum_ref, cols, first_term, second_term, column_sum)

    fixed = lambda r, c: blocks((r, c), lambda i, *_: (0, 0))
    moving = lambda c: blocks((rows, c), lambda i, *_: (i, 0))
    return pl.pallas_call(
        kernel,
        grid_spec=pltpu.PrefetchScalarGridSpec(
            num_scalar_prefetch=1,
            grid=(total // rows,),
            in_specs=[ANYWHERE] * (1 + nw) + [moving(D), fixed(1, cols)],
            out_specs=[moving(cols), moving(cols), fixed(D // 2, width), fixed(D // 2, width), fixed(1, cols)],
            scratch_shapes=chunk_scratch(total, width, team.shape[0], copy_count(w_pieces)),
        ),
        out_shape=[shaped((total, cols), bf16)] * 2 + [shaped((D // 2, width), bf16)] * 2 + [shaped((1, cols), f32)],
        **params(FENCE if width > D // 4 else 15),
    )(members, team, *w_pieces, a, b)


def turn_lanes(values, cosine, low_sine, high_sine):
    part = values[:, :LANES]
    part = part * cosine + pltpu.roll(part, LANES - ROT // 2, 1) * low_sine + pltpu.roll(part, ROT // 2, 1) * high_sine
    return jnp.concatenate([part, values[:, LANES:]], axis=1)


def attn_chunk(members, first, live, team, a, w_pieces, b, rotary, rows_dev, rows=512):
    total, width = a.shape[0], w_pieces[0].shape[-1]
    nw = len(w_pieces)
    slots = BLK_DEV * BLOCK
    buffers = rows // slots

    def kernel(members_ref, first_ref, live_ref, team_ref, *refs):
        w_refs = refs[:nw]
        a_ref, b_ref, cos_ref, low_ref, high_ref, att_ref, dm_ref, keep_ref, send_ref, sum_ref = refs[nw : nw + 10]
        acc_ref, y_all, w_all, y_sems, w_sems = refs[nw + 10 :]
        step, last = pl.program_id(0), pl.num_programs(0) - 1
        y = open_chunk(step, rows, rows_dev, members_ref, team_ref, w_refs, y_all, w_all, y_sems, w_sems)
        a = a_ref[...]
        mixed = dot(a, w_all[:, : 3 * HEAD]) + b_ref[...]
        datt_all = dot(y, w_all[:, 3 * HEAD :]).astype(bf16)
        row = lax.broadcasted_iota(jnp.int32, (slots, slots), 0)
        col = lax.broadcasted_iota(jnp.int32, (slots, slots), 1)
        for k in range(buffers):
            buf = step * buffers + k
            part = slice(k * slots, (k + 1) * slots)
            cosine, low_sine, high_sine = cos_ref[part], low_ref[part], high_ref[part]
            queries = turn_lanes(mixed[part, :HEAD], cosine, low_sine, high_sine).astype(bf16)
            keys = turn_lanes(mixed[part, HEAD : 2 * HEAD], cosine, low_sine, high_sine).astype(bf16)
            values = mixed[part, 2 * HEAD :].astype(bf16)
            datt = datt_all[part]
            parted = jnp.where(first_ref[buf, 0] == first_ref[buf, 1], 0, 1)
            live_end = jnp.where(col < BLOCK, live_ref[buf, 0], live_ref[buf, 1] + BLOCK)
            other = jnp.where((row >= BLOCK) & (col < BLOCK), parted, 0)
            allowed = (col <= row) & (other == 0) & ((col < live_end) | (col == row))
            scores = jnp.where(allowed, dot(queries, keys, contract_cols) * HEAD ** (-0.5), masked_score)
            raised = jnp.exp(scores - jnp.max(scores, axis=1, keepdims=True))
            probs = raised / jnp.sum(raised, axis=1, keepdims=True)
            probs_low = probs.astype(bf16)
            att_ref[part] = dot(probs_low, values).astype(bf16)
            d_probs = dot(datt, values, contract_cols)
            d_scores = (probs * (d_probs - jnp.sum(probs * d_probs, axis=1, keepdims=True))).astype(bf16)
            d_queries = dot(d_scores, keys) * HEAD ** (-0.5)
            d_keys = dot(d_scores, queries, contract_rows) * HEAD ** (-0.5)
            dm_ref[part, :HEAD] = turn_lanes(d_queries, cosine, -low_sine, -high_sine).astype(bf16)
            dm_ref[part, HEAD : 2 * HEAD] = turn_lanes(d_keys, cosine, -low_sine, -high_sine).astype(bf16)
            dm_ref[part, 2 * HEAD :] = dot(probs_low, datt, contract_rows).astype(bf16)
        d_mixed = dm_ref[...]
        column_sum = jnp.sum(d_mixed.astype(f32), axis=0, keepdims=True)
        first_term, second_term = dot(a, d_mixed, contract_rows), dot(y, att_ref[...], contract_rows)
        close_chunk(step, last, acc_ref, keep_ref, send_ref, sum_ref, 3 * HEAD, first_term, second_term, column_sum)

    fixed = lambda r, c: blocks((r, c), lambda i, *_: (0, 0))
    moving = lambda c: blocks((rows, c), lambda i, *_: (i, 0))
    return pl.pallas_call(
        kernel,
        grid_spec=pltpu.PrefetchScalarGridSpec(
            num_scalar_prefetch=3,
            grid=(total // rows,),
            in_specs=[ANYWHERE] * (1 + nw) + [moving(D), fixed(1, 3 * HEAD)] + [moving(LANES)] * 3,
            out_specs=[moving(HEAD), moving(3 * HEAD), fixed(D // 2, width), fixed(D // 2, width), fixed(1, 3 * HEAD)],
            scratch_shapes=chunk_scratch(total, width, team.shape[0], copy_count(w_pieces)),
        ),
        out_shape=[shaped((total, HEAD), bf16), shaped((total, 3 * HEAD), bf16)]
        + [shaped((D // 2, width), bf16)] * 2
        + [shaped((1, 3 * HEAD), f32)],
        **params(FENCE),
    )(members, first, live, team, *w_pieces, a, b, *rotary)


def token_block(i, low_first):
    half = TEAM // 2
    within = i % half
    if low_first:
        within = within % 2 * 2 + within // 2
    return (i // half + 1) % 2 * half + within


def write_half(value, send_ref, keep_ref):
    first_half = pl.program_id(0) < TEAM // 2

    @pl.when(first_half)
    def _():
        send_ref[...] = value

    @pl.when(jnp.logical_not(first_half))
    def _():
        keep_ref[...] = value


def half_outputs(rows, total):
    half = TEAM // 2
    specs = [
        blocks((rows, D), lambda i: (jnp.minimum(i, half - 1), 0)),
        blocks((rows, D), lambda i: (jnp.maximum(i - half, 0), 0)),
    ]
    return specs, [shaped((total // 2, D), bf16)] * 2


def fetch_columns(groups, buffers, sems, places, rows_dev):
    copies = []
    for k, refs in enumerate(groups):
        begin, end = places[k]
        copies += stacked_copies(refs, buffers[k], sems[k], rows_dev, slice(begin, end))

    @pl.when(pl.program_id(0) == 0)
    def _():
        for copy in copies:
            copy.start()
        for copy in copies:
            copy.wait()


def out_part(lefts, weights, places, rows_dev):
    count, per, total = len(lefts), len(weights[0]), lefts[0].shape[0]
    rows = total // TEAM

    def kernel(*refs):
        groups = [refs[k * per : (k + 1) * per] for k in range(count)]
        left_refs = refs[count * per : count * per + count]
        send_ref, keep_ref, *scratch = refs[count * per + count :]
        fetch_columns(groups, scratch[:count], scratch[count:], places, rows_dev)
        buffers = scratch[:count]
        value = None
        for k in range(count):
            term = dot(left_refs[k][...], buffers[k][...], contract_cols)
            value = term if value is None else value + term
        write_half(value.astype(bf16), send_ref, keep_ref)

    specs, shapes = half_outputs(rows, total)
    return pl.pallas_call(
        kernel,
        grid=(TEAM,),
        in_specs=[ANYWHERE] * (count * per) + [blocks((rows, v.shape[1]), lambda i: (token_block(i, True), 0)) for v in lefts],
        out_specs=specs,
        out_shape=shapes,
        scratch_shapes=[pltpu.VMEM((D, e - b), bf16) for b, e in places]
        + [pltpu.SemaphoreType.DMA((copy_count(group),)) for group in weights],
        **params(19),
    )(*[piece for group in weights for piece in group], *lefts)


def back_part(hat, lefts, weights, places, attn_index, gain_one, gain_two, rows_dev):
    count, per, total = len(lefts), len(weights[0]), hat.shape[0]
    rows = total // TEAM

    def kernel(*refs):
        groups = [refs[k * per : (k + 1) * per] for k in range(count)]
        left_refs = refs[count * per : count * per + count]
        hat_ref, one_ref, two_ref, send_ref, keep_ref, sums_ref, *scratch = refs[count * per + count :]
        fetch_columns(groups, scratch[:count], scratch[count:], places, rows_dev)
        buffers = scratch[:count]
        d_one, d_two = None, None
        for k in range(count):
            term = dot(left_refs[k][...], buffers[k][...], contract_cols)
            if k == attn_index:
                d_one = term
            else:
                d_two = term if d_two is None else d_two + term
        write_half((d_one * one_ref[...] + d_two * two_ref[...]).astype(bf16), send_ref, keep_ref)
        hat_now = hat_ref[...].astype(f32)
        sums = [jnp.sum(v, axis=0, keepdims=True) for v in (d_one * hat_now, d_one, d_two * hat_now, d_two)]

        @pl.when(pl.program_id(0) == 0)
        def _():
            for k in range(4):
                sums_ref[k : k + 1] = sums[k]

        @pl.when(pl.program_id(0) > 0)
        def _():
            for k in range(4):
                sums_ref[k : k + 1] += sums[k]

    moving = lambda c: blocks((rows, c), lambda i: (token_block(i, False), 0))
    fixed = lambda r, c: blocks((r, c), lambda i: (0, 0))
    specs, shapes = half_outputs(rows, total)
    return pl.pallas_call(
        kernel,
        grid=(TEAM,),
        in_specs=[ANYWHERE] * (count * per)
        + [moving(v.shape[1]) for v in lefts]
        + [moving(D), fixed(1, D), fixed(1, D)],
        out_specs=specs + [fixed(8, D)],
        out_shape=shapes + [shaped((8, D), f32)],
        scratch_shapes=[pltpu.VMEM((D, e - b), bf16) for b, e in places]
        + [pltpu.SemaphoreType.DMA((copy_count(group),)) for group in weights],
        **params(FENCE),
    )(*[piece for group in weights for piece in group], *lefts, hat, gain_one, gain_two)


def split_sum(left, right, steps):
    rows, width = left.shape
    block = rows // 2 // steps

    def kernel(l_low, l_high, r_low, r_high, keep_ref, send_ref):
        keep_ref[...] = l_low[...].astype(f32) + r_low[...].astype(f32)
        send_ref[...] = (l_high[...].astype(f32) + r_high[...].astype(f32)).astype(bf16)

    low = blocks((block, width), lambda i: (i, 0))
    high = blocks((block, width), lambda i: (i + steps, 0))
    return pl.pallas_call(
        kernel,
        grid=(steps,),
        in_specs=[low, high, low, high],
        out_specs=[low, low],
        out_shape=[shaped((rows // 2, width), f32), shaped((rows // 2, width), bf16)],
        **params(4),
    )(left, left, right, right)


def last_sum(kept, got, steps, cost):
    rows, width = kept.shape

    def kernel(l_ref, r_ref, out_ref):
        out_ref[...] = (l_ref[...] + r_ref[...].astype(f32)).astype(bf16)

    spec = blocks((rows // steps, width), lambda i: (i, 0))
    return pl.pallas_call(
        kernel,
        grid=(steps,),
        in_specs=[spec, spec],
        out_specs=spec,
        out_shape=shaped((rows, width), bf16),
        **params(cost),
    )(kept, got)


def finish_tokens(order, tokens, other, kept, got, back):
    slots = tokens.shape[0]
    steps = 2
    rows = slots // steps

    def kernel(order_ref, x_ref, other_ref, kept_ref, got_ref, out_ref, sum_ref):
        for k in range(D // LANES):
            source = pl.ds(pl.multiple_of(order_ref[k] * LANES, LANES), LANES)
            sum_ref[:, k * LANES : (k + 1) * LANES] = kept_ref[:, source] + got_ref[:, source].astype(f32)
        total = sum_ref[...]
        x = x_ref[...].astype(f32)
        if back:
            hat, scale = normalize(x)
            inner = jnp.mean(total * hat, axis=-1, keepdims=True)
            total = scale * (total - jnp.mean(total, axis=-1, keepdims=True) - hat * inner)
            x = other_ref[...].astype(f32)
        else:
            total = total + other_ref[...]
        out_ref[...] = (x + total).astype(bf16)

    moving = blocks((rows, D), lambda i, *_: (i, 0))
    return pl.pallas_call(
        kernel,
        grid_spec=pltpu.PrefetchScalarGridSpec(
            num_scalar_prefetch=1,
            grid=(steps,),
            in_specs=[moving, moving if back else blocks((1, D), lambda i, *_: (0, 0)), moving, moving],
            out_specs=moving,
            scratch_shapes=[pltpu.VMEM((rows, D), f32)],
        ),
        out_shape=shaped((slots, D), bf16),
        **params(4),
    )(order, tokens, other, kept, got)


def adamw_columns(got, weight, first_m, second_m, section, unit, offset, sections, cost, held=None):
    rows, width = weight.shape
    span = TEAM * unit
    part = max(rows // 4, 16) if rows % 16 == 0 else rows
    got_spec = blocks((TEAM, part, unit), lambda k, i: (0, i, section + k))
    full = blocks((part, span), lambda k, i: (i, offset + k))

    def kernel(g_ref, w_ref, m_ref, u_ref, *refs):
        grad_ref, new_ref, mo_ref, uo_ref = refs[-4:]
        for k in range(TEAM):
            here = slice(k * unit, (k + 1) * unit)
            grad = g_ref[k].astype(f32)
            new, m_new, u_new = adamw_update(
                w_ref[:, here], grad, m_ref[:, here], u_ref[:, here], learn_rate, decay_matrix
            )
            grad_ref[:, here] = grad
            new_ref[:, here] = new
            mo_ref[:, here] = m_new
            uo_ref[:, here] = u_new

    extra = list(held) if held is not None else []
    return pl.pallas_call(
        kernel,
        grid=(sections, rows // part),
        in_specs=[got_spec, full, full, full] + [ANYWHERE] * len(extra),
        out_specs=[full] * 4,
        out_shape=[shaped((rows, width), f32)] * 4,
        input_output_aliases={4 + k: k for k in range(len(extra))},
        **params(cost),
    )(got, weight, first_m, second_m, *extra)


def body(
    tokens,
    cotangent,
    block_first,
    block_live,
    w_qkv,
    w_attn_out,
    w_mlp_in,
    w_mlp_out,
    vectors,
    first_qkv,
    second_qkv,
    first_attn_out,
    second_attn_out,
    first_mlp_in,
    second_mlp_in,
    first_mlp_out,
    second_mlp_out,
    first_vectors,
    second_vectors,
):
    far_size = lax.axis_size("far")
    paired = far_size == 2
    groups = 2 * far_size
    slot_total = tokens.shape[0]
    rows_dev = w_qkv.shape[0]
    rows_team = rows_dev * TEAM
    team_slots = slot_total * TEAM
    piece = vectors.shape[0]
    half = TEAM // 2
    count = len(CHUNKS)
    me = lax.axis_index(NEAR)
    far, column = lax.axis_index("far"), lax.axis_index("col")

    def flips(values, col_axis, far_axis):
        if not paired:
            return values
        values = jnp.where(column == 1, jnp.flip(values, col_axis), values)
        return jnp.where(far == 1, jnp.flip(values, far_axis), values)

    def local_order(values):
        lead = values.shape[:-1]
        k = len(lead)
        parts = values.reshape(*lead, far_size, half, 2, 2 * rows_dev)
        parts = jnp.transpose(parts, (*range(k), k + 2, k, k + 1, k + 3))
        return flips(parts, k, k + 1).reshape(*lead, D)

    def own_order(values):
        lead = values.shape[:-1]
        k = len(lead)
        parts = flips(values.reshape(*lead, 2, far_size, half, 2 * rows_dev), k, k + 1)
        return jnp.transpose(parts, (*range(k), k + 1, k + 2, k, k + 3)).reshape(*lead, D)

    place_in_row = jnp.arange(D // LANES, dtype=jnp.int32)
    if paired:
        c, f, r = place_in_row // (2 * half), place_in_row // half % 2, place_in_row % half
        to_local = ((f ^ far) * half + r) * 2 + (c ^ column)
        f, r, c = place_in_row // (2 * half), place_in_row // 2 % half, place_in_row % 2
        to_own = ((c ^ column) * 2 + (f ^ far)) * half + r
    else:
        to_local, to_own = place_in_row, place_in_row

    payload = jnp.concatenate([vectors.astype(bf16), block_first.astype(bf16), block_live.astype(bf16)])

    def columns(chunk):
        cut = lambda w, parts: w.astype(bf16).reshape(rows_dev, parts, TEAM, -1)
        if chunk is None:
            query = cut(w_qkv, 3).transpose(2, 0, 1, 3).reshape(TEAM, rows_dev, 3 * HEAD)
            return jnp.concatenate([query, cut(w_attn_out, 1)[:, 0].transpose(1, 0, 2)], axis=2)
        begin, end = chunk
        span = slice(TEAM * begin, TEAM * end)
        return jnp.concatenate([cut(w[:, span], 1)[:, 0].transpose(1, 0, 2) for w in (w_mlp_in, w_mlp_out)], axis=2)

    owns, far_got = [], [None] * count
    for index, chunk in enumerate(CHUNKS):
        block = columns(chunk)
        if index == 0 and paired:
            width = block.shape[2]
            extra = jnp.pad(payload, (0, PACK_ROWS * width - payload.shape[0])).reshape(1, PACK_ROWS, width)
            block = jnp.concatenate([block, jnp.broadcast_to(extra, (TEAM, PACK_ROWS, width))], axis=1)
        waits = owns[-1:]
        if paired and index == 2:
            far_got[0] = lax.ppermute(owns[0], "far", SWAP)
            waits = waits + far_got[:1]
        got = lax.all_to_all(after(block, *waits) if waits else block, NEAR, 0, 0, tiled=True)
        owns.append(got if got.shape[1] != rows_dev else got.reshape(rows_team, got.shape[2]))

    if paired:
        both_send = prepare_tokens(to_local, block_live, tokens, cotangent)
    else:
        both_send = prepare_tokens(to_local, block_live, local_order(tokens), local_order(cotangent))
    team = lax.all_gather(both_send, NEAR, axis=0, tiled=False)
    members = jnp.array([4 * l + 2 * r + c for c in range(2) for r in range(2) for l in range(2)], jnp.int32) ^ me

    w_chunks = []

    def send_far(index, *waits):
        far_got[index] = lax.ppermute(after(owns[index], far_got[index - 1], *waits), "far", SWAP)

    def cross(index, *waits):
        if paired:
            w_chunks[index][1] = far_got[index]
            over = after(far_got[index], *waits) if waits else far_got[index]
            w_chunks[index][3] = lax.ppermute(over, "col", SWAP)

    if paired:
        for own in owns:
            w_chunks.append([own, None, lax.ppermute(own, "col", SWAP), None])
        send_far(1, owns[2])
        send_far(2, owns[3])
    else:
        for own in owns:
            w_chunks.append([lax.all_gather(own, CROSS, axis=0, tiled=True)])
    cross(0)
    cross(1)

    length = piece + 2 * BLK_DEV
    if paired:
        got = jnp.stack([part[:, rows_dev:].reshape(TEAM, -1)[:, :length] for part in (*w_chunks[0][:3], after(w_chunks[0][3], far_got[1]))])
        mine = got[0]
        got = flips(got.reshape(2, 2, half, 2, length), 0, 1)
        everyone = got.transpose(1, 2, 0, 3, 4).reshape(4 * TEAM, length)
    else:
        everyone = lax.all_gather(payload, EVERY, axis=0, tiled=False).reshape(-1, length)
        mine = lax.all_gather(payload, NEAR, axis=0, tiled=False).reshape(TEAM, length)
    tables = mine[members, piece:].astype(f32).astype(jnp.int32)
    first_table, live_table = tables[:, :BLK_DEV], tables[:, BLK_DEV:]
    vec_full = everyone[:, :piece].astype(f32).reshape(VEC)
    b_query, b_value, b_att, b_in, b_mlp, *norm_vectors = split_vectors(vec_full)
    gain_one, shift_one, gain_two, shift_two = (local_order(v)[None] for v in norm_vectors)
    slot = jnp.arange(slot_total, dtype=jnp.int32)
    position = slot[None, :] - BLOCK * jnp.repeat(first_table, BLOCK, axis=1)
    rotary = rotary_rows(position.reshape(team_slots).astype(f32))
    bias_q = lax.dynamic_slice(b_query, (me * HEAD,), (HEAD,))
    bias_v = lax.dynamic_slice(b_value, (me * HEAD,), (HEAD,))
    bias_qkv = jnp.concatenate([bias_q, jnp.zeros_like(bias_q), bias_v])[None]

    def bias_in(begin, end):
        return lax.dynamic_slice(b_in, (TEAM * begin + me * (end - begin),), (end - begin,))[None]

    attn_in, mlp_in, hat = norm_inputs(members, team, gain_one, shift_one, gain_two, shift_two)

    lefts_out, lefts_back, places_out, places_back, sums, terms = [], [], [], [], [], []

    def run_chunk(index, *waits):
        chunk = CHUNKS[index]
        ready = after(attn_in if chunk is None else mlp_in, *waits) if waits else (attn_in if chunk is None else mlp_in)
        if chunk is None:
            left_out, left_back, keep, send, total = attn_chunk(
                members, first_table, live_table, team, ready, w_chunks[index], bias_qkv, rotary, rows_dev
            )
            places_out.append((3 * HEAD, 4 * HEAD))
            places_back.append((0, 3 * HEAD))
        else:
            begin, end = chunk
            left_out, left_back, keep, send, total = mlp_chunk(
                members, team, ready, w_chunks[index], bias_in(begin, end), rows_dev
            )
            places_out.append((end - begin, 2 * (end - begin)))
            places_back.append((0, end - begin))
        lefts_out.append(left_out)
        lefts_back.append(left_back)
        sums.append(total[0])
        terms.append((keep, lax.ppermute(send, "col", SWAP) if paired else send))
        return total

    grouped, owned = [None] * count, [None] * count

    def sum_columns(index, *tokens):
        keep, got = terms[index]
        if not paired:
            term = jnp.concatenate([keep, got], axis=0)
            owned[index] = lax.psum_scatter(term, CROSS, scatter_dimension=0, tiled=True)
            return tokens[0]
        kept, sent = split_sum(after(keep, *tokens), got, 2)
        grouped[index] = (kept, lax.ppermute(sent, "far", SWAP))
        return kept

    def sum_far(index, *tokens, cost=2.5):
        if not paired:
            return tokens[0]
        kept, got = grouped[index]
        owned[index] = last_sum(after(kept, *tokens), got, 2, cost)
        return owned[index]

    def to_rows(index):
        term = owned[index]
        return lax.all_to_all(term.reshape(TEAM, rows_dev, term.shape[1]), NEAR, 0, 0, tiled=True)

    held = {}

    def update(index, got, *tokens):
        chunk = CHUNKS[index]
        got = after(got, *tokens)
        if chunk is None:
            held["qkv"] = adamw_columns(got, w_qkv, first_qkv, second_qkv, 0, HEAD, 0, 3, FENCE)
            held["att"] = adamw_columns(got, w_attn_out, first_attn_out, second_attn_out, 3, HEAD, 0, 1, 3)
            return held["att"][0]
        begin, end = chunk
        unit = end - begin
        for kind, name, arrays in ((0, "in", (w_mlp_in, first_mlp_in, second_mlp_in)), (1, "out", (w_mlp_out, first_mlp_out, second_mlp_out))):
            held[name] = adamw_columns(got, *arrays, kind, unit, begin // unit, 1, 4, held.get(name))
        return held["out"][0]

    token = run_chunk(0)
    cross(2, token)
    if paired:
        send_far(3, token)
    token = run_chunk(1, token, *far_got[2:3] if paired else ())
    cross(3, token)
    token = sum_columns(0, token)
    token = run_chunk(2, token, *far_got[3:4] if paired else ())
    token = sum_far(0, token)
    rows_zero = to_rows(0)
    token = run_chunk(3, token)
    token = sum_columns(1, token)
    attn_index = CHUNKS.index(None)
    lefts_back[0] = after(lefts_back[0], token, rows_zero)
    back_send, back_keep, norm_sums = back_part(
        hat, lefts_back, w_chunks, places_back, attn_index, gain_one, gain_two, rows_dev
    )
    lefts_out[0] = after(lefts_out[0], back_keep)
    out_send, out_keep = out_part(lefts_out, w_chunks, places_out, rows_dev)

    def own_step(pair, axis, steps, *tokens):
        kept, sent = pair
        return split_sum(after(kept, *tokens), lax.ppermute(sent, axis, SWAP), steps)

    alive = (jnp.arange(BLOCK, dtype=jnp.int32)[None, :] < block_live[:, None]).reshape(slot_total)
    seed_own = jnp.where(alive[:, None], cotangent, jnp.zeros_like(cotangent))
    seed_sum = jnp.sum(seed_own.astype(f32), axis=0)

    def place(values, width):
        return lax.dynamic_update_slice(jnp.zeros((width,), f32), values, (me * values.shape[0],))

    mlp_order = sorted((k for k in range(count) if CHUNKS[k] is not None), key=lambda k: CHUNKS[k][0])
    local_vec = jnp.concatenate(
        [
            place(sums[attn_index][:HEAD], D),
            place(sums[attn_index][2 * HEAD :], D),
            seed_sum,
            *[place(sums[k], TEAM * sums[k].shape[0]) for k in mlp_order],
            seed_sum,
            own_order(norm_sums[:4]).reshape(4 * D),
        ]
    )
    vec_terms = local_vec.reshape(far_size, half, 2, 2, piece).transpose(1, 3, 0, 2, 4).reshape(TEAM, groups, piece)
    vec_team = jnp.sum(lax.all_to_all(vec_terms, NEAR, 0, 0, tiled=True), axis=0)
    if paired:
        pick = lambda f, c: lax.dynamic_index_in_dim(vec_team, 2 * (far ^ f) + (column ^ c), 0, keepdims=False)
        grad_vectors = pick(0, 0) + lax.ppermute(pick(0, 1), "col", SWAP) + lax.ppermute(pick(1, 0), "far", SWAP)
        grad_vectors = grad_vectors + lax.ppermute(pick(1, 1), ("far", "col"), [(i, 3 - i) for i in range(4)])
    else:
        grad_vectors = jnp.sum(lax.all_to_all(vec_team, ("far", "col"), 0, 0, tiled=True), axis=0)
    new_vec, m_vec, u_vec = adamw_update(vectors, grad_vectors, first_vectors, second_vectors, vector_rate, 0.0)

    token = sum_columns(2, out_keep)
    token = sum_far(1, token, vec_team, cost=FENCE)
    rows_one = to_rows(1)
    back_pair = own_step((back_keep, back_send), "core", 4, token)
    out_pair = own_step((out_keep, out_send), "core", 4, back_pair[0])
    token = sum_columns(3, out_pair[0])
    token = update(0, rows_zero, token)
    token = update(1, rows_one, token)
    token = sum_far(2, token)
    rows_two = to_rows(2)
    back_pair = own_step(back_pair, "row", 2, token)
    out_pair = own_step(out_pair, "low", 2, back_pair[0])
    token = sum_far(3, out_pair[0])
    rows_three = to_rows(3)
    token = update(2, rows_two, token)
    ordered = (lambda v: v) if paired else own_order
    back_got = lax.ppermute(back_pair[1], "low", SWAP)
    out_got = lax.ppermute(out_pair[1], "row", SWAP)
    grad_tokens = finish_tokens(to_own, after(tokens, token), seed_own, ordered(back_pair[0]), ordered(back_got), True)
    bias_out = (b_att + b_mlp)[None]
    out = finish_tokens(
        to_own, after(tokens, grad_tokens), bias_out, ordered(out_pair[0]), ordered(out_got), False
    )
    update(3, rows_three, out)
    grad_qkv, new_qkv, m_qkv, u_qkv = held["qkv"]
    grad_attn_out, new_att, m_att, u_att = held["att"]
    grad_mlp_in, new_in, m_in, u_in = held["in"]
    grad_mlp_out, new_out, m_out, u_out = held["out"]
    return (
        out,
        grad_tokens,
        grad_qkv,
        grad_attn_out,
        grad_mlp_in,
        grad_mlp_out,
        grad_vectors,
        new_qkv,
        new_att,
        new_in,
        new_out,
        new_vec,
        m_qkv,
        u_qkv,
        m_att,
        u_att,
        m_in,
        u_in,
        m_out,
        u_out,
        m_vec,
        u_vec,
    )


def solution(mesh):
    devices = mesh.devices.reshape(-1)
    layout = Mesh(devices.reshape(devices.size // 16, 2, 2, 2, 2), EVERY)
    matrix, line = P(EVERY, None), P(EVERY)
    in_specs = (matrix, matrix, line, line) + (matrix,) * 4 + (line,) + (matrix,) * 8 + (line,) * 2
    out_specs = (matrix,) * 6 + (line,) + (matrix,) * 4 + (line,) + (matrix,) * 8 + (line,) * 2
    return jax.shard_map(body, mesh=layout, in_specs=in_specs, out_specs=out_specs, check_vma=False)
```

```python
import jax
import jax.numpy as jnp
from jax import lax
from jax.experimental import pallas as pl
from jax.experimental.pallas import tpu as pltpu
from jax.sharding import Mesh, PartitionSpec as P

D = 2048
HEADS = 8
HEAD = 256
FF = 8192
ROT = 64
BLOCK = 128
BLK_DEV = 2
STEP = 3
VEC = 24576
TEAM = 8
SLICE_FF = FF // TEAM
CHUNKS = ((0, 256), None, (512, 1024), (256, 512))
LOADS = ((0,), (1,), (2, 3))
PACK_ROWS = 16
LANES = 128

eps_norm = 1e-05
beta_one = 0.9
beta_two = 0.95
learn_rate = 0.03
vector_rate = 0.3
decay_matrix = 0.1
eps_adam = 1e-08
masked_score = -1e30
plain = (((1,), (0,)), ((), ()))
contract_rows = (((0,), (0,)), ((), ()))
contract_cols = (((1,), (1,)), ((), ()))
bf16 = jnp.bfloat16
f32 = jnp.float32
VMEM_BYTES = 56 * 1024 * 1024
NEAR = ("low", "row", "core")
CROSS = ("col", "far")
EVERY = ("far", "low", "row", "col", "core")
SWAP = [(0, 1), (1, 0)]
COST = {
    'norm': 100,
    'mlp1024': 20000,
    'attn': 300,
    'back': 10,
    'far0': 20000,
    'adam1': 90,
    'adam0in': 40,
    'adam0out': 10,
    'adam1b': 40,
    'out': 190,
    'mlp512': 150,
    'rows': 20000,
    'back_row': 300,
    'prep': 300,
    'far2': 30,
    'col1': 100,
    'fin': 30,
    'col0': 10,
    'back_core': 10,
}
ORDER = (
    'K0',
    'K1',
    'C0',
    'K2',
    'K3',
    'C1',
    'O',
    'B',
    'C3',
    'F0',
    'O1',
    'B1',
    'C2',
    'F2',
    'B2',
    'A1',
    'A0',
    'O2',
    'A2',
    'A3',
    'O3',
    'B3',
)
ANYWHERE = pl.BlockSpec(memory_space=pl.ANY)


def dot(left, right, dims=plain):
    return lax.dot_general(left, right, dims, preferred_element_type=f32)


def after(value, *others):
    return lax.optimization_barrier((value, *others))[0]


def params(role):
    return dict(
        compiler_params=pltpu.CompilerParams(vmem_limit_bytes=VMEM_BYTES),
        cost_estimate=pl.CostEstimate(flops=int(COST.get(role, 1) * 1e8), bytes_accessed=1024, transcendentals=0),
    )


def shaped(shape, dtype):
    return jax.ShapeDtypeStruct(shape, dtype)


def blocks(shape, index):
    return pl.BlockSpec(shape, index)


def split_vectors(vec_all):
    boundaries = [D, 2 * D, 3 * D, 3 * D + FF, 4 * D + FF, 5 * D + FF, 6 * D + FF, 7 * D + FF]
    return jnp.split(vec_all, boundaries)


def adamw_update(weight, grad, first_m, second_m, rate_value, decay_value):
    first_new = beta_one * first_m + (1.0 - beta_one) * grad
    second_new = beta_two * second_m + (1.0 - beta_two) * grad * grad
    fix_one = 1.0 - beta_one**STEP
    fix_two = 1.0 - beta_two**STEP
    direction = first_new / fix_one / (jnp.sqrt(second_new / fix_two) + eps_adam)
    return (weight - rate_value * (direction + decay_value * weight), first_new, second_new)


def normalize(values):
    centred = values - jnp.mean(values, axis=-1, keepdims=True)
    spread = jnp.mean(centred * centred, axis=-1, keepdims=True)
    scale = lax.rsqrt(spread + eps_norm)
    return centred * scale, scale


def rotary_rows(position):
    lane = jnp.arange(LANES)
    frequency = 10000.0 ** (-(2.0 * (lane % (ROT // 2)).astype(f32)) / ROT)
    angles = position[:, None] * frequency[None, :]
    sine = jnp.sin(angles)
    cosine = jnp.where(lane < ROT, jnp.cos(angles), 1.0)
    return (
        cosine,
        jnp.where(lane < ROT // 2, -sine, 0.0),
        jnp.where((lane >= ROT // 2) & (lane < ROT), sine, 0.0),
    )


def gelu_pair(hidden):
    cumulative = 0.5 * (1.0 + lax.erf(hidden * (0.5**0.5)))
    density = jnp.exp(-0.5 * hidden * hidden) * 0.3989422804014327
    return hidden * cumulative, cumulative + hidden * density


def stacked_copies(refs, buffer, sems, rows_dev, columns=None):
    copies, begin = [], 0
    for ref in refs:
        parts = [ref] if len(ref.shape) == 2 else [ref.at[k, 0:rows_dev] for k in range(ref.shape[0])]
        for part in parts:
            rows = part.shape[0]
            source = part if columns is None else part.at[:, columns]
            copies.append(pltpu.make_async_copy(source, buffer.at[begin : begin + rows], sems.at[len(copies)]))
            begin += rows
    return copies


def copy_count(pieces):
    return sum(1 if piece.ndim == 2 else piece.shape[0] for piece in pieces)


def extra_rows(pieces, rows_dev):
    count, (members, rows, width) = len(pieces), pieces[0].shape
    more = rows - rows_dev

    def kernel(*refs):
        for k in range(count):
            refs[-1][k] = refs[k][...]

    return pl.pallas_call(
        kernel,
        grid=(1,),
        in_specs=[blocks((members, more, width), lambda i: (0, rows_dev // more, 0))] * count,
        out_specs=blocks((count, members, more, width), lambda i: (0, 0, 0, 0)),
        out_shape=shaped((count, members, more, width), bf16),
        **params("rows"),
    )(*pieces)


def member_copies(members_ref, team_ref, kind, buffer, sems):
    count, both, _ = team_ref.shape
    rows = both // 2
    return [
        pltpu.make_async_copy(
            team_ref.at[members_ref[k], kind * rows : (kind + 1) * rows],
            buffer.at[k * rows : (k + 1) * rows],
            sems.at[k],
        )
        for k in range(count)
    ]


def prepare_tokens(order, live, tokens, cotangent):
    slots = tokens.shape[0]

    def kernel(order_ref, live_ref, x_ref, y_ref, both_ref):
        row = lax.broadcasted_iota(jnp.int32, (slots, LANES), 0)
        end = jnp.where(row < BLOCK, live_ref[0], live_ref[1] + BLOCK)
        alive = row < end
        for k in range(D // LANES):
            source = pl.ds(pl.multiple_of(order_ref[k] * LANES, LANES), LANES)
            here = slice(k * LANES, (k + 1) * LANES)
            both_ref[:slots, here] = x_ref[:, source]
            both_ref[slots:, here] = jnp.where(alive, y_ref[:, source].astype(f32), 0.0).astype(bf16)

    whole = blocks((slots, D), lambda i, *_: (0, 0))
    return pl.pallas_call(
        kernel,
        grid_spec=pltpu.PrefetchScalarGridSpec(
            num_scalar_prefetch=2,
            grid=(1,),
            in_specs=[whole, whole],
            out_specs=blocks((2 * slots, D), lambda i, *_: (0, 0)),
        ),
        out_shape=shaped((2 * slots, D), bf16),
        **params("prep"),
    )(order, live, tokens, cotangent)


def norm_inputs(members, team, gain_one, shift_one, gain_two, shift_two):
    count, both, _ = team.shape
    rows = both // 2

    def kernel(members_ref, team_ref, g1, s1, g2, s2, one_ref, two_ref, hat_ref, buffer, sems):
        step = pl.program_id(0)
        copies = member_copies(members_ref, team_ref, 0, buffer, sems)

        @pl.when(step == 0)
        def _():
            for copy in copies:
                copy.start()

        for k in range(count):

            @pl.when(step == k)
            def _(k=k):
                copies[k].wait()

        hat, _ = normalize(buffer[pl.ds(pl.multiple_of(step * rows, rows), rows), :].astype(f32))
        hat_ref[...] = hat.astype(bf16)
        one_ref[...] = (hat * g1[...] + s1[...]).astype(bf16)
        two_ref[...] = (hat * g2[...] + s2[...]).astype(bf16)

    line = blocks((1, D), lambda i, *_: (0, 0))
    return pl.pallas_call(
        kernel,
        grid_spec=pltpu.PrefetchScalarGridSpec(
            num_scalar_prefetch=1,
            grid=(count,),
            in_specs=[ANYWHERE] + [line] * 4,
            out_specs=[blocks((rows, D), lambda i, *_: (i, 0))] * 3,
            scratch_shapes=[pltpu.VMEM((count * rows, D), bf16), pltpu.SemaphoreType.DMA((count,))],
        ),
        out_shape=[shaped((count * rows, D), bf16)] * 3,
        **params("norm"),
    )(members, team, gain_one, shift_one, gain_two, shift_two)


def open_chunk(step, rows, rows_dev, members_ref, team_ref, w_refs, begin, y_all, w_all, y_sems, w_sems):
    y_copies = member_copies(members_ref, team_ref, 1, y_all, y_sems)
    w_copies = stacked_copies(w_refs, w_all, w_sems, rows_dev, slice(begin, begin + w_all.shape[1]))
    slots = team_ref.shape[1] // 2

    @pl.when(step == 0)
    def _():
        for copy in w_copies + y_copies:
            copy.start()
        for copy in w_copies:
            copy.wait()

    for k, copy in enumerate(y_copies):

        @pl.when(step == k * slots // rows)
        def _(copy=copy):
            copy.wait()

    return y_all[pl.ds(pl.multiple_of(step * rows, rows), rows), :]


def close_chunk(step, last, acc_ref, keep_ref, send_ref, sum_ref, cols, first_term, second_term, column_sum):
    @pl.when(step == 0)
    def _():
        acc_ref[:, :cols] = first_term
        acc_ref[:, cols:] = second_term
        sum_ref[...] = column_sum

    @pl.when((step > 0) & (step < last))
    def _():
        acc_ref[:, :cols] += first_term
        acc_ref[:, cols:] += second_term
        sum_ref[...] += column_sum

    @pl.when(step == last)
    def _():
        half = D // 2
        keep_ref[:, :cols] = (acc_ref[:half, :cols] + first_term[:half]).astype(bf16)
        keep_ref[:, cols:] = (acc_ref[:half, cols:] + second_term[:half]).astype(bf16)
        send_ref[:, :cols] = (acc_ref[half:, :cols] + first_term[half:]).astype(bf16)
        send_ref[:, cols:] = (acc_ref[half:, cols:] + second_term[half:]).astype(bf16)
        sum_ref[...] += column_sum


def chunk_scratch(total, width, y_count, w_count):
    return [
        pltpu.VMEM((D, width), f32),
        pltpu.VMEM((total, D), bf16),
        pltpu.VMEM((D, width), bf16),
        pltpu.SemaphoreType.DMA((y_count,)),
        pltpu.SemaphoreType.DMA((w_count,)),
    ]


def mlp_chunk(members, team, a, w_pieces, begin, b, rows_dev, rows=512):
    total, cols = a.shape[0], b.shape[1]
    width = 2 * cols
    nw = len(w_pieces)

    def kernel(members_ref, team_ref, *refs):
        w_refs = refs[:nw]
        a_ref, b_ref, act_ref, dh_ref, keep_ref, send_ref, sum_ref, acc_ref, y_all, w_all, y_sems, w_sems = refs[nw:]
        step, last = pl.program_id(0), pl.num_programs(0) - 1
        y = open_chunk(step, rows, rows_dev, members_ref, team_ref, w_refs, begin, y_all, w_all, y_sems, w_sems)
        a = a_ref[...]
        act, slope = gelu_pair(dot(a, w_all[:, :cols]) + b_ref[...])
        act = act.astype(bf16)
        dh = (dot(y, w_all[:, cols:]) * slope).astype(bf16)
        act_ref[...] = act
        dh_ref[...] = dh
        column_sum = jnp.sum(dh.astype(f32), axis=0, keepdims=True)
        first_term, second_term = dot(a, dh, contract_rows), dot(y, act, contract_rows)
        close_chunk(step, last, acc_ref, keep_ref, send_ref, sum_ref, cols, first_term, second_term, column_sum)

    fixed = lambda r, c: blocks((r, c), lambda i, *_: (0, 0))
    moving = lambda c: blocks((rows, c), lambda i, *_: (i, 0))
    return pl.pallas_call(
        kernel,
        grid_spec=pltpu.PrefetchScalarGridSpec(
            num_scalar_prefetch=1,
            grid=(total // rows,),
            in_specs=[ANYWHERE] * (1 + nw) + [moving(D), fixed(1, cols)],
            out_specs=[moving(cols), moving(cols), fixed(D // 2, width), fixed(D // 2, width), fixed(1, cols)],
            scratch_shapes=chunk_scratch(total, width, team.shape[0], copy_count(w_pieces)),
        ),
        out_shape=[shaped((total, cols), bf16)] * 2 + [shaped((D // 2, width), bf16)] * 2 + [shaped((1, cols), f32)],
        **params(f"mlp{width}"),
    )(members, team, *w_pieces, a, b)


def turn_lanes(values, cosine, low_sine, high_sine):
    part = values[:, :LANES]
    part = part * cosine + pltpu.roll(part, LANES - ROT // 2, 1) * low_sine + pltpu.roll(part, ROT // 2, 1) * high_sine
    return jnp.concatenate([part, values[:, LANES:]], axis=1)


def attn_chunk(members, first, live, team, a, w_pieces, begin, b, rotary, rows_dev, rows=512):
    total, width = a.shape[0], 4 * HEAD
    nw = len(w_pieces)
    slots = BLK_DEV * BLOCK
    buffers = rows // slots

    def kernel(members_ref, first_ref, live_ref, team_ref, *refs):
        w_refs = refs[:nw]
        a_ref, b_ref, cos_ref, low_ref, high_ref, att_ref, dm_ref, keep_ref, send_ref, sum_ref = refs[nw : nw + 10]
        acc_ref, y_all, w_all, y_sems, w_sems = refs[nw + 10 :]
        step, last = pl.program_id(0), pl.num_programs(0) - 1
        y = open_chunk(step, rows, rows_dev, members_ref, team_ref, w_refs, begin, y_all, w_all, y_sems, w_sems)
        a = a_ref[...]
        mixed = dot(a, w_all[:, : 3 * HEAD]) + b_ref[...]
        datt_all = dot(y, w_all[:, 3 * HEAD :]).astype(bf16)
        row = lax.broadcasted_iota(jnp.int32, (slots, slots), 0)
        col = lax.broadcasted_iota(jnp.int32, (slots, slots), 1)
        for k in range(buffers):
            buf = step * buffers + k
            part = slice(k * slots, (k + 1) * slots)
            apart = first_ref[buf, 1] == 1
            tables = []
            for ref in (cos_ref, low_ref, high_ref):
                start = ref[:BLOCK]
                tables.append(jnp.concatenate([start, jnp.where(apart, start, ref[BLOCK:])], axis=0))
            cosine, low_sine, high_sine = tables
            queries = turn_lanes(mixed[part, :HEAD], cosine, low_sine, high_sine).astype(bf16)
            keys = turn_lanes(mixed[part, HEAD : 2 * HEAD], cosine, low_sine, high_sine).astype(bf16)
            values = mixed[part, 2 * HEAD :].astype(bf16)
            datt = datt_all[part]
            parted = jnp.where(first_ref[buf, 0] == first_ref[buf, 1], 0, 1)
            live_end = jnp.where(col < BLOCK, live_ref[buf, 0], live_ref[buf, 1] + BLOCK)
            other = jnp.where((row >= BLOCK) & (col < BLOCK), parted, 0)
            allowed = (col <= row) & (other == 0) & ((col < live_end) | (col == row))
            scores = jnp.where(allowed, dot(queries, keys, contract_cols) * HEAD ** (-0.5), masked_score)
            raised = jnp.exp(scores - jnp.max(scores, axis=1, keepdims=True))
            probs = raised / jnp.sum(raised, axis=1, keepdims=True)
            probs_low = probs.astype(bf16)
            att_ref[part] = dot(probs_low, values).astype(bf16)
            d_probs = dot(datt, values, contract_cols)
            d_scores = (probs * (d_probs - jnp.sum(probs * d_probs, axis=1, keepdims=True))).astype(bf16)
            d_queries = dot(d_scores, keys) * HEAD ** (-0.5)
            d_keys = dot(d_scores, queries, contract_rows) * HEAD ** (-0.5)
            dm_ref[part, :HEAD] = turn_lanes(d_queries, cosine, -low_sine, -high_sine).astype(bf16)
            dm_ref[part, HEAD : 2 * HEAD] = turn_lanes(d_keys, cosine, -low_sine, -high_sine).astype(bf16)
            dm_ref[part, 2 * HEAD :] = dot(probs_low, datt, contract_rows).astype(bf16)
        d_mixed = dm_ref[...]
        column_sum = jnp.sum(d_mixed.astype(f32), axis=0, keepdims=True)
        first_term, second_term = dot(a, d_mixed, contract_rows), dot(y, att_ref[...], contract_rows)
        close_chunk(step, last, acc_ref, keep_ref, send_ref, sum_ref, 3 * HEAD, first_term, second_term, column_sum)

    fixed = lambda r, c: blocks((r, c), lambda i, *_: (0, 0))
    moving = lambda c: blocks((rows, c), lambda i, *_: (i, 0))
    return pl.pallas_call(
        kernel,
        grid_spec=pltpu.PrefetchScalarGridSpec(
            num_scalar_prefetch=3,
            grid=(total // rows,),
            in_specs=[ANYWHERE] * (1 + nw) + [moving(D), fixed(1, 3 * HEAD)] + [fixed(slots, LANES)] * 3,
            out_specs=[moving(HEAD), moving(3 * HEAD), fixed(D // 2, width), fixed(D // 2, width), fixed(1, 3 * HEAD)],
            scratch_shapes=chunk_scratch(total, width, team.shape[0], copy_count(w_pieces)),
        ),
        out_shape=[shaped((total, HEAD), bf16), shaped((total, 3 * HEAD), bf16)]
        + [shaped((D // 2, width), bf16)] * 2
        + [shaped((1, 3 * HEAD), f32)],
        **params("attn"),
    )(members, first, live, team, *w_pieces, a, b, *rotary)


def token_block(i, low_first):
    half = TEAM // 2
    within = i % half
    if low_first:
        within = within % 2 * 2 + within // 2
    return (i // half + 1) % 2 * half + within


def write_half(value, send_ref, keep_ref):
    first_half = pl.program_id(0) < TEAM // 2

    @pl.when(first_half)
    def _():
        send_ref[...] = value

    @pl.when(jnp.logical_not(first_half))
    def _():
        keep_ref[...] = value


def half_outputs(rows, total):
    half = TEAM // 2
    specs = [
        blocks((rows, D), lambda i: (jnp.minimum(i, half - 1), 0)),
        blocks((rows, D), lambda i: (jnp.maximum(i - half, 0), 0)),
    ]
    return specs, [shaped((total // 2, D), bf16)] * 2


def fetch_columns(groups, buffers, sems, places, rows_dev):
    copies = []
    for k, refs in enumerate(groups):
        begin, end = places[k]
        copies += stacked_copies(refs, buffers[k], sems[k], rows_dev, slice(begin, end))

    @pl.when(pl.program_id(0) == 0)
    def _():
        for copy in copies:
            copy.start()
        for copy in copies:
            copy.wait()


def out_part(lefts, weights, places, rows_dev):
    count, per, total = len(lefts), len(weights[0]), lefts[0].shape[0]
    rows = total // TEAM

    def kernel(*refs):
        groups = [refs[k * per : (k + 1) * per] for k in range(count)]
        left_refs = refs[count * per : count * per + count]
        send_ref, keep_ref, *scratch = refs[count * per + count :]
        fetch_columns(groups, scratch[:count], scratch[count:], places, rows_dev)
        buffers = scratch[:count]
        value = None
        for k in range(count):
            term = dot(left_refs[k][...], buffers[k][...], contract_cols)
            value = term if value is None else value + term
        write_half(value.astype(bf16), send_ref, keep_ref)

    specs, shapes = half_outputs(rows, total)
    return pl.pallas_call(
        kernel,
        grid=(TEAM,),
        in_specs=[ANYWHERE] * (count * per) + [blocks((rows, v.shape[1]), lambda i: (token_block(i, True), 0)) for v in lefts],
        out_specs=specs,
        out_shape=shapes,
        scratch_shapes=[pltpu.VMEM((D, e - b), bf16) for b, e in places]
        + [pltpu.SemaphoreType.DMA((copy_count(group),)) for group in weights],
        **params("out"),
    )(*[piece for group in weights for piece in group], *lefts)


def back_part(hat, lefts, weights, places, attn_index, gain_one, gain_two, rows_dev):
    count, per, total = len(lefts), len(weights[0]), hat.shape[0]
    rows = total // TEAM

    def kernel(*refs):
        groups = [refs[k * per : (k + 1) * per] for k in range(count)]
        left_refs = refs[count * per : count * per + count]
        hat_ref, one_ref, two_ref, send_ref, keep_ref, sums_ref, *scratch = refs[count * per + count :]
        fetch_columns(groups, scratch[:count], scratch[count:], places, rows_dev)
        buffers = scratch[:count]
        d_one, d_two = None, None
        for k in range(count):
            term = dot(left_refs[k][...], buffers[k][...], contract_cols)
            if k == attn_index:
                d_one = term
            else:
                d_two = term if d_two is None else d_two + term
        write_half((d_one * one_ref[...] + d_two * two_ref[...]).astype(bf16), send_ref, keep_ref)
        hat_now = hat_ref[...].astype(f32)
        sums = [jnp.sum(v, axis=0, keepdims=True) for v in (d_one * hat_now, d_one, d_two * hat_now, d_two)]

        @pl.when(pl.program_id(0) == 0)
        def _():
            for k in range(4):
                sums_ref[k : k + 1] = sums[k]

        @pl.when(pl.program_id(0) > 0)
        def _():
            for k in range(4):
                sums_ref[k : k + 1] += sums[k]

    moving = lambda c: blocks((rows, c), lambda i: (token_block(i, False), 0))
    fixed = lambda r, c: blocks((r, c), lambda i: (0, 0))
    specs, shapes = half_outputs(rows, total)
    return pl.pallas_call(
        kernel,
        grid=(TEAM,),
        in_specs=[ANYWHERE] * (count * per)
        + [moving(v.shape[1]) for v in lefts]
        + [moving(D), fixed(1, D), fixed(1, D)],
        out_specs=specs + [fixed(8, D)],
        out_shape=shapes + [shaped((8, D), f32)],
        scratch_shapes=[pltpu.VMEM((D, e - b), bf16) for b, e in places]
        + [pltpu.SemaphoreType.DMA((copy_count(group),)) for group in weights],
        **params("back"),
    )(*[piece for group in weights for piece in group], *lefts, hat, gain_one, gain_two)


def split_sum(left, right, steps, role):
    rows, width = left.shape
    block = rows // 2 // steps

    def kernel(l_low, l_high, r_low, r_high, keep_ref, send_ref):
        keep_ref[...] = l_low[...].astype(f32) + r_low[...].astype(f32)
        send_ref[...] = (l_high[...].astype(f32) + r_high[...].astype(f32)).astype(bf16)

    low = blocks((block, width), lambda i: (i, 0))
    high = blocks((block, width), lambda i: (i + steps, 0))
    return pl.pallas_call(
        kernel,
        grid=(steps,),
        in_specs=[low, high, low, high],
        out_specs=[low, low],
        out_shape=[shaped((rows // 2, width), f32), shaped((rows // 2, width), bf16)],
        **params(role),
    )(left, left, right, right)


def last_sum(kept, got, role):
    count, steps = len(kept), 2
    rows = kept[0].shape[0]
    widths = [v.shape[1] for v in kept]

    def kernel(*refs):
        begin = 0
        for k in range(count):
            here = slice(begin, begin + widths[k])
            refs[-1][:, here] = (refs[k][...] + refs[count + k][...].astype(f32)).astype(bf16)
            begin += widths[k]

    spec = lambda width: blocks((rows // steps, width), lambda i: (i, 0))
    return pl.pallas_call(
        kernel,
        grid=(steps,),
        in_specs=[spec(w) for w in widths] * 2,
        out_specs=spec(sum(widths)),
        out_shape=shaped((rows, sum(widths)), bf16),
        **params(role),
    )(*kept, *got)


def last_sum_members(kept, got, extra, role):
    count = len(kept)
    members, more, width = extra.shape
    rows = kept[0].shape[0] // members
    widths = [v.shape[1] for v in kept]

    def kernel(*refs):
        begin = 0
        for k in range(count):
            here = slice(begin, begin + widths[k])
            refs[-1][0, :rows, here] = (refs[k][...] + refs[count + k][...].astype(f32)).astype(bf16)
            begin += widths[k]
        refs[-1][0, rows:, :] = refs[-2][0]

    spec = lambda w: blocks((rows, w), lambda i: (i, 0))
    return pl.pallas_call(
        kernel,
        grid=(members,),
        in_specs=[spec(w) for w in widths] * 2 + [blocks((1, more, width), lambda i: (i, 0, 0))],
        out_specs=blocks((1, rows + more, width), lambda i: (i, 0, 0)),
        out_shape=shaped((members, rows + more, width), bf16),
        **params(role),
    )(*kept, *got, extra)


def finish_tokens(order, tokens, other, kept, got, back):
    slots = tokens.shape[0]
    steps = 2
    rows = slots // steps

    def kernel(order_ref, x_ref, other_ref, kept_ref, got_ref, out_ref, sum_ref):
        for k in range(D // LANES):
            source = pl.ds(pl.multiple_of(order_ref[k] * LANES, LANES), LANES)
            sum_ref[:, k * LANES : (k + 1) * LANES] = kept_ref[:, source] + got_ref[:, source].astype(f32)
        total = sum_ref[...]
        x = x_ref[...].astype(f32)
        if back:
            hat, scale = normalize(x)
            inner = jnp.mean(total * hat, axis=-1, keepdims=True)
            total = scale * (total - jnp.mean(total, axis=-1, keepdims=True) - hat * inner)
            x = other_ref[...].astype(f32)
        else:
            total = total + other_ref[...]
        out_ref[...] = (x + total).astype(bf16)

    moving = blocks((rows, D), lambda i, *_: (i, 0))
    return pl.pallas_call(
        kernel,
        grid_spec=pltpu.PrefetchScalarGridSpec(
            num_scalar_prefetch=1,
            grid=(steps,),
            in_specs=[moving, moving if back else blocks((1, D), lambda i, *_: (0, 0)), moving, moving],
            out_specs=moving,
            scratch_shapes=[pltpu.VMEM((rows, D), f32)],
        ),
        out_shape=shaped((slots, D), bf16),
        **params("fin"),
    )(order, tokens, other, kept, got)


def adamw_columns(got, weight, first_m, second_m, section, unit, offset, sections, role, held=None):
    rows, width = weight.shape
    span = TEAM * unit
    part = max(rows // 4, 16) if rows % 16 == 0 else rows
    got_spec = blocks((TEAM, part, unit), lambda k, i: (0, i, section + k))
    full = blocks((part, span), lambda k, i: (i, offset + k))

    def kernel(g_ref, w_ref, m_ref, u_ref, *refs):
        grad_ref, new_ref, mo_ref, uo_ref = refs[-4:]
        for k in range(TEAM):
            here = slice(k * unit, (k + 1) * unit)
            grad = g_ref[k].astype(f32)
            new, m_new, u_new = adamw_update(
                w_ref[:, here], grad, m_ref[:, here], u_ref[:, here], learn_rate, decay_matrix
            )
            grad_ref[:, here] = grad
            new_ref[:, here] = new
            mo_ref[:, here] = m_new
            uo_ref[:, here] = u_new

    extra = list(held) if held is not None else []
    return pl.pallas_call(
        kernel,
        grid=(sections, rows // part),
        in_specs=[got_spec, full, full, full] + [ANYWHERE] * len(extra),
        out_specs=[full] * 4,
        out_shape=[shaped((rows, width), f32)] * 4,
        input_output_aliases={4 + k: k for k in range(len(extra))},
        **params(role),
    )(got, weight, first_m, second_m, *extra)


def body(
    tokens,
    cotangent,
    block_first,
    block_live,
    w_qkv,
    w_attn_out,
    w_mlp_in,
    w_mlp_out,
    vectors,
    first_qkv,
    second_qkv,
    first_attn_out,
    second_attn_out,
    first_mlp_in,
    second_mlp_in,
    first_mlp_out,
    second_mlp_out,
    first_vectors,
    second_vectors,
):
    tokens_in = tokens
    far_size = lax.axis_size("far")
    paired = far_size == 2
    groups = 2 * far_size
    slot_total = tokens.shape[0]
    rows_dev = w_qkv.shape[0]
    rows_team = rows_dev * TEAM
    team_slots = slot_total * TEAM
    piece = vectors.shape[0]
    half = TEAM // 2
    count = len(CHUNKS)
    me = lax.axis_index(NEAR)
    far, column = lax.axis_index("far"), lax.axis_index("col")

    def flips(values, col_axis, far_axis):
        if not paired:
            return values
        values = jnp.where(column == 1, jnp.flip(values, col_axis), values)
        return jnp.where(far == 1, jnp.flip(values, far_axis), values)

    def local_order(values):
        lead = values.shape[:-1]
        k = len(lead)
        parts = values.reshape(*lead, far_size, half, 2, 2 * rows_dev)
        parts = jnp.transpose(parts, (*range(k), k + 2, k, k + 1, k + 3))
        return flips(parts, k, k + 1).reshape(*lead, D)

    def own_order(values):
        lead = values.shape[:-1]
        k = len(lead)
        parts = flips(values.reshape(*lead, 2, far_size, half, 2 * rows_dev), k, k + 1)
        return jnp.transpose(parts, (*range(k), k + 1, k + 2, k, k + 3)).reshape(*lead, D)

    place_in_row = jnp.arange(D // LANES, dtype=jnp.int32)
    if paired:
        c, f, r = place_in_row // (2 * half), place_in_row // half % 2, place_in_row % half
        to_local = ((f ^ far) * half + r) * 2 + (c ^ column)
        f, r, c = place_in_row // (2 * half), place_in_row // 2 % half, place_in_row % 2
        to_own = ((c ^ column) * 2 + (f ^ far)) * half + r
    else:
        to_local, to_own = place_in_row, place_in_row

    payload = jnp.concatenate([vectors.astype(bf16), block_first.astype(bf16), block_live.astype(bf16)])

    def columns(chunk):
        cut = lambda w, parts: w.astype(bf16).reshape(rows_dev, parts, TEAM, -1)
        if chunk is None:
            query = cut(w_qkv, 3).transpose(2, 0, 1, 3).reshape(TEAM, rows_dev, 3 * HEAD)
            return jnp.concatenate([query, cut(w_attn_out, 1)[:, 0].transpose(1, 0, 2)], axis=2)
        begin, end = chunk
        span = slice(TEAM * begin, TEAM * end)
        return jnp.concatenate([cut(w[:, span], 1)[:, 0].transpose(1, 0, 2) for w in (w_mlp_in, w_mlp_out)], axis=2)

    if paired:
        both_send = prepare_tokens(to_local, block_live, tokens, cotangent)
    else:
        both_send = prepare_tokens(to_local, block_live, local_order(tokens), local_order(cotangent))
    owns, far_got, load_of, begin_of = [], [None] * len(LOADS), {}, {}
    for load, chunks in enumerate(LOADS):
        parts, begin = [], 0
        for index in chunks:
            parts.append(columns(CHUNKS[index]))
            load_of[index], begin_of[index] = load, begin
            begin += parts[-1].shape[2]
        block = jnp.concatenate(parts, axis=2) if len(parts) > 1 else parts[0]
        if load == 0 and paired:
            extra = jnp.pad(payload, (0, PACK_ROWS * begin - payload.shape[0])).reshape(1, PACK_ROWS, begin)
            block = jnp.concatenate([block, jnp.broadcast_to(extra, (TEAM, PACK_ROWS, begin))], axis=1)
        waits = owns[-1:]
        if paired and load == 1:
            far_got[0] = lax.ppermute(owns[0], "far", SWAP)
        got = lax.all_to_all(after(block, *waits) if waits else block, NEAR, 0, 0, tiled=True)
        owns.append(got if got.shape[1] != rows_dev else got.reshape(rows_team, got.shape[2]))

    team = lax.all_gather(both_send, NEAR, axis=0, tiled=False)
    members = jnp.array([4 * l + 2 * r + c for c in range(2) for r in range(2) for l in range(2)], jnp.int32) ^ me

    loads = []

    def send_far(load, *waits):
        far_got[load] = lax.ppermute(after(owns[load], *waits) if waits else owns[load], "far", SWAP)

    def cross(load, *waits):
        if paired:
            loads[load][1] = far_got[load]
            over = after(far_got[load], *waits) if waits else far_got[load]
            loads[load][3] = lax.ppermute(over, "col", SWAP)

    if paired:
        for own in owns:
            loads.append([own, None, lax.ppermute(own, "col", SWAP), None])
        send_far(1, far_got[0])
        send_far(2, far_got[1])
    else:
        for own in owns:
            loads.append([lax.all_gather(own, CROSS, axis=0, tiled=True)])
    cross(0)
    cross(1)

    length = piece + 2 * BLK_DEV
    if paired:
        parts = lax.optimization_barrier((*loads[0], owns[2], far_got[1]))[:4]
        got = extra_rows(parts, rows_dev).reshape(4, TEAM, -1)[:, :, :length]
        mine = got[0]
        got = flips(got.reshape(2, 2, half, 2, length), 0, 1)
        everyone = got.transpose(1, 2, 0, 3, 4).reshape(4 * TEAM, length)
    else:
        everyone = lax.all_gather(payload, EVERY, axis=0, tiled=False).reshape(-1, length)
        mine = lax.all_gather(payload, NEAR, axis=0, tiled=False).reshape(TEAM, length)
    tables = mine[members, piece:].astype(f32).astype(jnp.int32)
    first_table, live_table = tables[:, :BLK_DEV], tables[:, BLK_DEV:]
    vec_full = everyone[:, :piece].astype(f32).reshape(VEC)
    b_query, b_value, b_att, b_in, b_mlp, *norm_vectors = split_vectors(vec_full)
    gain_one, shift_one, gain_two, shift_two = (local_order(v)[None] for v in norm_vectors)
    rotary = rotary_rows(jnp.arange(slot_total, dtype=jnp.int32).astype(f32))
    bias_q = lax.dynamic_slice(b_query, (me * HEAD,), (HEAD,))
    bias_v = lax.dynamic_slice(b_value, (me * HEAD,), (HEAD,))
    bias_qkv = jnp.concatenate([bias_q, jnp.zeros_like(bias_q), bias_v])[None]

    def bias_in(begin, end):
        return lax.dynamic_slice(b_in, (TEAM * begin + me * (end - begin),), (end - begin,))[None]

    attn_in, mlp_in, hat = norm_inputs(members, team, gain_one, shift_one, gain_two, shift_two)

    lefts_out, lefts_back, places_out, places_back, sums, terms = [], [], [], [], [], []

    def run_chunk(index, *waits):
        chunk = CHUNKS[index]
        pieces, offset = loads[load_of[index]], begin_of[index]
        ready = after(attn_in if chunk is None else mlp_in, *waits) if waits else (attn_in if chunk is None else mlp_in)
        if chunk is None:
            left_out, left_back, keep, send, total = attn_chunk(
                members, first_table, live_table, team, ready, pieces, offset, bias_qkv, rotary, rows_dev
            )
            places_out.append((offset + 3 * HEAD, offset + 4 * HEAD))
            places_back.append((offset, offset + 3 * HEAD))
        else:
            begin, end = chunk
            left_out, left_back, keep, send, total = mlp_chunk(
                members, team, ready, pieces, offset, bias_in(begin, end), rows_dev
            )
            places_out.append((offset + end - begin, offset + 2 * (end - begin)))
            places_back.append((offset, offset + end - begin))
        lefts_out.append(left_out)
        lefts_back.append(left_back)
        sums.append(total[0])
        terms.append((keep, lax.ppermute(send, "col", SWAP) if paired else send))
        return total

    grouped, owned = [None] * count, [None] * count

    def sum_columns(index, *tokens):
        keep, got = terms[index]
        if not paired:
            term = jnp.concatenate([keep, got], axis=0)
            owned[index] = lax.psum_scatter(term, CROSS, scatter_dimension=0, tiled=True)
            return tokens[0]
        kept, sent = split_sum(after(keep, *tokens), got, 2, f"col{index}")
        grouped[index] = (kept, lax.ppermute(sent, "far", SWAP))
        return kept

    def sum_far(chunks, *tokens, extra=None):
        if not paired:
            return jnp.concatenate([owned[index] for index in chunks], axis=1)
        kept = [grouped[index][0] for index in chunks]
        kept[0] = after(kept[0], *tokens)
        got = [grouped[index][1] for index in chunks]
        role = f"far{chunks[0]}"
        return last_sum(kept, got, role) if extra is None else last_sum_members(kept, got, extra, role)

    def to_rows(term):
        blocked = term if term.ndim == 3 else term.reshape(TEAM, rows_dev, term.shape[1])
        return lax.all_to_all(blocked, NEAR, 0, 0, tiled=True)

    held = {}

    def update(index, got, start, *tokens):
        chunk = CHUNKS[index]
        got = after(got, *tokens)
        if chunk is None:
            held["qkv"] = adamw_columns(got, w_qkv, first_qkv, second_qkv, start // HEAD, HEAD, 0, 3, "adam1")
            held["att"] = adamw_columns(got, w_attn_out, first_attn_out, second_attn_out, start // HEAD + 3, HEAD, 0, 1, "adam1b")
            return held["qkv"][0], held["att"][0]
        begin, end = chunk
        unit = end - begin
        for kind, name, arrays in ((0, "in", (w_mlp_in, first_mlp_in, second_mlp_in)), (1, "out", (w_mlp_out, first_mlp_out, second_mlp_out))):
            held[name] = adamw_columns(got, *arrays, start // unit + kind, unit, begin // unit, 1, f"adam{index}{name}", held.get(name))
        return held["in"][0], held["out"][0]

    w_of_chunk = [loads[load_of[index]] for index in range(count)]
    attn_index = CHUNKS.index(None)
    have = {}

    def do_chunk(index, *waits):
        done = run_chunk(index, *waits)
        if index == 0:
            cross(2, done)
        return (done,)

    def do_back(*waits):
        lefts = [after(lefts_back[0], *waits), *lefts_back[1:]]
        have["back_send"], have["back_keep"], have["norm_sums"] = back_part(
            hat, lefts, w_of_chunk, places_back, attn_index, gain_one, gain_two, rows_dev
        )
        return (have["back_keep"],)

    def do_out(*waits):
        lefts = [after(lefts_out[0], *waits), *lefts_out[1:]]
        have["out_send"], have["out_keep"] = out_part(lefts, w_of_chunk, places_out, rows_dev)
        return (have["out_keep"],)

    def own_step(pair, axis, steps, role, *waits):
        kept, sent = pair
        return split_sum(after(kept, *waits), lax.ppermute(sent, axis, SWAP), steps, role)

    def do_own(name, stage, *waits):
        if stage == "core":
            pair = own_step((have[f"{name}_keep"], have[f"{name}_send"]), "core", 4, f"{name}_core", *waits)
        else:
            pair = own_step(have[f"{name}_pair"], stage, 2, f"{name}_{stage}", *waits)
        have[f"{name}_pair"] = pair
        return (pair[0],)

    def do_far(chunks, *waits):
        more = {}
        if paired and chunks[0] == 2:
            width = 2 * sum(CHUNKS[index][1] - CHUNKS[index][0] for index in chunks)
            flat = after(vector_terms(), *waits).reshape(TEAM, groups * piece)
            high = flat.astype(bf16)
            split = jnp.concatenate([high, (flat - high.astype(f32)).astype(bf16)], axis=1)
            split = jnp.pad(split, ((0, 0), (0, PACK_ROWS * width - split.shape[1])))
            more = dict(extra=split.reshape(TEAM, PACK_ROWS, width))
        owned_now = sum_far(chunks, *waits, **more)
        have[f"rows{chunks[0]}"] = to_rows(owned_now)
        return (owned_now,)

    def do_finish(name, *waits):
        kept, sent = have[f"{name}_pair"]
        got = lax.ppermute(sent, "low" if name == "back" else "row", SWAP)
        if not paired:
            kept, got = own_order(kept), own_order(got)
        other = seed_own if name == "back" else (b_att + b_mlp)[None]
        have[name] = finish_tokens(to_own, after(tokens_in, *waits), other, kept, got, name == "back")
        return (have[name],)

    alive = (jnp.arange(BLOCK, dtype=jnp.int32)[None, :] < block_live[:, None]).reshape(slot_total)
    seed_own = jnp.where(alive[:, None], cotangent, jnp.zeros_like(cotangent))

    def vector_terms():
        norm_sums = have["norm_sums"]
        seed_sum = jnp.sum(seed_own.astype(f32), axis=0)

        def place(values, width):
            return lax.dynamic_update_slice(jnp.zeros((width,), f32), values, (me * values.shape[0],))

        mlp_order = sorted((k for k in range(count) if CHUNKS[k] is not None), key=lambda k: CHUNKS[k][0])
        local_vec = jnp.concatenate(
            [
                place(sums[attn_index][:HEAD], D),
                place(sums[attn_index][2 * HEAD :], D),
                seed_sum,
                *[place(sums[k], TEAM * sums[k].shape[0]) for k in mlp_order],
                seed_sum,
                own_order(norm_sums[:4]).reshape(4 * D),
            ]
        )
        vec_terms = local_vec.reshape(far_size, half, 2, 2, piece).transpose(1, 3, 0, 2, 4).reshape(TEAM, groups, piece)

        return vec_terms

    actions = {
        "K0": lambda *w: do_chunk(0, *w),
        "K1": lambda *w: do_chunk(1, *w),
        "K2": lambda *w: do_chunk(2, *w),
        "K3": lambda *w: do_chunk(3, *w),
        "C0": lambda *w: (sum_columns(0, *w),),
        "C1": lambda *w: (sum_columns(1, *w),),
        "C2": lambda *w: (sum_columns(2, *w),),
        "C3": lambda *w: (sum_columns(3, *w),),
        "B": do_back,
        "O": do_out,
        "B1": lambda *w: do_own("back", "core", *w),
        "B2": lambda *w: do_own("back", "row", *w),
        "B3": lambda *w: do_finish("back", *w),
        "O1": lambda *w: do_own("out", "core", *w),
        "O2": lambda *w: do_own("out", "low", *w),
        "O3": lambda *w: do_finish("out", *w),
        "F0": lambda *w: do_far((0, 1), *w),
        "F2": lambda *w: do_far((2, 3), *w),
        "A0": lambda *w: update(0, have["rows0"], 0, *w),
        "A1": lambda *w: update(1, have["rows0"], 512, *w),
        "A2": lambda *w: update(2, have["rows2"], 0, *w),
        "A3": lambda *w: update(3, have["rows2"], 1024, *w),
    }
    waits = ()
    for name in ORDER:
        waits = actions[name](*waits)
    out, grad_tokens, rows_high = have["out"], have["back"], have["rows2"]
    if paired:
        vec_got = rows_high[:, rows_dev:].reshape(TEAM, -1)[:, : 2 * groups * piece].astype(f32)
        vec_team = jnp.sum(vec_got.reshape(2 * TEAM, groups, piece), axis=0)
    else:
        vec_team = jnp.sum(lax.all_to_all(vector_terms(), NEAR, 0, 0, tiled=True), axis=0)
    if paired:
        pick = lambda f, c: lax.dynamic_index_in_dim(vec_team, 2 * (far ^ f) + (column ^ c), 0, keepdims=False)
        over_col = lax.ppermute(pick(0, 1), "col", SWAP)
        over_far = lax.ppermute(pick(1, 0), "far", SWAP)
        over_both = lax.ppermute(pick(1, 1), ("far", "col"), [(i, 3 - i) for i in range(4)])
        over_col, over_far, over_both, _ = lax.optimization_barrier((over_col, over_far, over_both, out))
        grad_vectors = pick(0, 0) + over_col + over_far + over_both
    else:
        grad_vectors = jnp.sum(lax.all_to_all(vec_team, ("far", "col"), 0, 0, tiled=True), axis=0)
    new_vec, m_vec, u_vec = adamw_update(vectors, grad_vectors, first_vectors, second_vectors, vector_rate, 0.0)
    grad_qkv, new_qkv, m_qkv, u_qkv = held["qkv"]
    grad_attn_out, new_att, m_att, u_att = held["att"]
    grad_mlp_in, new_in, m_in, u_in = held["in"]
    grad_mlp_out, new_out, m_out, u_out = held["out"]
    return (
        out,
        grad_tokens,
        grad_qkv,
        grad_attn_out,
        grad_mlp_in,
        grad_mlp_out,
        grad_vectors,
        new_qkv,
        new_att,
        new_in,
        new_out,
        new_vec,
        m_qkv,
        u_qkv,
        m_att,
        u_att,
        m_in,
        u_in,
        m_out,
        u_out,
        m_vec,
        u_vec,
    )


def solution(mesh):
    devices = mesh.devices.reshape(-1)
    layout = Mesh(devices.reshape(devices.size // 16, 2, 2, 2, 2), EVERY)
    matrix, line = P(EVERY, None), P(EVERY)
    in_specs = (matrix, matrix, line, line) + (matrix,) * 4 + (line,) + (matrix,) * 8 + (line,) * 2
    out_specs = (matrix,) * 6 + (line,) + (matrix,) * 4 + (line,) + (matrix,) * 8 + (line,) * 2
    return jax.shard_map(body, mesh=layout, in_specs=in_specs, out_specs=out_specs, check_vma=False)
```

```python
import jax
import jax.numpy as jnp
from jax import lax
from jax.experimental import pallas as pl
from jax.experimental.pallas import tpu as pltpu
from jax.sharding import Mesh, PartitionSpec as P

D = 2048
HEADS = 8
HEAD = 256
FF = 8192
ROT = 64
BLOCK = 128
BLK_DEV = 2
STEP = 3
VEC = 24576
TEAM = 8
SLICE_FF = FF // TEAM
CHUNKS = ((0, 256), None, (512, 1024), (256, 512))
LOADS = ((0,), (1,), (2, 3))
PACK_ROWS = 16
LANES = 128

eps_norm = 1e-05
beta_one = 0.9
beta_two = 0.95
learn_rate = 0.03
vector_rate = 0.3
decay_matrix = 0.1
eps_adam = 1e-08
masked_score = -1e30
plain = (((1,), (0,)), ((), ()))
contract_rows = (((0,), (0,)), ((), ()))
contract_cols = (((1,), (1,)), ((), ()))
bf16 = jnp.bfloat16
f32 = jnp.float32
VMEM_BYTES = 56 * 1024 * 1024
NEAR = ("low", "row", "core")
CROSS = ("col", "far")
EVERY = ("far", "low", "row", "col", "core")
SWAP = [(0, 1), (1, 0)]
COST = {
    'norm': 100,
    'mlp1024': 20000,
    'attn': 300,
    'back': 10,
    'far0': 20000,
    'adam1': 90,
    'adam0': 50,
    'adam1b': 40,
    'out': 190,
    'mlp512': 150,
    'rows': 20000,
    'back_row': 300,
    'prep': 300,
    'far2': 30,
    'col1': 100,
    'fin': 30,
    'col0': 10,
    'back_core': 10,
}
ORDER = (
    'K0',
    'K1',
    'C0',
    'K2',
    'K3',
    'C1',
    'O',
    'B',
    'C3',
    'F0',
    'O1',
    'B1',
    'C2',
    'F2',
    'B2',
    'A1',
    'A0',
    'O2',
    'A2',
    'A3',
    'O3',
    'B3',
)
ANYWHERE = pl.BlockSpec(memory_space=pl.ANY)


def dot(left, right, dims=plain):
    return lax.dot_general(left, right, dims, preferred_element_type=f32)


def after(value, *others):
    return lax.optimization_barrier((value, *others))[0]


def params(role):
    return dict(
        compiler_params=pltpu.CompilerParams(vmem_limit_bytes=VMEM_BYTES),
        cost_estimate=pl.CostEstimate(flops=int(COST.get(role, 1) * 1e8), bytes_accessed=1024, transcendentals=0),
    )


def shaped(shape, dtype):
    return jax.ShapeDtypeStruct(shape, dtype)


def blocks(shape, index):
    return pl.BlockSpec(shape, index)


def split_vectors(vec_all):
    boundaries = [D, 2 * D, 3 * D, 3 * D + FF, 4 * D + FF, 5 * D + FF, 6 * D + FF, 7 * D + FF]
    return jnp.split(vec_all, boundaries)


def adamw_update(weight, grad, first_m, second_m, rate_value, decay_value):
    first_new = beta_one * first_m + (1.0 - beta_one) * grad
    second_new = beta_two * second_m + (1.0 - beta_two) * grad * grad
    fix_one = 1.0 - beta_one**STEP
    fix_two = 1.0 - beta_two**STEP
    direction = first_new / fix_one / (jnp.sqrt(second_new / fix_two) + eps_adam)
    return (weight - rate_value * (direction + decay_value * weight), first_new, second_new)


def normalize(values):
    centred = values - jnp.mean(values, axis=-1, keepdims=True)
    spread = jnp.mean(centred * centred, axis=-1, keepdims=True)
    scale = lax.rsqrt(spread + eps_norm)
    return centred * scale, scale


def rotary_rows(position):
    lane = jnp.arange(LANES)
    frequency = 10000.0 ** (-(2.0 * (lane % (ROT // 2)).astype(f32)) / ROT)
    angles = position[:, None] * frequency[None, :]
    sine = jnp.sin(angles)
    cosine = jnp.where(lane < ROT, jnp.cos(angles), 1.0)
    return (
        cosine,
        jnp.where(lane < ROT // 2, -sine, 0.0),
        jnp.where((lane >= ROT // 2) & (lane < ROT), sine, 0.0),
    )


def gelu_pair(hidden):
    cumulative = 0.5 * (1.0 + lax.erf(hidden * (0.5**0.5)))
    density = jnp.exp(-0.5 * hidden * hidden) * 0.3989422804014327
    return hidden * cumulative, cumulative + hidden * density


def stacked_copies(refs, buffer, sems, rows_dev, columns=None):
    copies, begin = [], 0
    for ref in refs:
        parts = [ref] if len(ref.shape) == 2 else [ref.at[k, 0:rows_dev] for k in range(ref.shape[0])]
        for part in parts:
            rows = part.shape[0]
            source = part if columns is None else part.at[:, columns]
            copies.append(pltpu.make_async_copy(source, buffer.at[begin : begin + rows], sems.at[len(copies)]))
            begin += rows
    return copies


def copy_count(pieces):
    return sum(1 if piece.ndim == 2 else piece.shape[0] for piece in pieces)


def extra_rows(pieces, rows_dev):
    count, (members, rows, width) = len(pieces), pieces[0].shape
    more = rows - rows_dev

    def kernel(*refs):
        for k in range(count):
            refs[-1][k] = refs[k][...]

    return pl.pallas_call(
        kernel,
        grid=(1,),
        in_specs=[blocks((members, more, width), lambda i: (0, rows_dev // more, 0))] * count,
        out_specs=blocks((count, members, more, width), lambda i: (0, 0, 0, 0)),
        out_shape=shaped((count, members, more, width), bf16),
        **params("rows"),
    )(*pieces)


def member_copies(members_ref, team_refs, kind, buffer, sems):
    rows = team_refs[0].shape[1] // 2
    copies = []
    for k in range(TEAM):
        source = team_refs[k % 2].at[members_ref[k], kind * rows : (kind + 1) * rows]
        copies.append(pltpu.make_async_copy(source, buffer.at[k * rows : (k + 1) * rows], sems.at[k]))
    return copies


def prepare_tokens(order, live, tokens, cotangent):
    slots = tokens.shape[0]

    def kernel(order_ref, live_ref, x_ref, y_ref, both_ref):
        row = lax.broadcasted_iota(jnp.int32, (slots, LANES), 0)
        end = jnp.where(row < BLOCK, live_ref[0], live_ref[1] + BLOCK)
        alive = row < end
        for k in range(D // LANES):
            source = pl.ds(pl.multiple_of(order_ref[k] * LANES, LANES), LANES)
            here = slice(k * LANES, (k + 1) * LANES)
            both_ref[:slots, here] = x_ref[:, source]
            both_ref[slots:, here] = jnp.where(alive, y_ref[:, source].astype(f32), 0.0).astype(bf16)

    whole = blocks((slots, D), lambda i, *_: (0, 0))
    return pl.pallas_call(
        kernel,
        grid_spec=pltpu.PrefetchScalarGridSpec(
            num_scalar_prefetch=2,
            grid=(1,),
            in_specs=[whole, whole],
            out_specs=blocks((2 * slots, D), lambda i, *_: (0, 0)),
        ),
        out_shape=shaped((2 * slots, D), bf16),
        **params("prep"),
    )(order, live, tokens, cotangent)


def norm_inputs(members, team, gain_one, shift_one, gain_two, shift_two):
    count, rows = TEAM, team[0].shape[1] // 2

    def kernel(members_ref, near_ref, over_ref, g1, s1, g2, s2, one_ref, two_ref, hat_ref, buffer, sems):
        step = pl.program_id(0)
        copies = member_copies(members_ref, (near_ref, over_ref), 0, buffer, sems)

        @pl.when(step == 0)
        def _():
            for copy in copies:
                copy.start()

        for k in range(count):

            @pl.when(step == k)
            def _(k=k):
                copies[k].wait()

        hat, _ = normalize(buffer[pl.ds(pl.multiple_of(step * rows, rows), rows), :].astype(f32))
        hat_ref[...] = hat.astype(bf16)
        one_ref[...] = (hat * g1[...] + s1[...]).astype(bf16)
        two_ref[...] = (hat * g2[...] + s2[...]).astype(bf16)

    line = blocks((1, D), lambda i, *_: (0, 0))
    return pl.pallas_call(
        kernel,
        grid_spec=pltpu.PrefetchScalarGridSpec(
            num_scalar_prefetch=1,
            grid=(count,),
            in_specs=[ANYWHERE] * 2 + [line] * 4,
            out_specs=[blocks((rows, D), lambda i, *_: (i, 0))] * 3,
            scratch_shapes=[pltpu.VMEM((count * rows, D), bf16), pltpu.SemaphoreType.DMA((count,))],
        ),
        out_shape=[shaped((count * rows, D), bf16)] * 3,
        **params("norm"),
    )(members, *team, gain_one, shift_one, gain_two, shift_two)


def open_chunk(step, rows, rows_dev, members_ref, team_refs, w_refs, begin, y_all, w_all, y_sems, w_sems):
    y_copies = member_copies(members_ref, team_refs, 1, y_all, y_sems)
    w_copies = stacked_copies(w_refs, w_all, w_sems, rows_dev, slice(begin, begin + w_all.shape[1]))
    slots = team_refs[0].shape[1] // 2

    @pl.when(step == 0)
    def _():
        for copy in w_copies + y_copies:
            copy.start()
        for copy in w_copies:
            copy.wait()

    for k, copy in enumerate(y_copies):

        @pl.when(step == k * slots // rows)
        def _(copy=copy):
            copy.wait()

    return y_all[pl.ds(pl.multiple_of(step * rows, rows), rows), :]


def close_chunk(step, last, acc_ref, keep_ref, send_ref, sum_ref, cols, first_term, second_term, column_sum):
    @pl.when(step == 0)
    def _():
        acc_ref[:, :cols] = first_term
        acc_ref[:, cols:] = second_term
        sum_ref[...] = column_sum

    @pl.when((step > 0) & (step < last))
    def _():
        acc_ref[:, :cols] += first_term
        acc_ref[:, cols:] += second_term
        sum_ref[...] += column_sum

    @pl.when(step == last)
    def _():
        half = D // 2
        keep_ref[:, :cols] = (acc_ref[:half, :cols] + first_term[:half]).astype(bf16)
        keep_ref[:, cols:] = (acc_ref[:half, cols:] + second_term[:half]).astype(bf16)
        send_ref[:, :cols] = (acc_ref[half:, :cols] + first_term[half:]).astype(bf16)
        send_ref[:, cols:] = (acc_ref[half:, cols:] + second_term[half:]).astype(bf16)
        sum_ref[...] += column_sum


def chunk_scratch(total, width, y_count, w_count):
    return [
        pltpu.VMEM((D, width), f32),
        pltpu.VMEM((total, D), bf16),
        pltpu.VMEM((D, width), bf16),
        pltpu.SemaphoreType.DMA((y_count,)),
        pltpu.SemaphoreType.DMA((w_count,)),
    ]


def mlp_chunk(members, team, a, w_pieces, begin, b, rows_dev, rows=512):
    total, cols = a.shape[0], b.shape[1]
    width = 2 * cols
    nw = len(w_pieces)

    def kernel(members_ref, *refs):
        team_refs, w_refs, refs = refs[:2], refs[2 : 2 + nw], refs[2 + nw :]
        a_ref, b_ref, act_ref, dh_ref, keep_ref, send_ref, sum_ref, acc_ref, y_all, w_all, y_sems, w_sems = refs
        step, last = pl.program_id(0), pl.num_programs(0) - 1
        y = open_chunk(step, rows, rows_dev, members_ref, team_refs, w_refs, begin, y_all, w_all, y_sems, w_sems)
        a = a_ref[...]
        act, slope = gelu_pair(dot(a, w_all[:, :cols]) + b_ref[...])
        act = act.astype(bf16)
        dh = (dot(y, w_all[:, cols:]) * slope).astype(bf16)
        act_ref[...] = act
        dh_ref[...] = dh
        column_sum = jnp.sum(dh.astype(f32), axis=0, keepdims=True)
        first_term, second_term = dot(a, dh, contract_rows), dot(y, act, contract_rows)
        close_chunk(step, last, acc_ref, keep_ref, send_ref, sum_ref, cols, first_term, second_term, column_sum)

    fixed = lambda r, c: blocks((r, c), lambda i, *_: (0, 0))
    moving = lambda c: blocks((rows, c), lambda i, *_: (i, 0))
    return pl.pallas_call(
        kernel,
        grid_spec=pltpu.PrefetchScalarGridSpec(
            num_scalar_prefetch=1,
            grid=(total // rows,),
            in_specs=[ANYWHERE] * (2 + nw) + [moving(D), fixed(1, cols)],
            out_specs=[moving(cols), moving(cols), fixed(D // 2, width), fixed(D // 2, width), fixed(1, cols)],
            scratch_shapes=chunk_scratch(total, width, TEAM, copy_count(w_pieces)),
        ),
        out_shape=[shaped((total, cols), bf16)] * 2 + [shaped((D // 2, width), bf16)] * 2 + [shaped((1, cols), f32)],
        **params(f"mlp{width}"),
    )(members, *team, *w_pieces, a, b)


def turn_lanes(values, cosine, low_sine, high_sine):
    part = values[:, :LANES]
    part = part * cosine + pltpu.roll(part, LANES - ROT // 2, 1) * low_sine + pltpu.roll(part, ROT // 2, 1) * high_sine
    return jnp.concatenate([part, values[:, LANES:]], axis=1)


def attn_chunk(members, first, live, team, a, w_pieces, begin, b, rotary, rows_dev, rows=512):
    total, width = a.shape[0], 4 * HEAD
    nw = len(w_pieces)
    slots = BLK_DEV * BLOCK
    buffers = rows // slots

    def kernel(members_ref, first_ref, live_ref, *refs):
        team_refs, w_refs, refs = refs[:2], refs[2 : 2 + nw], refs[2 + nw :]
        a_ref, b_ref, cos_ref, low_ref, high_ref, att_ref, dm_ref, keep_ref, send_ref, sum_ref = refs[:10]
        acc_ref, y_all, w_all, y_sems, w_sems = refs[10:]
        step, last = pl.program_id(0), pl.num_programs(0) - 1
        y = open_chunk(step, rows, rows_dev, members_ref, team_refs, w_refs, begin, y_all, w_all, y_sems, w_sems)
        a = a_ref[...]
        mixed = dot(a, w_all[:, : 3 * HEAD]) + b_ref[...]
        datt_all = dot(y, w_all[:, 3 * HEAD :]).astype(bf16)
        row = lax.broadcasted_iota(jnp.int32, (slots, slots), 0)
        col = lax.broadcasted_iota(jnp.int32, (slots, slots), 1)
        for k in range(buffers):
            buf = step * buffers + k
            part = slice(k * slots, (k + 1) * slots)
            apart = first_ref[buf, 1] == 1
            tables = []
            for ref in (cos_ref, low_ref, high_ref):
                start = ref[:BLOCK]
                tables.append(jnp.concatenate([start, jnp.where(apart, start, ref[BLOCK:])], axis=0))
            cosine, low_sine, high_sine = tables
            queries = turn_lanes(mixed[part, :HEAD], cosine, low_sine, high_sine).astype(bf16)
            keys = turn_lanes(mixed[part, HEAD : 2 * HEAD], cosine, low_sine, high_sine).astype(bf16)
            values = mixed[part, 2 * HEAD :].astype(bf16)
            datt = datt_all[part]
            parted = jnp.where(first_ref[buf, 0] == first_ref[buf, 1], 0, 1)
            live_end = jnp.where(col < BLOCK, live_ref[buf, 0], live_ref[buf, 1] + BLOCK)
            other = jnp.where((row >= BLOCK) & (col < BLOCK), parted, 0)
            allowed = (col <= row) & (other == 0) & ((col < live_end) | (col == row))
            scores = jnp.where(allowed, dot(queries, keys, contract_cols) * HEAD ** (-0.5), masked_score)
            raised = jnp.exp(scores - jnp.max(scores, axis=1, keepdims=True))
            probs = raised / jnp.sum(raised, axis=1, keepdims=True)
            probs_low = probs.astype(bf16)
            att_ref[part] = dot(probs_low, values).astype(bf16)
            d_probs = dot(datt, values, contract_cols)
            d_scores = (probs * (d_probs - jnp.sum(probs * d_probs, axis=1, keepdims=True))).astype(bf16)
            d_queries = dot(d_scores, keys) * HEAD ** (-0.5)
            d_keys = dot(d_scores, queries, contract_rows) * HEAD ** (-0.5)
            dm_ref[part, :HEAD] = turn_lanes(d_queries, cosine, -low_sine, -high_sine).astype(bf16)
            dm_ref[part, HEAD : 2 * HEAD] = turn_lanes(d_keys, cosine, -low_sine, -high_sine).astype(bf16)
            dm_ref[part, 2 * HEAD :] = dot(probs_low, datt, contract_rows).astype(bf16)
        d_mixed = dm_ref[...]
        column_sum = jnp.sum(d_mixed.astype(f32), axis=0, keepdims=True)
        first_term, second_term = dot(a, d_mixed, contract_rows), dot(y, att_ref[...], contract_rows)
        close_chunk(step, last, acc_ref, keep_ref, send_ref, sum_ref, 3 * HEAD, first_term, second_term, column_sum)

    fixed = lambda r, c: blocks((r, c), lambda i, *_: (0, 0))
    moving = lambda c: blocks((rows, c), lambda i, *_: (i, 0))
    return pl.pallas_call(
        kernel,
        grid_spec=pltpu.PrefetchScalarGridSpec(
            num_scalar_prefetch=3,
            grid=(total // rows,),
            in_specs=[ANYWHERE] * (2 + nw) + [moving(D), fixed(1, 3 * HEAD)] + [fixed(slots, LANES)] * 3,
            out_specs=[moving(HEAD), moving(3 * HEAD), fixed(D // 2, width), fixed(D // 2, width), fixed(1, 3 * HEAD)],
            scratch_shapes=chunk_scratch(total, width, TEAM, copy_count(w_pieces)),
        ),
        out_shape=[shaped((total, HEAD), bf16), shaped((total, 3 * HEAD), bf16)]
        + [shaped((D // 2, width), bf16)] * 2
        + [shaped((1, 3 * HEAD), f32)],
        **params("attn"),
    )(members, first, live, *team, *w_pieces, a, b, *rotary)


def token_block(i, low_first):
    half = TEAM // 2
    within = i % half
    if low_first:
        within = within % 2 * 2 + within // 2
    return (i // half + 1) % 2 * half + within


def write_half(value, send_ref, keep_ref):
    first_half = pl.program_id(0) < TEAM // 2

    @pl.when(first_half)
    def _():
        send_ref[...] = value

    @pl.when(jnp.logical_not(first_half))
    def _():
        keep_ref[...] = value


def half_outputs(rows, total):
    half = TEAM // 2
    specs = [
        blocks((rows, D), lambda i: (jnp.minimum(i, half - 1), 0)),
        blocks((rows, D), lambda i: (jnp.maximum(i - half, 0), 0)),
    ]
    return specs, [shaped((total // 2, D), bf16)] * 2


def fetch_columns(groups, buffers, sems, places, rows_dev):
    copies = []
    for k, refs in enumerate(groups):
        begin, end = places[k]
        copies += stacked_copies(refs, buffers[k], sems[k], rows_dev, slice(begin, end))

    @pl.when(pl.program_id(0) == 0)
    def _():
        for copy in copies:
            copy.start()
        for copy in copies:
            copy.wait()


def out_part(lefts, weights, places, rows_dev):
    count, per, total = len(lefts), len(weights[0]), lefts[0].shape[0]
    rows = total // TEAM

    def kernel(*refs):
        groups = [refs[k * per : (k + 1) * per] for k in range(count)]
        left_refs = refs[count * per : count * per + count]
        send_ref, keep_ref, *scratch = refs[count * per + count :]
        fetch_columns(groups, scratch[:count], scratch[count:], places, rows_dev)
        buffers = scratch[:count]
        value = None
        for k in range(count):
            term = dot(left_refs[k][...], buffers[k][...], contract_cols)
            value = term if value is None else value + term
        write_half(value.astype(bf16), send_ref, keep_ref)

    specs, shapes = half_outputs(rows, total)
    return pl.pallas_call(
        kernel,
        grid=(TEAM,),
        in_specs=[ANYWHERE] * (count * per) + [blocks((rows, v.shape[1]), lambda i: (token_block(i, True), 0)) for v in lefts],
        out_specs=specs,
        out_shape=shapes,
        scratch_shapes=[pltpu.VMEM((D, e - b), bf16) for b, e in places]
        + [pltpu.SemaphoreType.DMA((copy_count(group),)) for group in weights],
        **params("out"),
    )(*[piece for group in weights for piece in group], *lefts)


def back_part(hat, lefts, weights, places, attn_index, gain_one, gain_two, rows_dev):
    count, per, total = len(lefts), len(weights[0]), hat.shape[0]
    rows = total // TEAM

    def kernel(*refs):
        groups = [refs[k * per : (k + 1) * per] for k in range(count)]
        left_refs = refs[count * per : count * per + count]
        hat_ref, one_ref, two_ref, send_ref, keep_ref, sums_ref, *scratch = refs[count * per + count :]
        fetch_columns(groups, scratch[:count], scratch[count:], places, rows_dev)
        buffers = scratch[:count]
        d_one, d_two = None, None
        for k in range(count):
            term = dot(left_refs[k][...], buffers[k][...], contract_cols)
            if k == attn_index:
                d_one = term
            else:
                d_two = term if d_two is None else d_two + term
        write_half((d_one * one_ref[...] + d_two * two_ref[...]).astype(bf16), send_ref, keep_ref)
        hat_now = hat_ref[...].astype(f32)
        sums = [jnp.sum(v, axis=0, keepdims=True) for v in (d_one * hat_now, d_one, d_two * hat_now, d_two)]

        @pl.when(pl.program_id(0) == 0)
        def _():
            for k in range(4):
                sums_ref[k : k + 1] = sums[k]

        @pl.when(pl.program_id(0) > 0)
        def _():
            for k in range(4):
                sums_ref[k : k + 1] += sums[k]

    moving = lambda c: blocks((rows, c), lambda i: (token_block(i, False), 0))
    fixed = lambda r, c: blocks((r, c), lambda i: (0, 0))
    specs, shapes = half_outputs(rows, total)
    return pl.pallas_call(
        kernel,
        grid=(TEAM,),
        in_specs=[ANYWHERE] * (count * per)
        + [moving(v.shape[1]) for v in lefts]
        + [moving(D), fixed(1, D), fixed(1, D)],
        out_specs=specs + [fixed(8, D)],
        out_shape=shapes + [shaped((8, D), f32)],
        scratch_shapes=[pltpu.VMEM((D, e - b), bf16) for b, e in places]
        + [pltpu.SemaphoreType.DMA((copy_count(group),)) for group in weights],
        **params("back"),
    )(*[piece for group in weights for piece in group], *lefts, hat, gain_one, gain_two)


def split_sum(left, right, steps, role):
    rows, width = left.shape
    block = rows // 2 // steps

    def kernel(l_low, l_high, r_low, r_high, keep_ref, send_ref):
        keep_ref[...] = l_low[...].astype(f32) + r_low[...].astype(f32)
        send_ref[...] = (l_high[...].astype(f32) + r_high[...].astype(f32)).astype(bf16)

    low = blocks((block, width), lambda i: (i, 0))
    high = blocks((block, width), lambda i: (i + steps, 0))
    return pl.pallas_call(
        kernel,
        grid=(steps,),
        in_specs=[low, high, low, high],
        out_specs=[low, low],
        out_shape=[shaped((rows // 2, width), f32), shaped((rows // 2, width), bf16)],
        **params(role),
    )(left, left, right, right)


def last_sum(kept, got, role):
    count, steps = len(kept), 2
    rows = kept[0].shape[0]
    widths = [v.shape[1] for v in kept]

    def kernel(*refs):
        begin = 0
        for k in range(count):
            here = slice(begin, begin + widths[k])
            refs[-1][:, here] = (refs[k][...] + refs[count + k][...].astype(f32)).astype(bf16)
            begin += widths[k]

    spec = lambda width: blocks((rows // steps, width), lambda i: (i, 0))
    return pl.pallas_call(
        kernel,
        grid=(steps,),
        in_specs=[spec(w) for w in widths] * 2,
        out_specs=spec(sum(widths)),
        out_shape=shaped((rows, sum(widths)), bf16),
        **params(role),
    )(*kept, *got)


def last_sum_members(kept, got, extra, role):
    count = len(kept)
    members, more, width = extra.shape
    rows = kept[0].shape[0] // members
    widths = [v.shape[1] for v in kept]

    def kernel(*refs):
        begin = 0
        for k in range(count):
            here = slice(begin, begin + widths[k])
            refs[-1][0, :rows, here] = (refs[k][...] + refs[count + k][...].astype(f32)).astype(bf16)
            begin += widths[k]
        refs[-1][0, rows:, :] = refs[-2][0]

    spec = lambda w: blocks((rows, w), lambda i: (i, 0))
    return pl.pallas_call(
        kernel,
        grid=(members,),
        in_specs=[spec(w) for w in widths] * 2 + [blocks((1, more, width), lambda i: (i, 0, 0))],
        out_specs=blocks((1, rows + more, width), lambda i: (i, 0, 0)),
        out_shape=shaped((members, rows + more, width), bf16),
        **params(role),
    )(*kept, *got, extra)


def finish_tokens(order, tokens, other, kept, got, back):
    slots = tokens.shape[0]
    steps = 2
    rows = slots // steps

    def kernel(order_ref, x_ref, other_ref, kept_ref, got_ref, out_ref, sum_ref):
        for k in range(D // LANES):
            source = pl.ds(pl.multiple_of(order_ref[k] * LANES, LANES), LANES)
            sum_ref[:, k * LANES : (k + 1) * LANES] = kept_ref[:, source] + got_ref[:, source].astype(f32)
        total = sum_ref[...]
        x = x_ref[...].astype(f32)
        if back:
            hat, scale = normalize(x)
            inner = jnp.mean(total * hat, axis=-1, keepdims=True)
            total = scale * (total - jnp.mean(total, axis=-1, keepdims=True) - hat * inner)
            x = other_ref[...].astype(f32)
        else:
            total = total + other_ref[...]
        out_ref[...] = (x + total).astype(bf16)

    moving = blocks((rows, D), lambda i, *_: (i, 0))
    return pl.pallas_call(
        kernel,
        grid_spec=pltpu.PrefetchScalarGridSpec(
            num_scalar_prefetch=1,
            grid=(steps,),
            in_specs=[moving, moving if back else blocks((1, D), lambda i, *_: (0, 0)), moving, moving],
            out_specs=moving,
            scratch_shapes=[pltpu.VMEM((rows, D), f32)],
        ),
        out_shape=shaped((slots, D), bf16),
        **params("fin"),
    )(order, tokens, other, kept, got)


def adamw_columns(got, matrices, unit, offset, sections, role, held=None):
    rows = matrices[0][1].shape[0]
    count, span = len(matrices), TEAM * unit
    part = max(rows // 4, 16) if rows % 16 == 0 else rows
    full = blocks((part, span), lambda k, i: (i, offset + k))

    def kernel(*refs):
        ins, outs = refs[: 4 * count], refs[-4 * count :]
        for j in range(count):
            g_ref, w_ref, m_ref, u_ref = ins[4 * j : 4 * j + 4]
            grad_ref, new_ref, mo_ref, uo_ref = outs[4 * j : 4 * j + 4]
            for k in range(TEAM):
                here = slice(k * unit, (k + 1) * unit)
                grad = g_ref[k].astype(f32)
                new, m_new, u_new = adamw_update(
                    w_ref[:, here], grad, m_ref[:, here], u_ref[:, here], learn_rate, decay_matrix
                )
                grad_ref[:, here] = grad
                new_ref[:, here] = new
                mo_ref[:, here] = m_new
                uo_ref[:, here] = u_new

    specs, args = [], []
    for section, *arrays in matrices:
        specs += [blocks((TEAM, part, unit), lambda k, i, s=section: (0, i, s + k)), full, full, full]
        args += [got, *arrays]
    extra = list(held) if held is not None else []
    return pl.pallas_call(
        kernel,
        grid=(sections, rows // part),
        in_specs=specs + [ANYWHERE] * len(extra),
        out_specs=[full] * (4 * count),
        out_shape=[shaped(w.shape, f32) for _, w, _, _ in matrices for _ in range(4)],
        input_output_aliases={4 * count + k: k for k in range(len(extra))},
        **params(role),
    )(*args, *extra)


def body(
    tokens,
    cotangent,
    block_first,
    block_live,
    w_qkv,
    w_attn_out,
    w_mlp_in,
    w_mlp_out,
    vectors,
    first_qkv,
    second_qkv,
    first_attn_out,
    second_attn_out,
    first_mlp_in,
    second_mlp_in,
    first_mlp_out,
    second_mlp_out,
    first_vectors,
    second_vectors,
):
    tokens_in = tokens
    far_size = lax.axis_size("far")
    paired = far_size == 2
    groups = 2 * far_size
    slot_total = tokens.shape[0]
    rows_dev = w_qkv.shape[0]
    rows_team = rows_dev * TEAM
    team_slots = slot_total * TEAM
    piece = vectors.shape[0]
    half = TEAM // 2
    count = len(CHUNKS)
    me = lax.axis_index(NEAR)
    far, column = lax.axis_index("far"), lax.axis_index("col")

    def flips(values, col_axis, far_axis):
        if not paired:
            return values
        values = jnp.where(column == 1, jnp.flip(values, col_axis), values)
        return jnp.where(far == 1, jnp.flip(values, far_axis), values)

    def local_order(values):
        lead = values.shape[:-1]
        k = len(lead)
        parts = values.reshape(*lead, far_size, half, 2, 2 * rows_dev)
        parts = jnp.transpose(parts, (*range(k), k + 2, k, k + 1, k + 3))
        return flips(parts, k, k + 1).reshape(*lead, D)

    def own_order(values):
        lead = values.shape[:-1]
        k = len(lead)
        parts = flips(values.reshape(*lead, 2, far_size, half, 2 * rows_dev), k, k + 1)
        return jnp.transpose(parts, (*range(k), k + 1, k + 2, k, k + 3)).reshape(*lead, D)

    place_in_row = jnp.arange(D // LANES, dtype=jnp.int32)
    if paired:
        c, f, r = place_in_row // (2 * half), place_in_row // half % 2, place_in_row % half
        to_local = ((f ^ far) * half + r) * 2 + (c ^ column)
        f, r, c = place_in_row // (2 * half), place_in_row // 2 % half, place_in_row % 2
        to_own = ((c ^ column) * 2 + (f ^ far)) * half + r
    else:
        to_local, to_own = place_in_row, place_in_row

    payload = jnp.concatenate([vectors.astype(bf16), block_first.astype(bf16), block_live.astype(bf16)])

    def columns(chunk):
        cut = lambda w, parts: w.astype(bf16).reshape(rows_dev, parts, TEAM, -1)
        if chunk is None:
            query = cut(w_qkv, 3).transpose(2, 0, 1, 3).reshape(TEAM, rows_dev, 3 * HEAD)
            return jnp.concatenate([query, cut(w_attn_out, 1)[:, 0].transpose(1, 0, 2)], axis=2)
        begin, end = chunk
        span = slice(TEAM * begin, TEAM * end)
        return jnp.concatenate([cut(w[:, span], 1)[:, 0].transpose(1, 0, 2) for w in (w_mlp_in, w_mlp_out)], axis=2)

    if paired:
        both_send = prepare_tokens(to_local, block_live, tokens, cotangent)
    else:
        both_send = prepare_tokens(to_local, block_live, local_order(tokens), local_order(cotangent))
    both_low = lax.ppermute(both_send, "low", SWAP)
    owns, far_got, load_of, begin_of = [], [None] * len(LOADS), {}, {}
    for load, chunks in enumerate(LOADS):
        parts, begin = [], 0
        for index in chunks:
            parts.append(columns(CHUNKS[index]))
            load_of[index], begin_of[index] = load, begin
            begin += parts[-1].shape[2]
        block = jnp.concatenate(parts, axis=2) if len(parts) > 1 else parts[0]
        if load == 0 and paired:
            extra = jnp.pad(payload, (0, PACK_ROWS * begin - payload.shape[0])).reshape(1, PACK_ROWS, begin)
            block = jnp.concatenate([block, jnp.broadcast_to(extra, (TEAM, PACK_ROWS, begin))], axis=1)
        waits = owns[-1:] if load else [both_send]
        if paired and load == 1:
            far_got[0] = lax.ppermute(owns[0], "far", SWAP)
        if paired and load == 2:
            far_got[0] = lax.ppermute(owns[0], "far", SWAP)
            both_low = after(both_low, owns[1], far_got[0])
            waits = waits + [far_got[0]]
        got = lax.all_to_all(after(block, *waits) if waits else block, NEAR, 0, 0, tiled=True)
        owns.append(got if got.shape[1] != rows_dev else got.reshape(rows_team, got.shape[2]))

    team = [lax.all_gather(v, ("row", "core"), axis=0, tiled=False) for v in (both_send, both_low)]
    order = jnp.array([4 * l + 2 * r + c for c in range(2) for r in range(2) for l in range(2)], jnp.int32)
    near_members = order ^ me
    members = near_members % 4

    loads = []

    def send_far(load, *waits):
        far_got[load] = lax.ppermute(after(owns[load], *waits) if waits else owns[load], "far", SWAP)

    def cross(load, *waits):
        if paired:
            loads[load][1] = far_got[load]
            over = after(far_got[load], *waits) if waits else far_got[load]
            loads[load][3] = lax.ppermute(over, "col", SWAP)

    if paired:
        for own in owns:
            loads.append([own, None, lax.ppermute(own, "col", SWAP), None])
        send_far(1, far_got[0])
        send_far(2, far_got[1])
    else:
        for own in owns:
            loads.append([lax.all_gather(own, CROSS, axis=0, tiled=True)])
    cross(0)
    cross(1)

    length = piece + 2 * BLK_DEV
    if paired:
        parts = lax.optimization_barrier((*loads[0], owns[2], far_got[1], *team))[:4]
        got = extra_rows(parts, rows_dev).reshape(4, TEAM, -1)[:, :, :length]
        mine = got[0]
        got = flips(got.reshape(2, 2, half, 2, length), 0, 1)
        everyone = got.transpose(1, 2, 0, 3, 4).reshape(4 * TEAM, length)
    else:
        everyone = lax.all_gather(payload, EVERY, axis=0, tiled=False).reshape(-1, length)
        mine = lax.all_gather(payload, NEAR, axis=0, tiled=False).reshape(TEAM, length)
    tables = mine[near_members, piece:].astype(f32).astype(jnp.int32)
    first_table, live_table = tables[:, :BLK_DEV], tables[:, BLK_DEV:]
    vec_full = everyone[:, :piece].astype(f32).reshape(VEC)
    b_query, b_value, b_att, b_in, b_mlp, *norm_vectors = split_vectors(vec_full)
    gain_one, shift_one, gain_two, shift_two = (local_order(v)[None] for v in norm_vectors)
    rotary = rotary_rows(jnp.arange(slot_total, dtype=jnp.int32).astype(f32))
    bias_q = lax.dynamic_slice(b_query, (me * HEAD,), (HEAD,))
    bias_v = lax.dynamic_slice(b_value, (me * HEAD,), (HEAD,))
    bias_qkv = jnp.concatenate([bias_q, jnp.zeros_like(bias_q), bias_v])[None]

    def bias_in(begin, end):
        return lax.dynamic_slice(b_in, (TEAM * begin + me * (end - begin),), (end - begin,))[None]

    attn_in, mlp_in, hat = norm_inputs(members, team, gain_one, shift_one, gain_two, shift_two)

    lefts_out, lefts_back, places_out, places_back, sums, terms = [], [], [], [], [], []

    def run_chunk(index, *waits):
        chunk = CHUNKS[index]
        pieces, offset = loads[load_of[index]], begin_of[index]
        ready = after(attn_in if chunk is None else mlp_in, *waits) if waits else (attn_in if chunk is None else mlp_in)
        if chunk is None:
            left_out, left_back, keep, send, total = attn_chunk(
                members, first_table, live_table, team, ready, pieces, offset, bias_qkv, rotary, rows_dev
            )
            places_out.append((offset + 3 * HEAD, offset + 4 * HEAD))
            places_back.append((offset, offset + 3 * HEAD))
        else:
            begin, end = chunk
            left_out, left_back, keep, send, total = mlp_chunk(
                members, team, ready, pieces, offset, bias_in(begin, end), rows_dev
            )
            places_out.append((offset + end - begin, offset + 2 * (end - begin)))
            places_back.append((offset, offset + end - begin))
        lefts_out.append(left_out)
        lefts_back.append(left_back)
        sums.append(total[0])
        terms.append((keep, lax.ppermute(send, "col", SWAP) if paired else send))
        return total

    grouped, owned = [None] * count, [None] * count

    def sum_columns(index, *tokens):
        keep, got = terms[index]
        if not paired:
            term = jnp.concatenate([keep, got], axis=0)
            owned[index] = lax.psum_scatter(term, CROSS, scatter_dimension=0, tiled=True)
            return tokens[0]
        kept, sent = split_sum(after(keep, *tokens), got, 2, f"col{index}")
        grouped[index] = (kept, lax.ppermute(sent, "far", SWAP))
        return kept

    def sum_far(chunks, *tokens, extra=None):
        if not paired:
            return jnp.concatenate([owned[index] for index in chunks], axis=1)
        kept = [grouped[index][0] for index in chunks]
        kept[0] = after(kept[0], *tokens)
        got = [grouped[index][1] for index in chunks]
        role = f"far{chunks[0]}"
        return last_sum(kept, got, role) if extra is None else last_sum_members(kept, got, extra, role)

    def to_rows(term):
        blocked = term if term.ndim == 3 else term.reshape(TEAM, rows_dev, term.shape[1])
        return lax.all_to_all(blocked, NEAR, 0, 0, tiled=True)

    held = {}

    def update(index, got, start, *tokens):
        chunk = CHUNKS[index]
        got = after(got, *tokens)
        if chunk is None:
            held["qkv"] = adamw_columns(
                got, [(start // HEAD, w_qkv, first_qkv, second_qkv)], HEAD, 0, 3, "adam1"
            )
            held["att"] = adamw_columns(
                got, [(start // HEAD + 3, w_attn_out, first_attn_out, second_attn_out)], HEAD, 0, 1, "adam1b"
            )
            return held["qkv"][0], held["att"][0]
        begin, end = chunk
        unit = end - begin
        pair = [
            (start // unit, w_mlp_in, first_mlp_in, second_mlp_in),
            (start // unit + 1, w_mlp_out, first_mlp_out, second_mlp_out),
        ]
        held["mlp"] = adamw_columns(got, pair, unit, begin // unit, 1, f"adam{index}", held.get("mlp"))
        return (held["mlp"][0],)

    w_of_chunk = [loads[load_of[index]] for index in range(count)]
    attn_index = CHUNKS.index(None)
    have = {}

    def do_chunk(index, *waits):
        done = run_chunk(index, *waits)
        if index == 0:
            cross(2, done)
        return (done,)

    def do_back(*waits):
        lefts = [after(lefts_back[0], *waits), *lefts_back[1:]]
        have["back_send"], have["back_keep"], have["norm_sums"] = back_part(
            hat, lefts, w_of_chunk, places_back, attn_index, gain_one, gain_two, rows_dev
        )
        return (have["back_keep"],)

    def do_out(*waits):
        lefts = [after(lefts_out[0], *waits), *lefts_out[1:]]
        have["out_send"], have["out_keep"] = out_part(lefts, w_of_chunk, places_out, rows_dev)
        return (have["out_keep"],)

    def own_step(pair, axis, steps, role, *waits):
        kept, sent = pair
        return split_sum(after(kept, *waits), lax.ppermute(sent, axis, SWAP), steps, role)

    def do_own(name, stage, *waits):
        if stage == "core":
            pair = own_step((have[f"{name}_keep"], have[f"{name}_send"]), "core", 4, f"{name}_core", *waits)
        else:
            pair = own_step(have[f"{name}_pair"], stage, 2, f"{name}_{stage}", *waits)
        have[f"{name}_pair"] = pair
        return (pair[0],)

    def do_far(chunks, *waits):
        more = {}
        if paired and chunks[0] == 2:
            width = 2 * sum(CHUNKS[index][1] - CHUNKS[index][0] for index in chunks)
            flat = after(vector_terms(), *waits).reshape(TEAM, groups * piece)
            high = flat.astype(bf16)
            split = jnp.concatenate([high, (flat - high.astype(f32)).astype(bf16)], axis=1)
            split = jnp.pad(split, ((0, 0), (0, PACK_ROWS * width - split.shape[1])))
            more = dict(extra=split.reshape(TEAM, PACK_ROWS, width))
        owned_now = sum_far(chunks, *waits, **more)
        have[f"rows{chunks[0]}"] = to_rows(owned_now)
        return (owned_now,)

    def do_finish(name, *waits):
        kept, sent = have[f"{name}_pair"]
        got = lax.ppermute(sent, "low" if name == "back" else "row", SWAP)
        if not paired:
            kept, got = own_order(kept), own_order(got)
        other = seed_own if name == "back" else (b_att + b_mlp)[None]
        have[name] = finish_tokens(to_own, after(tokens_in, *waits), other, kept, got, name == "back")
        return (have[name],)

    alive = (jnp.arange(BLOCK, dtype=jnp.int32)[None, :] < block_live[:, None]).reshape(slot_total)
    seed_own = jnp.where(alive[:, None], cotangent, jnp.zeros_like(cotangent))

    def vector_terms():
        norm_sums = have["norm_sums"]
        seed_sum = jnp.sum(seed_own.astype(f32), axis=0)

        def place(values, width):
            return lax.dynamic_update_slice(jnp.zeros((width,), f32), values, (me * values.shape[0],))

        mlp_order = sorted((k for k in range(count) if CHUNKS[k] is not None), key=lambda k: CHUNKS[k][0])
        local_vec = jnp.concatenate(
            [
                place(sums[attn_index][:HEAD], D),
                place(sums[attn_index][2 * HEAD :], D),
                seed_sum,
                *[place(sums[k], TEAM * sums[k].shape[0]) for k in mlp_order],
                seed_sum,
                own_order(norm_sums[:4]).reshape(4 * D),
            ]
        )
        vec_terms = local_vec.reshape(far_size, half, 2, 2, piece).transpose(1, 3, 0, 2, 4).reshape(TEAM, groups, piece)

        return vec_terms

    actions = {
        "K0": lambda *w: do_chunk(0, *w),
        "K1": lambda *w: do_chunk(1, *w),
        "K2": lambda *w: do_chunk(2, *w),
        "K3": lambda *w: do_chunk(3, *w),
        "C0": lambda *w: (sum_columns(0, *w),),
        "C1": lambda *w: (sum_columns(1, *w),),
        "C2": lambda *w: (sum_columns(2, *w),),
        "C3": lambda *w: (sum_columns(3, *w),),
        "B": do_back,
        "O": do_out,
        "B1": lambda *w: do_own("back", "core", *w),
        "B2": lambda *w: do_own("back", "row", *w),
        "B3": lambda *w: do_finish("back", *w),
        "O1": lambda *w: do_own("out", "core", *w),
        "O2": lambda *w: do_own("out", "low", *w),
        "O3": lambda *w: do_finish("out", *w),
        "F0": lambda *w: do_far((0, 1), *w),
        "F2": lambda *w: do_far((2, 3), *w),
        "A0": lambda *w: update(0, have["rows0"], 0, *w),
        "A1": lambda *w: update(1, have["rows0"], 512, *w),
        "A2": lambda *w: update(2, have["rows2"], 0, *w),
        "A3": lambda *w: update(3, have["rows2"], 1024, *w),
    }
    waits = ()
    for name in ORDER:
        waits = actions[name](*waits)
    out, grad_tokens, rows_high = have["out"], have["back"], have["rows2"]
    if paired:
        vec_got = rows_high[:, rows_dev:].reshape(TEAM, -1)[:, : 2 * groups * piece].astype(f32)
        vec_team = jnp.sum(vec_got.reshape(2 * TEAM, groups, piece), axis=0)
    else:
        vec_team = jnp.sum(lax.all_to_all(vector_terms(), NEAR, 0, 0, tiled=True), axis=0)
    if paired:
        pick = lambda f, c: lax.dynamic_index_in_dim(vec_team, 2 * (far ^ f) + (column ^ c), 0, keepdims=False)
        over_col = lax.ppermute(pick(0, 1), "col", SWAP)
        over_far = lax.ppermute(pick(1, 0), "far", SWAP)
        over_both = lax.ppermute(pick(1, 1), ("far", "col"), [(i, 3 - i) for i in range(4)])
        over_col, over_far, over_both, _ = lax.optimization_barrier((over_col, over_far, over_both, out))
        grad_vectors = pick(0, 0) + over_col + over_far + over_both
    else:
        grad_vectors = jnp.sum(lax.all_to_all(vec_team, ("far", "col"), 0, 0, tiled=True), axis=0)
    new_vec, m_vec, u_vec = adamw_update(vectors, grad_vectors, first_vectors, second_vectors, vector_rate, 0.0)
    grad_qkv, new_qkv, m_qkv, u_qkv = held["qkv"]
    grad_attn_out, new_att, m_att, u_att = held["att"]
    grad_mlp_in, new_in, m_in, u_in, grad_mlp_out, new_out, m_out, u_out = held["mlp"]
    return (
        out,
        grad_tokens,
        grad_qkv,
        grad_attn_out,
        grad_mlp_in,
        grad_mlp_out,
        grad_vectors,
        new_qkv,
        new_att,
        new_in,
        new_out,
        new_vec,
        m_qkv,
        u_qkv,
        m_att,
        u_att,
        m_in,
        u_in,
        m_out,
        u_out,
        m_vec,
        u_vec,
    )


def solution(mesh):
    devices = mesh.devices.reshape(-1)
    layout = Mesh(devices.reshape(devices.size // 16, 2, 2, 2, 2), EVERY)
    matrix, line = P(EVERY, None), P(EVERY)
    in_specs = (matrix, matrix, line, line) + (matrix,) * 4 + (line,) + (matrix,) * 8 + (line,) * 2
    out_specs = (matrix,) * 6 + (line,) + (matrix,) * 4 + (line,) + (matrix,) * 8 + (line,) * 2
    return jax.shard_map(body, mesh=layout, in_specs=in_specs, out_specs=out_specs, check_vma=False)
```

```python
import jax
import jax.numpy as jnp
from jax import lax
from jax.experimental import pallas as pl
from jax.experimental.pallas import tpu as pltpu
from jax.sharding import Mesh, PartitionSpec as P

D = 2048
HEADS = 8
HEAD = 256
FF = 8192
ROT = 64
BLOCK = 128
BLK_DEV = 2
STEP = 3
VEC = 24576
TEAM = 8
SLICE_FF = FF // TEAM
CHUNKS = ((0, 256), None, (512, 1024), (256, 512))
LOADS = ((0,), (1,), (2, 3))
PACK_ROWS = 16
LANES = 128

eps_norm = 1e-05
beta_one = 0.9
beta_two = 0.95
learn_rate = 0.03
vector_rate = 0.3
decay_matrix = 0.1
eps_adam = 1e-08
masked_score = -1e30
plain = (((1,), (0,)), ((), ()))
contract_rows = (((0,), (0,)), ((), ()))
contract_cols = (((1,), (1,)), ((), ()))
bf16 = jnp.bfloat16
f32 = jnp.float32
VMEM_BYTES = 56 * 1024 * 1024
NEAR = ("low", "row", "core")
CROSS = ("col", "far")
EVERY = ("far", "low", "row", "col", "core")
SWAP = [(0, 1), (1, 0)]
COST = {
    'norm': 100,
    'mlp1024': 20000,
    'attn': 300,
    'back': 10,
    'far0': 20000,
    'adam1': 90,
    'adam0': 50,
    'adam1b': 40,
    'out': 190,
    'mlp512': 150,
    'rows': 20000,
    'back_row': 300,
    'prep': 300,
    'far2': 30,
    'col1': 100,
    'fin': 30,
    'col0': 10,
    'back_core': 10,
}
ORDER = (
    'K0',
    'K1',
    'C0',
    'K2',
    'K3',
    'C1',
    'O',
    'B',
    'C3',
    'F0',
    'O1',
    'B1',
    'C2',
    'F2',
    'B2',
    'A1',
    'A0',
    'O2',
    'A2',
    'A3',
    'O3',
    'B3',
)
ANYWHERE = pl.BlockSpec(memory_space=pl.ANY)


def dot(left, right, dims=plain):
    return lax.dot_general(left, right, dims, preferred_element_type=f32)


def after(value, *others):
    return lax.optimization_barrier((value, *others))[0]


def params(role):
    return dict(
        compiler_params=pltpu.CompilerParams(vmem_limit_bytes=VMEM_BYTES),
        cost_estimate=pl.CostEstimate(flops=int(COST.get(role, 1) * 1e8), bytes_accessed=1024, transcendentals=0),
    )


def shaped(shape, dtype):
    return jax.ShapeDtypeStruct(shape, dtype)


def blocks(shape, index):
    return pl.BlockSpec(shape, index)


def split_vectors(vec_all):
    boundaries = [D, 2 * D, 3 * D, 3 * D + FF, 4 * D + FF, 5 * D + FF, 6 * D + FF, 7 * D + FF]
    return jnp.split(vec_all, boundaries)


def adamw_update(weight, grad, first_m, second_m, rate_value, decay_value):
    first_new = beta_one * first_m + (1.0 - beta_one) * grad
    second_new = beta_two * second_m + (1.0 - beta_two) * grad * grad
    fix_one = 1.0 - beta_one**STEP
    fix_two = 1.0 - beta_two**STEP
    direction = first_new / fix_one / (jnp.sqrt(second_new / fix_two) + eps_adam)
    return (weight - rate_value * (direction + decay_value * weight), first_new, second_new)


def normalize(values):
    centred = values - jnp.mean(values, axis=-1, keepdims=True)
    spread = jnp.mean(centred * centred, axis=-1, keepdims=True)
    scale = lax.rsqrt(spread + eps_norm)
    return centred * scale, scale


def rotary_rows(position):
    lane = jnp.arange(LANES)
    frequency = 10000.0 ** (-(2.0 * (lane % (ROT // 2)).astype(f32)) / ROT)
    angles = position[:, None] * frequency[None, :]
    sine = jnp.sin(angles)
    cosine = jnp.where(lane < ROT, jnp.cos(angles), 1.0)
    return (
        cosine,
        jnp.where(lane < ROT // 2, -sine, 0.0),
        jnp.where((lane >= ROT // 2) & (lane < ROT), sine, 0.0),
    )


def gelu_pair(hidden):
    cumulative = 0.5 * (1.0 + lax.erf(hidden * (0.5**0.5)))
    density = jnp.exp(-0.5 * hidden * hidden) * 0.3989422804014327
    return hidden * cumulative, cumulative + hidden * density


def stacked_copies(refs, buffer, sems, rows_dev, columns=None):
    copies, begin = [], 0
    for ref in refs:
        parts = [ref] if len(ref.shape) == 2 else [ref.at[k, 0:rows_dev] for k in range(ref.shape[0])]
        for part in parts:
            rows = part.shape[0]
            source = part if columns is None else part.at[:, columns]
            copies.append(pltpu.make_async_copy(source, buffer.at[begin : begin + rows], sems.at[len(copies)]))
            begin += rows
    return copies


def copy_count(pieces):
    return sum(1 if piece.ndim == 2 else piece.shape[0] for piece in pieces)


def extra_rows(pieces, rows_dev):
    count, (members, rows, width) = len(pieces), pieces[0].shape
    more = rows - rows_dev

    def kernel(*refs):
        for k in range(count):
            refs[-1][k] = refs[k][...]

    return pl.pallas_call(
        kernel,
        grid=(1,),
        in_specs=[blocks((members, more, width), lambda i: (0, rows_dev // more, 0))] * count,
        out_specs=blocks((count, members, more, width), lambda i: (0, 0, 0, 0)),
        out_shape=shaped((count, members, more, width), bf16),
        **params("rows"),
    )(*pieces)


def member_copies(members_ref, team_refs, kind, buffer, sems):
    rows = team_refs[0].shape[1] // 2
    copies = []
    for k in range(TEAM):
        source = team_refs[k % 2].at[members_ref[k], kind * rows : (kind + 1) * rows]
        copies.append(pltpu.make_async_copy(source, buffer.at[k * rows : (k + 1) * rows], sems.at[k]))
    return copies


def prepare_tokens(order, live, tokens, cotangent):
    slots = tokens.shape[0]

    def kernel(order_ref, live_ref, x_ref, y_ref, both_ref):
        row = lax.broadcasted_iota(jnp.int32, (slots, LANES), 0)
        end = jnp.where(row < BLOCK, live_ref[0], live_ref[1] + BLOCK)
        alive = row < end
        for k in range(D // LANES):
            source = pl.ds(pl.multiple_of(order_ref[k] * LANES, LANES), LANES)
            here = slice(k * LANES, (k + 1) * LANES)
            both_ref[:slots, here] = x_ref[:, source]
            both_ref[slots:, here] = jnp.where(alive, y_ref[:, source].astype(f32), 0.0).astype(bf16)

    whole = blocks((slots, D), lambda i, *_: (0, 0))
    return pl.pallas_call(
        kernel,
        grid_spec=pltpu.PrefetchScalarGridSpec(
            num_scalar_prefetch=2,
            grid=(1,),
            in_specs=[whole, whole],
            out_specs=blocks((2 * slots, D), lambda i, *_: (0, 0)),
        ),
        out_shape=shaped((2 * slots, D), bf16),
        **params("prep"),
    )(order, live, tokens, cotangent)


def norm_inputs(members, team, gain_one, shift_one, gain_two, shift_two):
    count, rows = TEAM, team[0].shape[1] // 2

    def kernel(members_ref, near_ref, over_ref, g1, s1, g2, s2, one_ref, two_ref, hat_ref, buffer, sems):
        step = pl.program_id(0)
        copies = member_copies(members_ref, (near_ref, over_ref), 0, buffer, sems)

        @pl.when(step == 0)
        def _():
            for copy in copies:
                copy.start()

        for k in range(count):

            @pl.when(step == k)
            def _(k=k):
                copies[k].wait()

        hat, _ = normalize(buffer[pl.ds(pl.multiple_of(step * rows, rows), rows), :].astype(f32))
        hat_ref[...] = hat.astype(bf16)
        one_ref[...] = (hat * g1[...] + s1[...]).astype(bf16)
        two_ref[...] = (hat * g2[...] + s2[...]).astype(bf16)

    line = blocks((1, D), lambda i, *_: (0, 0))
    return pl.pallas_call(
        kernel,
        grid_spec=pltpu.PrefetchScalarGridSpec(
            num_scalar_prefetch=1,
            grid=(count,),
            in_specs=[ANYWHERE] * 2 + [line] * 4,
            out_specs=[blocks((rows, D), lambda i, *_: (i, 0))] * 3,
            scratch_shapes=[pltpu.VMEM((count * rows, D), bf16), pltpu.SemaphoreType.DMA((count,))],
        ),
        out_shape=[shaped((count * rows, D), bf16)] * 3,
        **params("norm"),
    )(members, *team, gain_one, shift_one, gain_two, shift_two)


def open_chunk(step, rows, rows_dev, members_ref, team_refs, w_refs, begin, y_all, w_all, y_sems, w_sems):
    y_copies = member_copies(members_ref, team_refs, 1, y_all, y_sems)
    w_copies = stacked_copies(w_refs, w_all, w_sems, rows_dev, slice(begin, begin + w_all.shape[1]))
    slots = team_refs[0].shape[1] // 2

    @pl.when(step == 0)
    def _():
        for copy in w_copies + y_copies:
            copy.start()
        for copy in w_copies:
            copy.wait()

    for k, copy in enumerate(y_copies):

        @pl.when(step == k * slots // rows)
        def _(copy=copy):
            copy.wait()

    return y_all[pl.ds(pl.multiple_of(step * rows, rows), rows), :]


def close_chunk(step, last, acc_ref, keep_ref, send_ref, sum_ref, cols, first_term, second_term, column_sum):
    @pl.when(step == 0)
    def _():
        acc_ref[:, :cols] = first_term
        acc_ref[:, cols:] = second_term
        sum_ref[...] = column_sum

    @pl.when((step > 0) & (step < last))
    def _():
        acc_ref[:, :cols] += first_term
        acc_ref[:, cols:] += second_term
        sum_ref[...] += column_sum

    @pl.when(step == last)
    def _():
        half = D // 2
        keep_ref[:, :cols] = (acc_ref[:half, :cols] + first_term[:half]).astype(bf16)
        keep_ref[:, cols:] = (acc_ref[:half, cols:] + second_term[:half]).astype(bf16)
        send_ref[:, :cols] = (acc_ref[half:, :cols] + first_term[half:]).astype(bf16)
        send_ref[:, cols:] = (acc_ref[half:, cols:] + second_term[half:]).astype(bf16)
        sum_ref[...] += column_sum


def chunk_scratch(total, width, y_count, w_count):
    return [
        pltpu.VMEM((D, width), f32),
        pltpu.VMEM((total, D), bf16),
        pltpu.VMEM((D, width), bf16),
        pltpu.SemaphoreType.DMA((y_count,)),
        pltpu.SemaphoreType.DMA((w_count,)),
    ]


def mlp_chunk(members, team, a, w_pieces, begin, b, rows_dev, rows=512):
    total, cols = a.shape[0], b.shape[1]
    width = 2 * cols
    nw = len(w_pieces)

    def kernel(members_ref, *refs):
        team_refs, w_refs, refs = refs[:2], refs[2 : 2 + nw], refs[2 + nw :]
        a_ref, b_ref, act_ref, dh_ref, keep_ref, send_ref, sum_ref, acc_ref, y_all, w_all, y_sems, w_sems = refs
        step, last = pl.program_id(0), pl.num_programs(0) - 1
        y = open_chunk(step, rows, rows_dev, members_ref, team_refs, w_refs, begin, y_all, w_all, y_sems, w_sems)
        a = a_ref[...]
        act, slope = gelu_pair(dot(a, w_all[:, :cols]) + b_ref[...])
        act = act.astype(bf16)
        dh = (dot(y, w_all[:, cols:]) * slope).astype(bf16)
        act_ref[...] = act
        dh_ref[...] = dh
        column_sum = jnp.sum(dh.astype(f32), axis=0, keepdims=True)
        first_term, second_term = dot(a, dh, contract_rows), dot(y, act, contract_rows)
        close_chunk(step, last, acc_ref, keep_ref, send_ref, sum_ref, cols, first_term, second_term, column_sum)

    fixed = lambda r, c: blocks((r, c), lambda i, *_: (0, 0))
    moving = lambda c: blocks((rows, c), lambda i, *_: (i, 0))
    return pl.pallas_call(
        kernel,
        grid_spec=pltpu.PrefetchScalarGridSpec(
            num_scalar_prefetch=1,
            grid=(total // rows,),
            in_specs=[ANYWHERE] * (2 + nw) + [moving(D), fixed(1, cols)],
            out_specs=[moving(cols), moving(cols), fixed(D // 2, width), fixed(D // 2, width), fixed(1, cols)],
            scratch_shapes=chunk_scratch(total, width, TEAM, copy_count(w_pieces)),
        ),
        out_shape=[shaped((total, cols), bf16)] * 2 + [shaped((D // 2, width), bf16)] * 2 + [shaped((1, cols), f32)],
        **params(f"mlp{width}"),
    )(members, *team, *w_pieces, a, b)


def turn_lanes(values, cosine, low_sine, high_sine):
    part = values[:, :LANES]
    part = part * cosine + pltpu.roll(part, LANES - ROT // 2, 1) * low_sine + pltpu.roll(part, ROT // 2, 1) * high_sine
    return jnp.concatenate([part, values[:, LANES:]], axis=1)


def attn_chunk(members, first, live, team, a, w_pieces, begin, b, rotary, rows_dev, rows=512):
    total, width = a.shape[0], 4 * HEAD
    nw = len(w_pieces)
    slots = BLK_DEV * BLOCK
    buffers = rows // slots

    def kernel(members_ref, first_ref, live_ref, *refs):
        team_refs, w_refs, refs = refs[:2], refs[2 : 2 + nw], refs[2 + nw :]
        a_ref, b_ref, cos_ref, low_ref, high_ref, att_ref, dm_ref, keep_ref, send_ref, sum_ref = refs[:10]
        acc_ref, y_all, w_all, y_sems, w_sems = refs[10:]
        step, last = pl.program_id(0), pl.num_programs(0) - 1
        y = open_chunk(step, rows, rows_dev, members_ref, team_refs, w_refs, begin, y_all, w_all, y_sems, w_sems)
        a = a_ref[...]
        mixed = dot(a, w_all[:, : 3 * HEAD]) + b_ref[...]
        datt_all = dot(y, w_all[:, 3 * HEAD :]).astype(bf16)
        row = lax.broadcasted_iota(jnp.int32, (slots, slots), 0)
        col = lax.broadcasted_iota(jnp.int32, (slots, slots), 1)
        for k in range(buffers):
            buf = step * buffers + k
            part = slice(k * slots, (k + 1) * slots)
            apart = first_ref[buf, 1] == 1
            tables = []
            for ref in (cos_ref, low_ref, high_ref):
                start = ref[:BLOCK]
                tables.append(jnp.concatenate([start, jnp.where(apart, start, ref[BLOCK:])], axis=0))
            cosine, low_sine, high_sine = tables
            queries = turn_lanes(mixed[part, :HEAD], cosine, low_sine, high_sine).astype(bf16)
            keys = turn_lanes(mixed[part, HEAD : 2 * HEAD], cosine, low_sine, high_sine).astype(bf16)
            values = mixed[part, 2 * HEAD :].astype(bf16)
            datt = datt_all[part]
            parted = jnp.where(first_ref[buf, 0] == first_ref[buf, 1], 0, 1)
            live_end = jnp.where(col < BLOCK, live_ref[buf, 0], live_ref[buf, 1] + BLOCK)
            other = jnp.where((row >= BLOCK) & (col < BLOCK), parted, 0)
            allowed = (col <= row) & (other == 0) & ((col < live_end) | (col == row))
            scores = jnp.where(allowed, dot(queries, keys, contract_cols) * HEAD ** (-0.5), masked_score)
            raised = jnp.exp(scores - jnp.max(scores, axis=1, keepdims=True))
            probs = raised / jnp.sum(raised, axis=1, keepdims=True)
            probs_low = probs.astype(bf16)
            att_ref[part] = dot(probs_low, values).astype(bf16)
            d_probs = dot(datt, values, contract_cols)
            d_scores = (probs * (d_probs - jnp.sum(probs * d_probs, axis=1, keepdims=True))).astype(bf16)
            d_queries = dot(d_scores, keys) * HEAD ** (-0.5)
            d_keys = dot(d_scores, queries, contract_rows) * HEAD ** (-0.5)
            dm_ref[part, :HEAD] = turn_lanes(d_queries, cosine, -low_sine, -high_sine).astype(bf16)
            dm_ref[part, HEAD : 2 * HEAD] = turn_lanes(d_keys, cosine, -low_sine, -high_sine).astype(bf16)
            dm_ref[part, 2 * HEAD :] = dot(probs_low, datt, contract_rows).astype(bf16)
        d_mixed = dm_ref[...]
        column_sum = jnp.sum(d_mixed.astype(f32), axis=0, keepdims=True)
        first_term, second_term = dot(a, d_mixed, contract_rows), dot(y, att_ref[...], contract_rows)
        close_chunk(step, last, acc_ref, keep_ref, send_ref, sum_ref, 3 * HEAD, first_term, second_term, column_sum)

    fixed = lambda r, c: blocks((r, c), lambda i, *_: (0, 0))
    moving = lambda c: blocks((rows, c), lambda i, *_: (i, 0))
    return pl.pallas_call(
        kernel,
        grid_spec=pltpu.PrefetchScalarGridSpec(
            num_scalar_prefetch=3,
            grid=(total // rows,),
            in_specs=[ANYWHERE] * (2 + nw) + [moving(D), fixed(1, 3 * HEAD)] + [fixed(slots, LANES)] * 3,
            out_specs=[moving(HEAD), moving(3 * HEAD), fixed(D // 2, width), fixed(D // 2, width), fixed(1, 3 * HEAD)],
            scratch_shapes=chunk_scratch(total, width, TEAM, copy_count(w_pieces)),
        ),
        out_shape=[shaped((total, HEAD), bf16), shaped((total, 3 * HEAD), bf16)]
        + [shaped((D // 2, width), bf16)] * 2
        + [shaped((1, 3 * HEAD), f32)],
        **params("attn"),
    )(members, first, live, *team, *w_pieces, a, b, *rotary)


def token_block(i, low_first):
    half = TEAM // 2
    within = i % half
    if low_first:
        within = within % 2 * 2 + within // 2
    return (i // half + 1) % 2 * half + within


def write_half(value, send_ref, keep_ref):
    first_half = pl.program_id(0) < TEAM // 2

    @pl.when(first_half)
    def _():
        send_ref[...] = value

    @pl.when(jnp.logical_not(first_half))
    def _():
        keep_ref[...] = value


def half_outputs(rows, total):
    half = TEAM // 2
    specs = [
        blocks((rows, D), lambda i: (jnp.minimum(i, half - 1), 0)),
        blocks((rows, D), lambda i: (jnp.maximum(i - half, 0), 0)),
    ]
    return specs, [shaped((total // 2, D), bf16)] * 2


def fetch_columns(groups, buffers, sems, places, rows_dev):
    copies = []
    for k, refs in enumerate(groups):
        begin, end = places[k]
        copies += stacked_copies(refs, buffers[k], sems[k], rows_dev, slice(begin, end))

    @pl.when(pl.program_id(0) == 0)
    def _():
        for copy in copies:
            copy.start()
        for copy in copies:
            copy.wait()


def out_part(lefts, weights, places, rows_dev):
    count, per, total = len(lefts), len(weights[0]), lefts[0].shape[0]
    rows = total // TEAM

    def kernel(*refs):
        groups = [refs[k * per : (k + 1) * per] for k in range(count)]
        left_refs = refs[count * per : count * per + count]
        send_ref, keep_ref, *scratch = refs[count * per + count :]
        fetch_columns(groups, scratch[:count], scratch[count:], places, rows_dev)
        buffers = scratch[:count]
        value = None
        for k in range(count):
            term = dot(left_refs[k][...], buffers[k][...], contract_cols)
            value = term if value is None else value + term
        write_half(value.astype(bf16), send_ref, keep_ref)

    specs, shapes = half_outputs(rows, total)
    return pl.pallas_call(
        kernel,
        grid=(TEAM,),
        in_specs=[ANYWHERE] * (count * per) + [blocks((rows, v.shape[1]), lambda i: (token_block(i, True), 0)) for v in lefts],
        out_specs=specs,
        out_shape=shapes,
        scratch_shapes=[pltpu.VMEM((D, e - b), bf16) for b, e in places]
        + [pltpu.SemaphoreType.DMA((copy_count(group),)) for group in weights],
        **params("out"),
    )(*[piece for group in weights for piece in group], *lefts)


def back_part(hat, lefts, weights, places, attn_index, gain_one, gain_two, rows_dev):
    count, per, total = len(lefts), len(weights[0]), hat.shape[0]
    rows = total // TEAM

    def kernel(*refs):
        groups = [refs[k * per : (k + 1) * per] for k in range(count)]
        left_refs = refs[count * per : count * per + count]
        hat_ref, one_ref, two_ref, send_ref, keep_ref, sums_ref, *scratch = refs[count * per + count :]
        fetch_columns(groups, scratch[:count], scratch[count:], places, rows_dev)
        buffers = scratch[:count]
        d_one, d_two = None, None
        for k in range(count):
            term = dot(left_refs[k][...], buffers[k][...], contract_cols)
            if k == attn_index:
                d_one = term
            else:
                d_two = term if d_two is None else d_two + term
        write_half((d_one * one_ref[...] + d_two * two_ref[...]).astype(bf16), send_ref, keep_ref)
        hat_now = hat_ref[...].astype(f32)
        sums = [jnp.sum(v, axis=0, keepdims=True) for v in (d_one * hat_now, d_one, d_two * hat_now, d_two)]

        @pl.when(pl.program_id(0) == 0)
        def _():
            for k in range(4):
                sums_ref[k : k + 1] = sums[k]

        @pl.when(pl.program_id(0) > 0)
        def _():
            for k in range(4):
                sums_ref[k : k + 1] += sums[k]

    moving = lambda c: blocks((rows, c), lambda i: (token_block(i, False), 0))
    fixed = lambda r, c: blocks((r, c), lambda i: (0, 0))
    specs, shapes = half_outputs(rows, total)
    return pl.pallas_call(
        kernel,
        grid=(TEAM,),
        in_specs=[ANYWHERE] * (count * per)
        + [moving(v.shape[1]) for v in lefts]
        + [moving(D), fixed(1, D), fixed(1, D)],
        out_specs=specs + [fixed(8, D)],
        out_shape=shapes + [shaped((8, D), f32)],
        scratch_shapes=[pltpu.VMEM((D, e - b), bf16) for b, e in places]
        + [pltpu.SemaphoreType.DMA((copy_count(group),)) for group in weights],
        **params("back"),
    )(*[piece for group in weights for piece in group], *lefts, hat, gain_one, gain_two)


def split_sum(left, right, steps, role):
    rows, width = left.shape
    block = rows // 2 // steps

    def kernel(l_low, l_high, r_low, r_high, keep_ref, send_ref):
        keep_ref[...] = l_low[...].astype(f32) + r_low[...].astype(f32)
        send_ref[...] = (l_high[...].astype(f32) + r_high[...].astype(f32)).astype(bf16)

    low = blocks((block, width), lambda i: (i, 0))
    high = blocks((block, width), lambda i: (i + steps, 0))
    return pl.pallas_call(
        kernel,
        grid=(steps,),
        in_specs=[low, high, low, high],
        out_specs=[low, low],
        out_shape=[shaped((rows // 2, width), f32), shaped((rows // 2, width), bf16)],
        **params(role),
    )(left, left, right, right)


def last_sum(kept, got, role):
    count, steps = len(kept), 4
    rows = kept[0].shape[0]
    widths = [v.shape[1] for v in kept]

    def kernel(*refs):
        begin = 0
        for k in range(count):
            here = slice(begin, begin + widths[k])
            refs[-1][:, here] = (refs[k][...] + refs[count + k][...].astype(f32)).astype(bf16)
            begin += widths[k]

    spec = lambda width: blocks((rows // steps, width), lambda i: (i, 0))
    return pl.pallas_call(
        kernel,
        grid=(steps,),
        in_specs=[spec(w) for w in widths] * 2,
        out_specs=spec(sum(widths)),
        out_shape=shaped((rows, sum(widths)), bf16),
        **params(role),
    )(*kept, *got)


def last_sum_members(kept, got, extra, role):
    count = len(kept)
    members, more, width = extra.shape
    rows = kept[0].shape[0] // members
    widths = [v.shape[1] for v in kept]

    def kernel(*refs):
        begin = 0
        for k in range(count):
            here = slice(begin, begin + widths[k])
            refs[-1][0, :rows, here] = (refs[k][...] + refs[count + k][...].astype(f32)).astype(bf16)
            begin += widths[k]
        refs[-1][0, rows:, :] = refs[-2][0]

    spec = lambda w: blocks((rows, w), lambda i: (i, 0))
    return pl.pallas_call(
        kernel,
        grid=(members,),
        in_specs=[spec(w) for w in widths] * 2 + [blocks((1, more, width), lambda i: (i, 0, 0))],
        out_specs=blocks((1, rows + more, width), lambda i: (i, 0, 0)),
        out_shape=shaped((members, rows + more, width), bf16),
        **params(role),
    )(*kept, *got, extra)


def finish_tokens(order, tokens, other, kept, got, back):
    slots = tokens.shape[0]
    steps = 4
    rows = slots // steps

    def kernel(order_ref, x_ref, other_ref, kept_ref, got_ref, out_ref, sum_ref):
        for k in range(D // LANES):
            source = pl.ds(pl.multiple_of(order_ref[k] * LANES, LANES), LANES)
            sum_ref[:, k * LANES : (k + 1) * LANES] = kept_ref[:, source] + got_ref[:, source].astype(f32)
        total = sum_ref[...]
        x = x_ref[...].astype(f32)
        if back:
            hat, scale = normalize(x)
            inner = jnp.mean(total * hat, axis=-1, keepdims=True)
            total = scale * (total - jnp.mean(total, axis=-1, keepdims=True) - hat * inner)
            x = other_ref[...].astype(f32)
        else:
            total = total + other_ref[...]
        out_ref[...] = (x + total).astype(bf16)

    moving = blocks((rows, D), lambda i, *_: (i, 0))
    return pl.pallas_call(
        kernel,
        grid_spec=pltpu.PrefetchScalarGridSpec(
            num_scalar_prefetch=1,
            grid=(steps,),
            in_specs=[moving, moving if back else blocks((1, D), lambda i, *_: (0, 0)), moving, moving],
            out_specs=moving,
            scratch_shapes=[pltpu.VMEM((rows, D), f32)],
        ),
        out_shape=shaped((slots, D), bf16),
        **params("fin"),
    )(order, tokens, other, kept, got)


def adamw_columns(got, matrices, unit, offset, sections, role, held=None):
    rows = matrices[0][1].shape[0]
    count, span = len(matrices), TEAM * unit
    part = max(rows // 4, 16) if rows % 16 == 0 else rows
    full = blocks((part, span), lambda k, i: (i, offset + k))

    def kernel(*refs):
        ins, outs = refs[: 4 * count], refs[-4 * count :]
        for j in range(count):
            g_ref, w_ref, m_ref, u_ref = ins[4 * j : 4 * j + 4]
            grad_ref, new_ref, mo_ref, uo_ref = outs[4 * j : 4 * j + 4]
            for k in range(TEAM):
                here = slice(k * unit, (k + 1) * unit)
                grad = g_ref[k].astype(f32)
                new, m_new, u_new = adamw_update(
                    w_ref[:, here], grad, m_ref[:, here], u_ref[:, here], learn_rate, decay_matrix
                )
                grad_ref[:, here] = grad
                new_ref[:, here] = new
                mo_ref[:, here] = m_new
                uo_ref[:, here] = u_new

    specs, args = [], []
    for section, *arrays in matrices:
        specs += [blocks((TEAM, part, unit), lambda k, i, s=section: (0, i, s + k)), full, full, full]
        args += [got, *arrays]
    extra = list(held) if held is not None else []
    return pl.pallas_call(
        kernel,
        grid=(sections, rows // part),
        in_specs=specs + [ANYWHERE] * len(extra),
        out_specs=[full] * (4 * count),
        out_shape=[shaped(w.shape, f32) for _, w, _, _ in matrices for _ in range(4)],
        input_output_aliases={4 * count + k: k for k in range(len(extra))},
        **params(role),
    )(*args, *extra)


def body(
    tokens,
    cotangent,
    block_first,
    block_live,
    w_qkv,
    w_attn_out,
    w_mlp_in,
    w_mlp_out,
    vectors,
    first_qkv,
    second_qkv,
    first_attn_out,
    second_attn_out,
    first_mlp_in,
    second_mlp_in,
    first_mlp_out,
    second_mlp_out,
    first_vectors,
    second_vectors,
):
    tokens_in = tokens
    far_size = lax.axis_size("far")
    paired = far_size == 2
    groups = 2 * far_size
    slot_total = tokens.shape[0]
    rows_dev = w_qkv.shape[0]
    rows_team = rows_dev * TEAM
    team_slots = slot_total * TEAM
    piece = vectors.shape[0]
    half = TEAM // 2
    count = len(CHUNKS)
    me = lax.axis_index(NEAR)
    far, column = lax.axis_index("far"), lax.axis_index("col")

    def flips(values, col_axis, far_axis):
        if not paired:
            return values
        values = jnp.where(column == 1, jnp.flip(values, col_axis), values)
        return jnp.where(far == 1, jnp.flip(values, far_axis), values)

    def local_order(values):
        lead = values.shape[:-1]
        k = len(lead)
        parts = values.reshape(*lead, far_size, half, 2, 2 * rows_dev)
        parts = jnp.transpose(parts, (*range(k), k + 2, k, k + 1, k + 3))
        return flips(parts, k, k + 1).reshape(*lead, D)

    def own_order(values):
        lead = values.shape[:-1]
        k = len(lead)
        parts = flips(values.reshape(*lead, 2, far_size, half, 2 * rows_dev), k, k + 1)
        return jnp.transpose(parts, (*range(k), k + 1, k + 2, k, k + 3)).reshape(*lead, D)

    place_in_row = jnp.arange(D // LANES, dtype=jnp.int32)
    if paired:
        c, f, r = place_in_row // (2 * half), place_in_row // half % 2, place_in_row % half
        to_local = ((f ^ far) * half + r) * 2 + (c ^ column)
        f, r, c = place_in_row // (2 * half), place_in_row // 2 % half, place_in_row % 2
        to_own = ((c ^ column) * 2 + (f ^ far)) * half + r
    else:
        to_local, to_own = place_in_row, place_in_row

    payload = jnp.concatenate([vectors.astype(bf16), block_first.astype(bf16), block_live.astype(bf16)])

    def columns(chunk):
        cut = lambda w, parts: w.astype(bf16).reshape(rows_dev, parts, TEAM, -1)
        if chunk is None:
            query = cut(w_qkv, 3).transpose(2, 0, 1, 3).reshape(TEAM, rows_dev, 3 * HEAD)
            return jnp.concatenate([query, cut(w_attn_out, 1)[:, 0].transpose(1, 0, 2)], axis=2)
        begin, end = chunk
        span = slice(TEAM * begin, TEAM * end)
        return jnp.concatenate([cut(w[:, span], 1)[:, 0].transpose(1, 0, 2) for w in (w_mlp_in, w_mlp_out)], axis=2)

    if paired:
        both_send = prepare_tokens(to_local, block_live, tokens, cotangent)
    else:
        both_send = prepare_tokens(to_local, block_live, local_order(tokens), local_order(cotangent))
    both_low = lax.ppermute(both_send, "low", SWAP)
    owns, far_got, load_of, begin_of = [], [None] * len(LOADS), {}, {}
    for load, chunks in enumerate(LOADS):
        parts, begin = [], 0
        for index in chunks:
            parts.append(columns(CHUNKS[index]))
            load_of[index], begin_of[index] = load, begin
            begin += parts[-1].shape[2]
        block = jnp.concatenate(parts, axis=2) if len(parts) > 1 else parts[0]
        if load == 0 and paired:
            extra = jnp.pad(payload, (0, PACK_ROWS * begin - payload.shape[0])).reshape(1, PACK_ROWS, begin)
            block = jnp.concatenate([block, jnp.broadcast_to(extra, (TEAM, PACK_ROWS, begin))], axis=1)
        waits = owns[-1:] if load else [both_send]
        if paired and load == 1:
            far_got[0] = lax.ppermute(owns[0], "far", SWAP)
        if paired and load == 2:
            far_got[0] = lax.ppermute(owns[0], "far", SWAP)
            both_low = after(both_low, owns[1], far_got[0])
            waits = waits + [far_got[0]]
        got = lax.all_to_all(after(block, *waits) if waits else block, NEAR, 0, 0, tiled=True)
        owns.append(got if got.shape[1] != rows_dev else got.reshape(rows_team, got.shape[2]))

    team = [lax.all_gather(v, ("row", "core"), axis=0, tiled=False) for v in (both_send, both_low)]
    order = jnp.array([4 * l + 2 * r + c for c in range(2) for r in range(2) for l in range(2)], jnp.int32)
    near_members = order ^ me
    members = near_members % 4

    loads = []

    def send_far(load, *waits):
        far_got[load] = lax.ppermute(after(owns[load], *waits) if waits else owns[load], "far", SWAP)

    def cross(load, *waits):
        if paired:
            loads[load][1] = far_got[load]
            over = after(far_got[load], *waits) if waits else far_got[load]
            loads[load][3] = lax.ppermute(over, "col", SWAP)

    if paired:
        for own in owns:
            loads.append([own, None, lax.ppermute(own, "col", SWAP), None])
        send_far(1, far_got[0])
        send_far(2, far_got[1])
    else:
        for own in owns:
            loads.append([lax.all_gather(own, CROSS, axis=0, tiled=True)])
    cross(0)
    cross(1)

    length = piece + 2 * BLK_DEV
    if paired:
        parts = lax.optimization_barrier((*loads[0], owns[2], far_got[1], *team))[:4]
        got = extra_rows(parts, rows_dev).reshape(4, TEAM, -1)[:, :, :length]
        mine = got[0]
        got = flips(got.reshape(2, 2, half, 2, length), 0, 1)
        everyone = got.transpose(1, 2, 0, 3, 4).reshape(4 * TEAM, length)
    else:
        everyone = lax.all_gather(payload, EVERY, axis=0, tiled=False).reshape(-1, length)
        mine = lax.all_gather(payload, NEAR, axis=0, tiled=False).reshape(TEAM, length)
    tables = mine[near_members, piece:].astype(f32).astype(jnp.int32)
    first_table, live_table = tables[:, :BLK_DEV], tables[:, BLK_DEV:]
    vec_full = everyone[:, :piece].astype(f32).reshape(VEC)
    b_query, b_value, b_att, b_in, b_mlp, *norm_vectors = split_vectors(vec_full)
    gain_one, shift_one, gain_two, shift_two = (local_order(v)[None] for v in norm_vectors)
    rotary = rotary_rows(jnp.arange(slot_total, dtype=jnp.int32).astype(f32))
    bias_q = lax.dynamic_slice(b_query, (me * HEAD,), (HEAD,))
    bias_v = lax.dynamic_slice(b_value, (me * HEAD,), (HEAD,))
    bias_qkv = jnp.concatenate([bias_q, jnp.zeros_like(bias_q), bias_v])[None]

    def bias_in(begin, end):
        return lax.dynamic_slice(b_in, (TEAM * begin + me * (end - begin),), (end - begin,))[None]

    attn_in, mlp_in, hat = norm_inputs(members, team, gain_one, shift_one, gain_two, shift_two)

    lefts_out, lefts_back, places_out, places_back, sums, terms = [], [], [], [], [], []

    def run_chunk(index, *waits):
        chunk = CHUNKS[index]
        pieces, offset = loads[load_of[index]], begin_of[index]
        ready = after(attn_in if chunk is None else mlp_in, *waits) if waits else (attn_in if chunk is None else mlp_in)
        if chunk is None:
            left_out, left_back, keep, send, total = attn_chunk(
                members, first_table, live_table, team, ready, pieces, offset, bias_qkv, rotary, rows_dev
            )
            places_out.append((offset + 3 * HEAD, offset + 4 * HEAD))
            places_back.append((offset, offset + 3 * HEAD))
        else:
            begin, end = chunk
            left_out, left_back, keep, send, total = mlp_chunk(
                members, team, ready, pieces, offset, bias_in(begin, end), rows_dev
            )
            places_out.append((offset + end - begin, offset + 2 * (end - begin)))
            places_back.append((offset, offset + end - begin))
        lefts_out.append(left_out)
        lefts_back.append(left_back)
        sums.append(total[0])
        terms.append((keep, lax.ppermute(send, "col", SWAP) if paired else send))
        return total

    grouped, owned = [None] * count, [None] * count

    def sum_columns(index, *tokens):
        keep, got = terms[index]
        if not paired:
            term = jnp.concatenate([keep, got], axis=0)
            owned[index] = lax.psum_scatter(term, CROSS, scatter_dimension=0, tiled=True)
            return tokens[0]
        kept, sent = split_sum(after(keep, *tokens), got, 4, f"col{index}")
        grouped[index] = (kept, lax.ppermute(sent, "far", SWAP))
        return kept

    def sum_far(chunks, *tokens, extra=None):
        if not paired:
            return jnp.concatenate([owned[index] for index in chunks], axis=1)
        kept = [grouped[index][0] for index in chunks]
        kept[0] = after(kept[0], *tokens)
        got = [grouped[index][1] for index in chunks]
        role = f"far{chunks[0]}"
        return last_sum(kept, got, role) if extra is None else last_sum_members(kept, got, extra, role)

    def to_rows(term):
        blocked = term if term.ndim == 3 else term.reshape(TEAM, rows_dev, term.shape[1])
        return lax.all_to_all(blocked, NEAR, 0, 0, tiled=True)

    held = {}

    def update(index, got, start, *tokens):
        chunk = CHUNKS[index]
        got = after(got, *tokens)
        if chunk is None:
            held["qkv"] = adamw_columns(
                got, [(start // HEAD, w_qkv, first_qkv, second_qkv)], HEAD, 0, 3, "adam1"
            )
            held["att"] = adamw_columns(
                got, [(start // HEAD + 3, w_attn_out, first_attn_out, second_attn_out)], HEAD, 0, 1, "adam1b"
            )
            return held["qkv"][0], held["att"][0]
        begin, end = chunk
        unit = end - begin
        pair = [
            (start // unit, w_mlp_in, first_mlp_in, second_mlp_in),
            (start // unit + 1, w_mlp_out, first_mlp_out, second_mlp_out),
        ]
        held["mlp"] = adamw_columns(got, pair, unit, begin // unit, 1, f"adam{index}", held.get("mlp"))
        return (held["mlp"][0],)

    w_of_chunk = [loads[load_of[index]] for index in range(count)]
    attn_index = CHUNKS.index(None)
    have = {}

    def do_chunk(index, *waits):
        done = run_chunk(index, *waits)
        if index == 0:
            cross(2, done)
        return (done,)

    def do_back(*waits):
        lefts = [after(lefts_back[0], *waits), *lefts_back[1:]]
        have["back_send"], have["back_keep"], have["norm_sums"] = back_part(
            hat, lefts, w_of_chunk, places_back, attn_index, gain_one, gain_two, rows_dev
        )
        return (have["back_keep"],)

    def do_out(*waits):
        lefts = [after(lefts_out[0], *waits), *lefts_out[1:]]
        have["out_send"], have["out_keep"] = out_part(lefts, w_of_chunk, places_out, rows_dev)
        return (have["out_keep"],)

    def own_step(pair, axis, steps, role, *waits):
        kept, sent = pair
        return split_sum(after(kept, *waits), lax.ppermute(sent, axis, SWAP), steps, role)

    def do_own(name, stage, *waits):
        if stage == "core":
            pair = own_step((have[f"{name}_keep"], have[f"{name}_send"]), "core", 8, f"{name}_core", *waits)
        else:
            pair = own_step(have[f"{name}_pair"], stage, 4, f"{name}_{stage}", *waits)
        have[f"{name}_pair"] = pair
        return (pair[0],)

    def do_far(chunks, *waits):
        more = {}
        if paired and chunks[0] == 2:
            width = 2 * sum(CHUNKS[index][1] - CHUNKS[index][0] for index in chunks)
            flat = after(vector_terms(), *waits).reshape(TEAM, groups * piece)
            high = flat.astype(bf16)
            split = jnp.concatenate([high, (flat - high.astype(f32)).astype(bf16)], axis=1)
            split = jnp.pad(split, ((0, 0), (0, PACK_ROWS * width - split.shape[1])))
            more = dict(extra=split.reshape(TEAM, PACK_ROWS, width))
        owned_now = sum_far(chunks, *waits, **more)
        have[f"rows{chunks[0]}"] = to_rows(owned_now)
        return (owned_now,)

    def do_finish(name, *waits):
        kept, sent = have[f"{name}_pair"]
        got = lax.ppermute(sent, "low" if name == "back" else "row", SWAP)
        if not paired:
            kept, got = own_order(kept), own_order(got)
        other = seed_own if name == "back" else (b_att + b_mlp)[None]
        have[name] = finish_tokens(to_own, after(tokens_in, *waits), other, kept, got, name == "back")
        return (have[name],)

    alive = (jnp.arange(BLOCK, dtype=jnp.int32)[None, :] < block_live[:, None]).reshape(slot_total)
    seed_own = jnp.where(alive[:, None], cotangent, jnp.zeros_like(cotangent))

    def vector_terms():
        norm_sums = have["norm_sums"]
        seed_sum = jnp.sum(seed_own.astype(f32), axis=0)

        def place(values, width):
            return lax.dynamic_update_slice(jnp.zeros((width,), f32), values, (me * values.shape[0],))

        mlp_order = sorted((k for k in range(count) if CHUNKS[k] is not None), key=lambda k: CHUNKS[k][0])
        local_vec = jnp.concatenate(
            [
                place(sums[attn_index][:HEAD], D),
                place(sums[attn_index][2 * HEAD :], D),
                seed_sum,
                *[place(sums[k], TEAM * sums[k].shape[0]) for k in mlp_order],
                seed_sum,
                own_order(norm_sums[:4]).reshape(4 * D),
            ]
        )
        vec_terms = local_vec.reshape(far_size, half, 2, 2, piece).transpose(1, 3, 0, 2, 4).reshape(TEAM, groups, piece)

        return vec_terms

    actions = {
        "K0": lambda *w: do_chunk(0, *w),
        "K1": lambda *w: do_chunk(1, *w),
        "K2": lambda *w: do_chunk(2, *w),
        "K3": lambda *w: do_chunk(3, *w),
        "C0": lambda *w: (sum_columns(0, *w),),
        "C1": lambda *w: (sum_columns(1, *w),),
        "C2": lambda *w: (sum_columns(2, *w),),
        "C3": lambda *w: (sum_columns(3, *w),),
        "B": do_back,
        "O": do_out,
        "B1": lambda *w: do_own("back", "core", *w),
        "B2": lambda *w: do_own("back", "row", *w),
        "B3": lambda *w: do_finish("back", *w),
        "O1": lambda *w: do_own("out", "core", *w),
        "O2": lambda *w: do_own("out", "low", *w),
        "O3": lambda *w: do_finish("out", *w),
        "F0": lambda *w: do_far((0, 1), *w),
        "F2": lambda *w: do_far((2, 3), *w),
        "A0": lambda *w: update(0, have["rows0"], 0, *w),
        "A1": lambda *w: update(1, have["rows0"], 512, *w),
        "A2": lambda *w: update(2, have["rows2"], 0, *w),
        "A3": lambda *w: update(3, have["rows2"], 1024, *w),
    }
    waits = ()
    for name in ORDER:
        waits = actions[name](*waits)
    out, grad_tokens, rows_high = have["out"], have["back"], have["rows2"]
    if paired:
        vec_got = rows_high[:, rows_dev:].reshape(TEAM, -1)[:, : 2 * groups * piece].astype(f32)
        vec_team = jnp.sum(vec_got.reshape(2 * TEAM, groups, piece), axis=0)
    else:
        vec_team = jnp.sum(lax.all_to_all(vector_terms(), NEAR, 0, 0, tiled=True), axis=0)
    if paired:
        pick = lambda f, c: lax.dynamic_index_in_dim(vec_team, 2 * (far ^ f) + (column ^ c), 0, keepdims=False)
        over_col = lax.ppermute(pick(0, 1), "col", SWAP)
        over_far = lax.ppermute(pick(1, 0), "far", SWAP)
        over_both = lax.ppermute(pick(1, 1), ("far", "col"), [(i, 3 - i) for i in range(4)])
        over_col, over_far, over_both, _ = lax.optimization_barrier((over_col, over_far, over_both, out))
        grad_vectors = pick(0, 0) + over_col + over_far + over_both
    else:
        grad_vectors = jnp.sum(lax.all_to_all(vec_team, ("far", "col"), 0, 0, tiled=True), axis=0)
    new_vec, m_vec, u_vec = adamw_update(vectors, grad_vectors, first_vectors, second_vectors, vector_rate, 0.0)
    grad_qkv, new_qkv, m_qkv, u_qkv = held["qkv"]
    grad_attn_out, new_att, m_att, u_att = held["att"]
    grad_mlp_in, new_in, m_in, u_in, grad_mlp_out, new_out, m_out, u_out = held["mlp"]
    return (
        out,
        grad_tokens,
        grad_qkv,
        grad_attn_out,
        grad_mlp_in,
        grad_mlp_out,
        grad_vectors,
        new_qkv,
        new_att,
        new_in,
        new_out,
        new_vec,
        m_qkv,
        u_qkv,
        m_att,
        u_att,
        m_in,
        u_in,
        m_out,
        u_out,
        m_vec,
        u_vec,
    )


def solution(mesh):
    devices = mesh.devices.reshape(-1)
    layout = Mesh(devices.reshape(devices.size // 16, 2, 2, 2, 2), EVERY)
    matrix, line = P(EVERY, None), P(EVERY)
    in_specs = (matrix, matrix, line, line) + (matrix,) * 4 + (line,) + (matrix,) * 8 + (line,) * 2
    out_specs = (matrix,) * 6 + (line,) + (matrix,) * 4 + (line,) + (matrix,) * 8 + (line,) * 2
    return jax.shard_map(body, mesh=layout, in_specs=in_specs, out_specs=out_specs, check_vma=False)
```
